128 devices in a mesh: gx: 16 (over x_lo, y, core), gy: 8 (over x_hi, z).
Axes of the slice: x: 4 (x_hi: 2, x_lo: 2; x = x_hi * 2 + x_lo), y: 4, z: 4, core: 2. Of those that a mesh axis runs over, the one named last changes fastest.
Arguments:
- e_field: float32 [3, 3, 4096, 4096], P(None, None, 'gx', 'gy'), may hold values from -6 to 6
- h_field: float32 [3, 3, 4096, 4096], P(None, None, 'gx', 'gy'), may hold values from -6 to 6
- material: int32 [3, 4096, 4096], P(None, 'gx', 'gy'), may hold values from 0 to 7
- eps_table: float32 [8], replicated, may hold values from 1 to 12
- src_pos: int32 [4096, 3], replicated, may hold values from 0 to 4095, as said below
- src_amp: float32 [4096], replicated, may hold values from -40 to 40
- freqs: float32 [2], replicated, may hold values from 0.3 to 2.8
Outputs:
- e_out: float32 [3, 3, 4096, 4096], P(None, None, 'gx', 'gy')
- h_out: float32 [3, 3, 4096, 4096], P(None, None, 'gx', 'gy')
- far_field: float32 [1024, 8, 2, 1024], P('gx', None, None, 'gy')
The draws below stay inside these ranges and needn't reach their ends.
Inputs may be any that keep to these rules, and one draw needn't show every extreme that they name: `src_pos`: each row is a cell (layer, row, column) of the slab; several sources may share a cell.
All inputs are finite; a program needn't handle non-finite values.
Results may differ from the reference program's by a relative error of at most 0.0054.
Values may be sent and summed in bfloat16 or wider, within the bound.
No kernel may reach another device: no remote copies, remote signals or barrier semaphores. Data moves between devices by JAX's collectives and lax.ppermute only.
A program may use at most 192 MiB of HBM per device.

```python
import math
import jax
import jax.numpy as jnp
from jax import lax

NX = 4096
NY = 4096
LZ = 3
FACE = 1
STEPS = 2
NF = 2
ITEMS = 8
NA = 1024
NMAT = 8
NSRC = 4096


def draw_src_pos(key, part):
    key_layer, key_row, key_col = jax.random.split(jax.random.fold_in(key, 17), 3)
    layers = jax.random.randint(key_layer, (NSRC,), 0, LZ)
    rows_drawn = jax.random.randint(key_row, (NSRC,), 0, NX)
    cols_drawn = jax.random.randint(key_col, (NSRC,), 0, NY)
    positions = jnp.stack([layers, rows_drawn, cols_drawn], 1).astype(jnp.int32)
    corner = jnp.array([0, NX - 1, NY - 1], jnp.int32)
    return positions.at[0].set(corner)


def place_ends(entries, stream_key, low, high):
    index_at = [jax.random.randint(jax.random.fold_in(stream_key, axis), (), 0, length) for axis, length in enumerate(entries.shape)]
    widest = entries.shape.index(max(entries.shape))
    next_to = index_at[:widest] + [(index_at[widest] + 1) % entries.shape[widest]] + index_at[widest + 1:]
    return entries.at[tuple(index_at)].set(low).at[tuple(next_to)].set(high)


def levels(stream_key, shape, cuts, smallest, high):
    level = 1.0
    for position, parts in cuts:
        heights = jax.random.uniform(jax.random.fold_in(jax.random.fold_in(stream_key, 6), position), (parts,), jnp.float32, smallest / len(cuts), high / len(cuts))
        level = level * jnp.repeat(jnp.exp(heights), shape[position] // parts).reshape((-1,) + (1,) * (len(shape) - 1 - position))
    return level


def normal_values(rng, dims, spread, reach, shards=(), held_as=jnp.bfloat16):
    drawn = jax.random.normal(rng, dims, jnp.float32) * spread
    if len(shards) > 0:
        drawn = levels(rng, dims, shards, -0.22, 0.18) * drawn
    return jnp.clip(drawn, min=-reach, max=reach).astype(held_as)


def setup_inputs(seed: int = 0) -> dict:
    key_list = jax.random.split(jax.random.key(seed), 8)
    e_field = normal_values(key_list[0], (3, LZ, NX, NY), 1.0, 6.0, ((2, 16), (3, 8)), jnp.float32)
    h_field = normal_values(key_list[1], (3, LZ, NX, NY), 1.0, 6.0, ((2, 16), (3, 8)), jnp.float32)
    material = place_ends(jax.random.randint(key_list[2], (LZ, NX, NY), 0, NMAT), jax.random.fold_in(key_list[2], 1), 0, NMAT - 1).astype(jnp.int32)
    eps_table = jnp.clip(jnp.exp(jax.random.uniform(key_list[3], (NMAT,), jnp.float32, math.log(1.0), math.log(12.0))), 1.0, 12.0)
    src_pos = draw_src_pos(jax.random.fold_in(key_list[7], 71), 0)
    src_amp = normal_values(key_list[5], (NSRC,), 8.0, 40.0, (), jnp.float32)
    freqs = jnp.clip(jax.random.uniform(key_list[6], (NF,), jnp.float32, 0.3, 2.8), 0.3, 2.8)
    return {"e_field": e_field, "h_field": h_field, "material": material, "eps_table": eps_table, "src_pos": src_pos, "src_amp": src_amp, "freqs": freqs}


courant = 0.5
source_rate = 0.7
zoom_factor = 4

def chirp(freq_index, cell_index, period):
    remainder = jnp.remainder(freq_index * cell_index, period)
    phase_angle = remainder.astype(jnp.float32) * (2.0 * math.pi / period)
    return (jnp.cos(phase_angle), -jnp.sin(phase_angle))

def forward(field, dimension, boundary):
    inner = lax.slice_in_dim(field, 1, field.shape[dimension], axis=dimension)
    return jnp.concatenate([inner, jnp.expand_dims(boundary, dimension)], dimension)

def backward(field, dimension, boundary):
    inner = lax.slice_in_dim(field, 0, field.shape[dimension] - 1, axis=dimension)
    return jnp.concatenate([jnp.expand_dims(boundary, dimension), inner], dimension)

def curl_forward(electric, row_rim, col_rim):
    field_x, field_y, field_z = (electric[0], electric[1], electric[2])
    zero_layer = jnp.zeros(field_x.shape[1:], jnp.float32)
    curl_x = forward(field_z, 2, col_rim[1]) - field_z - (forward(field_y, 0, zero_layer) - field_y)
    curl_y = forward(field_x, 0, zero_layer) - field_x - (forward(field_z, 1, row_rim[1]) - field_z)
    curl_z = forward(field_y, 1, row_rim[0]) - field_y - (forward(field_x, 2, col_rim[0]) - field_x)
    return jnp.stack([curl_x, curl_y, curl_z])

def curl_backward(magnetic, row_rim, col_rim):
    field_x, field_y, field_z = (magnetic[0], magnetic[1], magnetic[2])
    zero_layer = jnp.zeros(field_x.shape[1:], jnp.float32)
    curl_x = field_z - backward(field_z, 2, col_rim[1]) - (field_y - backward(field_y, 0, zero_layer))
    curl_y = field_x - backward(field_x, 0, zero_layer) - (field_z - backward(field_z, 1, row_rim[1]))
    curl_z = field_y - backward(field_y, 1, row_rim[0]) - (field_x - backward(field_x, 2, col_rim[0]))
    return jnp.stack([curl_x, curl_y, curl_z])

def reference(e_field, h_field, material, eps_table, src_pos, src_amp, freqs):
    update_scale = courant / eps_table[material]
    source_grid = jnp.zeros((LZ, NX, NY), jnp.float32).at[src_pos[:, 0], src_pos[:, 1], src_pos[:, 2]].add(src_amp)
    row_zero = jnp.zeros((2, LZ, NY), jnp.float32)
    col_zero = jnp.zeros((2, LZ, NX), jnp.float32)
    electric, magnetic = (e_field, h_field)
    real_sum = jnp.zeros((NF, 4, NX, NY), jnp.float32)
    imag_sum = jnp.zeros((NF, 4, NX, NY), jnp.float32)
    for step_index in range(STEPS):
        moment = float(step_index + 1)
        magnetic = magnetic - courant * curl_forward(electric, row_zero, col_zero)
        electric = electric + update_scale * curl_backward(magnetic, row_zero, col_zero)
        electric = electric.at[2].add(math.sin(source_rate * moment) * source_grid)
        face_now = jnp.stack([-magnetic[1, FACE], magnetic[0, FACE], electric[1, FACE], -electric[0, FACE]])
        real_sum = real_sum + face_now[None] * jnp.cos(freqs * moment)[:, None, None, None]
        imag_sum = imag_sum + face_now[None] * jnp.sin(freqs * moment)[:, None, None, None]
    currents = jnp.stack([real_sum.reshape(ITEMS, NX, NY), imag_sum.reshape(ITEMS, NX, NY)], 1).astype(jnp.bfloat16)
    u_index = jnp.arange(NA, dtype=jnp.int32)
    x_index = jnp.arange(NX, dtype=jnp.int32)
    y_index = jnp.arange(NY, dtype=jnp.int32)
    x_real, x_imag = chirp((u_index - NA // 2)[:, None], x_index[None, :], zoom_factor * NX)
    x_table = jnp.stack([x_real, x_imag]).astype(jnp.bfloat16).astype(jnp.float32)
    y_real, y_imag = chirp(y_index[:, None], (u_index + NA // 4)[None, :], zoom_factor * NY)
    y_table = jnp.concatenate([y_real, y_imag], 1).astype(jnp.bfloat16).astype(jnp.float32)
    inv_norm = 1.0 / math.sqrt(NX * NY)

    def one_item(item_currents):
        values = item_currents.astype(jnp.float32)
        product = jnp.einsum('aux,bxy->abuy', x_table, values, precision=lax.Precision.HIGHEST)
        sectioned = jnp.stack([product[0, 0] - product[1, 1], product[0, 1] + product[1, 0]]).astype(jnp.bfloat16)
        second = jnp.einsum('buy,yw->buw', sectioned.astype(jnp.float32), y_table, precision=lax.Precision.HIGHEST)
        result = jnp.stack([second[0, :, :NA] - second[1, :, NA:], second[0, :, NA:] + second[1, :, :NA]])
        return result * inv_norm
    far_all = lax.map(one_item, currents)
    far_field = jnp.transpose(far_all, (2, 0, 1, 3))
    return (electric, magnetic, far_field)
```

```python
import functools
import math

import jax
import jax.numpy as jnp
import ml_dtypes
import numpy as np
from jax import lax
from jax.experimental import pallas as pl
from jax.experimental.pallas import tpu as pltpu
from jax.sharding import Mesh, PartitionSpec as P

LZ = 3
NA = 1024
NMAT = 8
N = 4096
NSRC = 4096
ROWS = 256
COLS = 512
OFF = 8
EXT_R = 280
EXT_C = 640
USED_R = 272
CHUNKS = 4
courant = 0.5
source_rate = 0.7
PERIOD = 4 * N
GX = ("ga", "gc")
MIB = 1 << 20
F32 = jnp.float32
BF16 = jnp.bfloat16


def tables():
    cell = np.arange(N, dtype=np.int64)
    t = np.arange(16)[:, None, None]
    q = np.arange(5)[None, :, None]
    m = np.arange(8)[None, None, :]
    w = (64 * m + 4 * t + q)[..., None]
    phase = np.remainder(w * cell, PERIOD) * (2.0 * math.pi / PERIOD)
    x_table = np.stack([np.cos(phase), np.sin(phase)], 2).reshape(16 * 80, N)
    v = np.arange(NA, dtype=np.int64) + NA // 4
    phase = np.remainder(cell[:, None] * v[None, :], PERIOD) * (2.0 * math.pi / PERIOD)
    y_table = np.concatenate([np.cos(phase), -np.sin(phase)], 1)
    y_table = y_table.reshape(8, 2, 256, 2 * NA).transpose(1, 0, 2, 3).reshape(16, 256, 2 * NA)
    return x_table.astype(ml_dtypes.bfloat16), y_table.astype(ml_dtypes.bfloat16)


def params(**more):
    return pltpu.CompilerParams(vmem_limit_bytes=56 * MIB, **more)


def vmem():
    return pl.BlockSpec(memory_space=pltpu.VMEM)


def smem():
    return pl.BlockSpec(memory_space=pltpu.SMEM)


def scale_of(material, eps_ref):
    eps = jnp.full(material.shape, eps_ref[0], F32)
    for k in range(1, NMAT):
        eps = jnp.where(material == k, eps_ref[k], eps)
    return courant / eps


def pack_cols_kernel(e_lo, e_hi, h_lo, h_hi, m_lo, m_hi, eps_ref, left_ref, right_ref):
    rows = left_ref.shape[0]
    lane = lax.broadcasted_iota(jnp.int32, (rows, 128), 1)
    left = jnp.zeros((rows, 128), F32)
    right = jnp.zeros((rows, 128), F32)
    for a in range(7):
        for layer in range(LZ):
            q = (a * LZ + layer) * 2
            if a < 3:
                lo, hi = e_lo[a, layer], e_hi[a, layer]
            elif a < 6:
                lo, hi = h_lo[a - 3, layer], h_hi[a - 3, layer]
            else:
                lo, hi = scale_of(m_lo[layer], eps_ref), scale_of(m_hi[layer], eps_ref)
            here = (lane == q) | (lane == q + 1)
            moved = pltpu.roll(lo, q, 1) if q else lo
            left = jnp.where(here, moved, left)
            right = jnp.where(here, pltpu.roll(hi, (q + 2) % 128, 1), right)
    left_ref[...] = left
    right_ref[...] = right


def pack_cols(e, h, material, eps):
    rows = 32
    lo4 = pl.BlockSpec((3, LZ, rows, 128), lambda r: (0, 0, r, 0))
    hi4 = pl.BlockSpec((3, LZ, rows, 128), lambda r: (0, 0, r, COLS // 128 - 1))
    lo3 = pl.BlockSpec((LZ, rows, 128), lambda r: (0, r, 0))
    hi3 = pl.BlockSpec((LZ, rows, 128), lambda r: (0, r, COLS // 128 - 1))
    out = pl.BlockSpec((rows, 128), lambda r: (r, 0))
    return pl.pallas_call(
        pack_cols_kernel,
        grid=(ROWS // rows,),
        in_specs=[lo4, hi4, lo4, hi4, lo3, hi3, smem()],
        out_specs=[out, out],
        out_shape=[jax.ShapeDtypeStruct((ROWS, 128), F32)] * 2,
        compiler_params=params(),
        name="pack_cols",
    )(e, e, h, h, material, material, eps)


def rim_tile(from_left, from_right, index):
    lane = lax.broadcasted_iota(jnp.int32, from_left.shape, 1)
    q = 2 * index
    right = pltpu.roll(from_right, (128 - q) % 128, 1) if q else from_right
    left = pltpu.roll(from_left, 126 - q, 1)
    return jnp.where(lane < 2, right, jnp.where(lane >= 126, left, 0.0))


def pack_rows_kernel(
    e_lo, e_hi, h_lo, h_hi, s_lo, s_hi, fl_lo, fl_hi, fr_lo, fr_hi, up_ref, down_ref
):
    sub = lax.broadcasted_iota(jnp.int32, (8, EXT_C), 0)
    up = down = None
    for a in range(7):
        for layer in range(LZ):
            index = a * LZ + layer
            if a < 3:
                lo, hi = e_lo[a, layer], e_hi[a, layer]
            elif a < 6:
                lo, hi = h_lo[a - 3, layer], h_hi[a - 3, layer]
            else:
                lo, hi = s_lo[layer], s_hi[layer]
            lo = jnp.concatenate([lo, rim_tile(fl_lo[...], fr_lo[...], index)], 1)
            hi = jnp.concatenate([hi, rim_tile(fl_hi[...], fr_hi[...], index)], 1)
            p = 2 * (index % 4)
            if p == 0:
                up = jnp.zeros((8, EXT_C), F32)
                down = jnp.zeros((8, EXT_C), F32)
            here = (sub == p) | (sub == p + 1)
            up = jnp.where(here, pltpu.roll(lo, p, 0) if p else lo, up)
            down = jnp.where(here, pltpu.roll(hi, (p + 2) % 8, 0) if p != 6 else hi, down)
            tile = index // 4
            up_ref[8 * tile : 8 * tile + 8, :] = up
            down_ref[8 * tile : 8 * tile + 8, :] = down


def pack_rows(e, h, scale, from_left, from_right):
    last = ROWS // 8 - 1
    lo4 = pl.BlockSpec((3, LZ, 8, COLS), lambda r: (0, 0, 0, 0))
    hi4 = pl.BlockSpec((3, LZ, 8, COLS), lambda r: (0, 0, last, 0))
    lo3 = pl.BlockSpec((LZ, 8, COLS), lambda r: (0, 0, 0))
    hi3 = pl.BlockSpec((LZ, 8, COLS), lambda r: (0, last, 0))
    lo2 = pl.BlockSpec((8, 128), lambda r: (0, 0))
    hi2 = pl.BlockSpec((8, 128), lambda r: (last, 0))
    out = pl.BlockSpec((48, EXT_C), lambda r: (0, 0))
    return pl.pallas_call(
        pack_rows_kernel,
        grid=(1,),
        in_specs=[lo4, hi4, lo4, hi4, lo3, hi3, lo2, hi2, lo2, hi2],
        out_specs=[out, out],
        out_shape=[jax.ShapeDtypeStruct((48, EXT_C), F32)] * 2,
        compiler_params=params(),
        name="pack_rows",
    )(e, e, h, h, scale, scale, from_left, from_left, from_right, from_right)


def prepare_kernel(material_ref, eps_ref, pos_ref, amp_ref, place_ref, scale_ref, grid_ref):
    def scale_strip(s, _):
        r = pl.multiple_of(s * 8, 8)
        for layer in range(LZ):
            scale_ref[layer, pl.ds(r, 8), :] = scale_of(material_ref[layer, pl.ds(r, 8), :], eps_ref)
        return 0

    lax.fori_loop(0, ROWS // 8, scale_strip, 0)

    groups = NSRC // 128
    row = pos_ref[1] - place_ref[0] * ROWS + OFF
    col = pos_ref[2] - place_ref[1] * COLS
    inside = (row >= OFF - 1) & (row <= ROWS + OFF) & (col >= -1) & (col <= COLS)
    col = jnp.where(col < 0, EXT_C - 1, col)
    taken = jnp.where(inside, 1.0, 0.0)
    lane_a = lax.broadcasted_iota(jnp.int32, (128, 128), 0)
    lane_b = lax.broadcasted_iota(jnp.int32, (128, 128), 1)
    before = jnp.where(lane_a < lane_b, 1.0, 0.0).astype(BF16)
    group_a = lax.broadcasted_iota(jnp.int32, (groups, groups), 0)
    group_b = lax.broadcasted_iota(jnp.int32, (groups, groups), 1)
    earlier = jnp.where(group_b < group_a, 1.0, 0.0).astype(BF16)
    in_group = jnp.dot(taken.astype(BF16), before, preferred_element_type=F32)
    ahead = jnp.dot(earlier, taken.astype(BF16), preferred_element_type=F32)
    rank = in_group + jnp.sum(ahead, axis=1, keepdims=True)
    rank = jnp.where(inside, rank, -1.0)
    features = (
        row.astype(F32),
        col.astype(F32),
        pos_ref[0].astype(F32),
        amp_ref[...],
    )
    count = jnp.sum(taken).astype(jnp.int32)
    slot = lax.broadcasted_iota(jnp.int32, (128, 128), 0).astype(F32)
    feature_lane = lax.broadcasted_iota(jnp.int32, (128, 128), 1)
    row_of = lax.broadcasted_iota(jnp.int32, (USED_R, 128), 0).astype(F32)
    col_of = lax.broadcasted_iota(jnp.int32, (EXT_C, 128), 0).astype(F32)
    grid_ref[...] = jnp.zeros(grid_ref.shape, F32)

    def one_pass(p, _):
        base = (p * 128).astype(F32)
        sums = [jnp.zeros((128, 128), F32) for _ in features]
        found = jnp.zeros((128, 128), F32)
        for g in range(groups):
            chosen = slot == rank[g : g + 1, :] - base
            found = jnp.where(chosen, 1.0, found)
            for f, feature in enumerate(features):
                sums[f] = jnp.where(chosen, feature[g : g + 1, :], sums[f])
        packed = jnp.zeros((128, 128), F32)
        for f, total in enumerate(sums + [found]):
            packed = jnp.where(feature_lane == f, jnp.sum(total, axis=1, keepdims=True), packed)
        packed = packed.T
        src_row, src_col, src_layer = packed[0:1], packed[1:2], packed[2:3]
        amp, valid = packed[3:4], packed[4:5]
        amp_1 = amp.astype(BF16).astype(F32)
        amp_2 = (amp - amp_1).astype(BF16).astype(F32)
        amp_3 = amp - amp_1 - amp_2
        at_col = jnp.where(col_of == src_col, 1.0, 0.0).astype(BF16)
        at_col = jnp.concatenate([at_col] * 3, 1)
        for layer in range(LZ):
            at_row = (row_of == src_row) & (src_layer == layer) & (valid > 0.0)
            weights = jnp.concatenate(
                [jnp.where(at_row, part, 0.0).astype(BF16) for part in (amp_1, amp_2, amp_3)], 1
            )
            grid_ref[layer] += lax.dot_general(
                weights, at_col, (((1,), (1,)), ((), ())), preferred_element_type=F32
            )
        return 0

    lax.fori_loop(0, (count + 127) // 128, one_pass, 0)


def prepare(material, eps, pos, amp, place):
    return pl.pallas_call(
        prepare_kernel,
        in_specs=[vmem(), smem(), vmem(), vmem(), smem()],
        out_specs=[vmem(), vmem()],
        out_shape=[
            jax.ShapeDtypeStruct((LZ, ROWS, COLS), F32),
            jax.ShapeDtypeStruct((LZ, USED_R, EXT_C), F32),
        ],
        compiler_params=params(),
        cost_estimate=pl.CostEstimate(flops=3_000_000_000, bytes_accessed=6_000_000, transcendentals=0),
        name="prepare",
    )(material, eps, pos, amp, place)


def yee_kernel(
    with_fields,
    with_face,
    e_in,
    h_in,
    scale_in,
    grid_in,
    from_left,
    from_right,
    from_top,
    from_bottom,
    place_ref,
    *refs,
):
    refs = list(refs)
    e_out, h_out = (refs.pop(0), refs.pop(0)) if with_fields else (None, None)
    face_out = refs.pop(0) if with_face else None
    e, h, scale, grid = refs[:4]
    refs = refs[4:]
    first = refs.pop(0) if with_face else None
    in_sem, out_sem = refs

    copies = []
    for layer in range(LZ):
        for a in range(3):
            for source, target in ((e_in, e), (h_in, h)):
                copies.append(
                    pltpu.make_async_copy(
                        source.at[a, layer],
                        target.at[a, layer, pl.ds(OFF, ROWS), pl.ds(0, COLS)],
                        in_sem.at[len(copies)],
                    )
                )
        copies.append(
            pltpu.make_async_copy(
                scale_in.at[layer],
                scale.at[layer, pl.ds(OFF, ROWS), pl.ds(0, COLS)],
                in_sem.at[len(copies)],
            )
        )
    copies.append(pltpu.make_async_copy(grid_in, grid, in_sem.at[len(copies)]))
    for copy in copies:
        copy.start()

    sub = lax.broadcasted_iota(jnp.int32, (8, EXT_C), 0)
    lane = lax.broadcasted_iota(jnp.int32, (8, EXT_C), 1)

    def array_of(a, layer):
        if a < 3:
            return e.at[a, layer]
        if a < 6:
            return h.at[a - 3, layer]
        return scale.at[layer]

    for a in range(7):
        for layer in range(LZ):
            index = a * LZ + layer
            target = array_of(a, layer)
            p, tile = 2 * (index % 4), index // 4
            top = from_top[8 * tile : 8 * tile + 8, :]
            top = pltpu.roll(top, (6 - p) % 8, 0) if p != 6 else top
            target[0:8, :] = jnp.where(sub >= 6, top, 0.0)
            bottom = from_bottom[8 * tile : 8 * tile + 8, :]
            bottom = pltpu.roll(bottom, (8 - p) % 8, 0) if p else bottom
            target[ROWS + OFF : ROWS + OFF + 8, :] = jnp.where(sub < 2, bottom, 0.0)
            if a < 3:
                target[USED_R : USED_R + 8, :] = jnp.zeros((8, EXT_C), F32)

    def rim_strip(s, _):
        r = pl.multiple_of(s * 8, 8)
        left = from_left[pl.ds(r, 8), :]
        right = from_right[pl.ds(r, 8), :]
        for a in range(7):
            for layer in range(LZ):
                array_of(a, layer)[pl.ds(pl.multiple_of(r + OFF, 8), 8), COLS:EXT_C] = rim_tile(
                    left, right, a * LZ + layer
                )
        return 0

    lax.fori_loop(0, ROWS // 8, rim_strip, 0)

    row_place, col_place = place_ref[0], place_ref[1]
    half = jnp.full((8, EXT_C), courant, F32)
    half = jnp.where((lane >= COLS + 64) & (col_place == 0), 0.0, half)
    half = jnp.where((lane >= COLS) & (lane < COLS + 64) & (col_place == 7), 0.0, half)
    half_top = jnp.where(row_place == 0, 0.0, half)
    half_bottom = jnp.where(row_place == 15, 0.0, half)

    for copy in copies:
        copy.wait()

    def x_next(ref, here, r):
        after = ref[pl.ds(pl.multiple_of(r + 8, 8), 8), :]
        return jnp.where(sub == 7, pltpu.roll(after, 7, 0), pltpu.roll(here, 7, 0))

    def x_last(ref, here, r):
        if isinstance(r, int):
            return pltpu.roll(here, 1, 0)
        before = ref[pl.ds(pl.multiple_of(r - 8, 8), 8), :]
        return jnp.where(sub == 0, pltpu.roll(before, 1, 0), pltpu.roll(here, 1, 0))

    def y_next(here):
        return pltpu.roll(here, EXT_C - 1, 1)

    def y_last(here):
        return pltpu.roll(here, 1, 1)

    def update_h(r, coef):
        rows = pl.ds(r, 8)
        for layer in range(LZ):
            ex, ey, ez = (e[a, layer, rows, :] for a in range(3))
            if layer + 1 < LZ:
                ex_up, ey_up = e[0, layer + 1, rows, :], e[1, layer + 1, rows, :]
            else:
                ex_up = ey_up = 0.0
            h[0, layer, rows, :] -= coef * (y_next(ez) - ez - (ey_up - ey))
            h[1, layer, rows, :] -= coef * (ex_up - ex - (x_next(e.at[2, layer], ez, r) - ez))
            h[2, layer, rows, :] -= coef * (x_next(e.at[1, layer], ey, r) - ey - (y_next(ex) - ex))

    def update_e(r, moment):
        rows = pl.ds(r, 8)
        strength = math.sin(source_rate * moment)
        for layer in range(LZ):
            hx, hy, hz = (h[a, layer, rows, :] for a in range(3))
            if layer > 0:
                hx_low, hy_low = h[0, layer - 1, rows, :], h[1, layer - 1, rows, :]
            else:
                hx_low = hy_low = 0.0
            rate = scale[layer, rows, :]
            e[0, layer, rows, :] += rate * (hz - y_last(hz) - (hy - hy_low))
            e[1, layer, rows, :] += rate * (hx - hx_low - (hz - x_last(h.at[2, layer], hz, r)))
            e[2, layer, rows, :] = (
                e[2, layer, rows, :]
                + rate * (hy - x_last(h.at[1, layer], hy, r) - (hx - y_last(hx)))
                + strength * grid[layer, rows, :]
            )

    def face(r):
        rows = pl.ds(r, 8)
        return [
            h[1, 1, rows, 0:COLS],
            h[0, 1, rows, 0:COLS],
            e[1, 1, rows, 0:COLS],
            e[0, 1, rows, 0:COLS],
        ]

    update_h(0, half_top)
    update_e(0, 1.0)

    def first_step(s, _):
        r = pl.multiple_of(s * 8, 8)
        update_h(r, half)
        update_e(r, 1.0)
        if with_face:
            for k, now in enumerate(face(r)):
                first[k, pl.ds(pl.multiple_of(r - OFF, 8), 8), :] = now
        return 0

    lax.fori_loop(1, 1 + ROWS // 8, first_step, 0)
    update_h(pl.multiple_of(jnp.int32(ROWS + OFF), 8), half_bottom)
    update_e(pl.multiple_of(jnp.int32(ROWS + OFF), 8), 1.0)

    update_h(0, half_top)
    signs = (-1.0, 1.0, 1.0, -1.0)

    def second_step(s, _):
        own = pl.multiple_of(s * 16, 16)
        pieces = [[] for _ in range(8)]
        for part in range(2):
            r = pl.multiple_of(own + OFF + 8 * part, 8)
            update_h(r, half)
            update_e(r, 2.0)
            if with_face:
                for k, now in enumerate(face(r)):
                    then = first[k, pl.ds(pl.multiple_of(own + 8 * part, 8), 8), :]
                    pieces[2 * k].append(signs[k] * (then + now))
                    pieces[2 * k + 1].append(signs[k] * (then - now))
        if with_face:
            for k in range(8):
                block = jnp.concatenate(pieces[k], 0).astype(BF16)
                face_out[2 * k, pl.ds(own, 16), :] = block[:, 0:256]
                face_out[2 * k + 1, pl.ds(own, 16), :] = block[:, 256:512]
        return 0

    span = ROWS // CHUNKS
    sent = []
    for chunk in range(CHUNKS):
        lax.fori_loop(chunk * (span // 16), (chunk + 1) * (span // 16), second_step, 0)
        if with_fields:
            window = pl.ds(OFF + chunk * span, span)
            target_rows = pl.ds(chunk * span, span)
            for layer in range(LZ):
                for a in range(3):
                    for source, target in ((e, e_out), (h, h_out)):
                        copy = pltpu.make_async_copy(
                            source.at[a, layer, window, pl.ds(0, COLS)],
                            target.at[a, layer, target_rows, :],
                            out_sem.at[len(sent)],
                        )
                        copy.start()
                        sent.append(copy)
    for copy in sent:
        copy.wait()


def yee(with_fields, with_face, e, h, scale, grid, rims, place):
    field = jax.ShapeDtypeStruct((3, LZ, ROWS, COLS), F32)
    anywhere = pl.BlockSpec(memory_space=pl.ANY)
    out_shape = []
    out_specs = []
    scratch = [
        pltpu.VMEM((3, LZ, EXT_R, EXT_C), F32),
        pltpu.VMEM((3, LZ, EXT_R, EXT_C), F32),
        pltpu.VMEM((LZ, EXT_R, EXT_C), F32),
        pltpu.VMEM((LZ, USED_R, EXT_C), F32),
    ]
    if with_fields:
        out_shape += [field, field]
        out_specs += [anywhere, anywhere]
    if with_face:
        out_shape.append(jax.ShapeDtypeStruct((16, ROWS, 256), BF16))
        out_specs.append(vmem())
        scratch.append(pltpu.VMEM((4, ROWS, COLS), F32))
    scratch += [
        pltpu.SemaphoreType.DMA((7 * LZ + 1,)),
        pltpu.SemaphoreType.DMA((CHUNKS * 6 * LZ,)),
    ]
    return pl.pallas_call(
        functools.partial(yee_kernel, with_fields, with_face),
        in_specs=[anywhere] * 4 + [vmem()] * 4 + [smem()],
        out_specs=out_specs,
        out_shape=out_shape,
        scratch_shapes=scratch,
        compiler_params=params(),
        cost_estimate=pl.CostEstimate(
            flops=3_000_000_000, bytes_accessed=24_000_000, transcendentals=0
        ),
        name="yee_fields" if with_fields else "yee_face",
    )(e, h, scale, grid, *rims, place)


def columns_kernel(rows_ref, table_ref, out_ref, total):
    step = pl.program_id(0)

    @pl.when(step == 0)
    def _():
        total[...] = jnp.zeros(total.shape, F32)

    total[...] += jnp.dot(rows_ref[0], table_ref[0], preferred_element_type=F32)

    @pl.when(step == 15)
    def _():
        for q in range(4):
            for plus in (True, False):
                base = 16 * (q if plus else 4 - q)
                cos_re, cos_im = total[base : base + 8, 0:NA], total[base : base + 8, NA : 2 * NA]
                sin_re = total[base + 8 : base + 16, 0:NA]
                sin_im = total[base + 8 : base + 16, NA : 2 * NA]
                if plus:
                    parts = (cos_re + sin_im, cos_im - sin_re)
                else:
                    parts = (cos_re - sin_im, cos_im + sin_re)
                for ri, value in enumerate(parts):
                    for j in range(8):
                        block = value[:, 128 * j : 128 * j + 128]
                        for m in range(8):
                            owner = 8 + m if plus else 7 - m
                            row = (owner * 8 + j) * 8 + 2 * q + ri
                            out_ref[row : row + 1, :] = block[m : m + 1, :]


def columns(rows, table):
    return pl.pallas_call(
        columns_kernel,
        grid=(16,),
        in_specs=[
            pl.BlockSpec((1, 80, 256), lambda t: (t, 0, 0)),
            pl.BlockSpec((1, 256, 2 * NA), lambda t: (t, 0, 0)),
        ],
        out_specs=pl.BlockSpec((1024, 128), lambda t: (0, 0)),
        out_shape=jax.ShapeDtypeStruct((1024, 128), F32),
        scratch_shapes=[pltpu.VMEM((80, 2 * NA), F32)],
        compiler_params=params(),
        name="columns",
    )(rows, table)


def combine_kernel(parts_ref, coef_ref, place_ref, out_ref):
    sub = lax.broadcasted_iota(jnp.int32, (8, 128), 0)
    real_row = (sub % 2) == 0
    side = jnp.where(real_row, -1.0, 1.0)

    def swap(value):
        return jnp.where(real_row, pltpu.roll(value, 7, 0), pltpu.roll(value, 1, 0)) * side

    def one_block(t, _):
        where = jnp.where(place_ref[0] >= 8, t, 15 - t)
        for comp in range(4):
            total = parts_ref[(2 * comp) * 16 + t]
            change = parts_ref[(2 * comp + 1) * 16 + t]
            total_swap, change_swap = swap(total), swap(change)
            for f in range(2):
                value = (
                    coef_ref[f, 0] * total
                    + coef_ref[f, 1] * total_swap
                    + coef_ref[f, 3] * change
                    - coef_ref[f, 2] * change_swap
                )
                item = f * 4 + comp
                for q in range(4):
                    out_ref[where, 16 * q + 2 * item : 16 * q + 2 * item + 2, :] = value[
                        2 * q : 2 * q + 2, :
                    ]
        return 0

    lax.fori_loop(0, 16, one_block, 0)


def combine(parts, coef, place):
    return pl.pallas_call(
        combine_kernel,
        in_specs=[vmem(), smem(), smem()],
        out_specs=vmem(),
        out_shape=jax.ShapeDtypeStruct((16, 64, 128), F32),
        compiler_params=params(),
        name="combine",
    )(parts, coef, place)


def on_device(x_table, y_table, e, h, material, eps, src_pos, src_amp, freqs):
    row_place = lax.axis_index(GX)
    col_place = lax.axis_index("gy")
    place = jnp.stack([row_place, col_place]).astype(jnp.int32)
    left, right = pack_cols(e, h, material, eps)
    from_left = lax.ppermute(right, "gy", [(k, k + 1) for k in range(7)])
    from_right = lax.ppermute(left, "gy", [(k + 1, k) for k in range(7)])
    pos = src_pos.T.reshape(3, NSRC // 128, 128)
    amp = src_amp.reshape(NSRC // 128, 128)
    scale, grid = prepare(material, eps, pos, amp, place)
    up, down = pack_rows(e, h, scale, from_left, from_right)
    from_top = lax.ppermute(down, GX, [(k, k + 1) for k in range(15)])
    from_bottom = lax.ppermute(up, GX, [(k + 1, k) for k in range(15)])
    rims = (from_left, from_right, from_top, from_bottom)
    (face,) = yee(False, True, e, h, scale, grid, rims, place)
    e_out, h_out = yee(True, False, e, h, scale, grid, rims, place)

    half = jnp.cos(freqs * 0.5), jnp.sin(freqs * 0.5)
    turn = jnp.cos(freqs * 1.5), jnp.sin(freqs * 1.5)
    coef = jnp.stack(
        [turn[0] * half[0], turn[1] * half[0], turn[0] * half[1], turn[1] * half[1]], 1
    ) * (1.0 / N)

    face = lax.all_to_all(face, GX, 0, 0, tiled=True)
    rows = jnp.dot(x_table, face.reshape(N, 256), preferred_element_type=F32).astype(BF16)
    rows = lax.all_to_all(rows.reshape(16, 80, 256), ("gc", "gy"), 0, 0, tiled=True)
    far = columns(rows, y_table)
    far = lax.all_to_all(far.reshape(128, 8, 128), GX + ("gy",), 0, 0, tiled=True)
    far = combine(far, coef, place)
    return e_out, h_out, far.reshape(64, 8, 2, 128)


def solution(mesh):
    fine = Mesh(mesh.devices.reshape(8, 2, 8), ("ga", "gc", "gy"))
    field = P(None, None, GX, "gy")
    placed = (P(), P(), field, field, P(None, GX, "gy"), P(), P(), P(), P())
    mapped = jax.shard_map(
        on_device,
        mesh=fine,
        in_specs=placed,
        out_specs=(field, field, P(GX, None, None, "gy")),
        check_vma=False,
    )
    x_table, y_table = tables()

    def program(e_field, h_field, material, eps_table, src_pos, src_amp, freqs):
        return mapped(
            x_table, y_table, e_field, h_field, material, eps_table, src_pos, src_amp, freqs
        )

    return program
```

```python
import functools
import math

import jax
import jax.numpy as jnp
import ml_dtypes
import numpy as np
from jax import lax
from jax.experimental import pallas as pl
from jax.experimental.pallas import tpu as pltpu
from jax.sharding import Mesh, PartitionSpec as P

LZ = 3
NA = 1024
NMAT = 8
N = 4096
NSRC = 4096
ROWS = 256
COLS = 512
OFF = 8
EXT_R = 280
EXT_C = 640
TILES = 5
GROUP = 4
USED_R = 272
CHUNKS = 4
courant = 0.5
source_rate = 0.7
PERIOD = 4 * N
GX = ("ga", "gc")
MIB = 1 << 20
F32 = jnp.float32
BF16 = jnp.bfloat16


def tables():
    cell = np.arange(N, dtype=np.int64)
    t = np.arange(16)[:, None, None]
    q = np.arange(5)[None, :, None]
    m = np.arange(8)[None, None, :]
    w = (64 * m + 4 * t + q)[..., None]
    phase = np.remainder(w * cell, PERIOD) * (2.0 * math.pi / PERIOD)
    x_table = np.stack([np.cos(phase), np.sin(phase)], 2).reshape(16 * 80, N)
    v = np.arange(NA, dtype=np.int64) + NA // 4
    phase = np.remainder(cell[:, None] * v[None, :], PERIOD) * (2.0 * math.pi / PERIOD)
    y_table = np.concatenate([np.cos(phase), -np.sin(phase)], 1)
    y_table = y_table.reshape(8, 2, 256, 2 * NA).transpose(1, 0, 2, 3).reshape(16, 256, 2 * NA)
    return x_table.astype(ml_dtypes.bfloat16), y_table.astype(ml_dtypes.bfloat16)


def params(mib):
    return pltpu.CompilerParams(vmem_limit_bytes=mib * MIB)


def vmem():
    return pl.BlockSpec(memory_space=pltpu.VMEM)


def smem():
    return pl.BlockSpec(memory_space=pltpu.SMEM)


def scale_of(material, eps_ref):
    shape = (8, material.shape[-1])
    scale = None
    for k in range(NMAT):
        rate = (courant / jnp.full(shape, eps_ref[k], F32))[0:1]
        scale = rate if scale is None else jnp.where(material == k, rate, scale)
    return scale


def scale_kernel(material_ref, eps_ref, scale_ref):
    def strip(s, _):
        r = pl.multiple_of(s * 16, 16)
        for layer in range(LZ):
            scale_ref[layer, pl.ds(r, 16), :] = scale_of(
                material_ref[layer, pl.ds(r, 16), :], eps_ref
            )
        return 0

    lax.fori_loop(0, ROWS // 16, strip, 0)


def scales(material, eps):
    return pl.pallas_call(
        scale_kernel,
        in_specs=[vmem(), smem()],
        out_specs=vmem(),
        out_shape=jax.ShapeDtypeStruct((LZ, ROWS, COLS), F32),
        compiler_params=params(8),
        cost_estimate=pl.CostEstimate(
            flops=1_500_000_000, bytes_accessed=3_000_000, transcendentals=0
        ),
        name="scales",
    )(material, eps)


def pack_rows_kernel(e_lo, e_hi, h_lo, h_hi, m_lo, m_hi, eps_ref, up_ref, down_ref):
    sub = lax.broadcasted_iota(jnp.int32, (8, COLS), 0)
    up = down = None
    for a in range(7):
        for layer in range(LZ):
            index = a * LZ + layer
            if a < 3:
                lo, hi = e_lo[a, layer], e_hi[a, layer]
            elif a < 6:
                lo, hi = h_lo[a - 3, layer], h_hi[a - 3, layer]
            else:
                lo, hi = scale_of(m_lo[layer], eps_ref), scale_of(m_hi[layer], eps_ref)
            p = 2 * (index % 4)
            if p == 0:
                up = jnp.zeros((8, COLS), F32)
                down = jnp.zeros((8, COLS), F32)
            here = (sub == p) | (sub == p + 1)
            up = jnp.where(here, pltpu.roll(lo, p, 0) if p else lo, up)
            down = jnp.where(here, pltpu.roll(hi, (p + 2) % 8, 0) if p != 6 else hi, down)
            tile = index // 4
            up_ref[8 * tile : 8 * tile + 8, :] = up
            down_ref[8 * tile : 8 * tile + 8, :] = down


def pack_rows(e, h, material, eps):
    last = ROWS // 8 - 1
    lo4 = pl.BlockSpec((3, LZ, 8, COLS), lambda r: (0, 0, 0, 0))
    hi4 = pl.BlockSpec((3, LZ, 8, COLS), lambda r: (0, 0, last, 0))
    lo3 = pl.BlockSpec((LZ, 8, COLS), lambda r: (0, 0, 0))
    hi3 = pl.BlockSpec((LZ, 8, COLS), lambda r: (0, last, 0))
    out = pl.BlockSpec((48, COLS), lambda r: (0, 0))
    return pl.pallas_call(
        pack_rows_kernel,
        grid=(1,),
        in_specs=[lo4, hi4, lo4, hi4, lo3, hi3, smem()],
        out_specs=[out, out],
        out_shape=[jax.ShapeDtypeStruct((48, COLS), F32)] * 2,
        compiler_params=params(8),
        name="pack_rows",
    )(e, e, h, h, material, material, eps)


def rim_rows(packed, index, to_top):
    p, tile = 2 * (index % 4), index // 4
    value = packed[8 * tile : 8 * tile + 8, :]
    sub = lax.broadcasted_iota(jnp.int32, value.shape, 0)
    shift = (6 - p) % 8 if to_top else (8 - p) % 8
    value = pltpu.roll(value, shift, 0) if shift else value
    return jnp.where(sub >= 6 if to_top else sub < 2, value, 0.0)


def pack_cols_kernel(
    e_lo, e_hi, h_lo, h_hi, s_lo, s_hi, top_lo, top_hi, bot_lo, bot_hi, left_ref, right_ref
):
    rows = 32

    def packed(pair_of, shape):
        lane = lax.broadcasted_iota(jnp.int32, shape, 1)
        left = jnp.zeros(shape, F32)
        right = jnp.zeros(shape, F32)
        for index in range(7 * LZ):
            q = 2 * index
            lo, hi = pair_of(index)
            here = (lane == q) | (lane == q + 1)
            left = jnp.where(here, pltpu.roll(lo, q, 1) if q else lo, left)
            right = jnp.where(here, pltpu.roll(hi, q + 2, 1), right)
        return left, right

    def strip(s, _):
        r = pl.multiple_of(s * rows, rows)
        span = pl.ds(r, rows)

        def pair_of(index):
            a, layer = index // LZ, index % LZ
            if a < 3:
                return e_lo[a, layer, span, :], e_hi[a, layer, span, :]
            if a < 6:
                return h_lo[a - 3, layer, span, :], h_hi[a - 3, layer, span, :]
            return s_lo[layer, span, :], s_hi[layer, span, :]

        left, right = packed(pair_of, (rows, 128))
        target = pl.ds(pl.multiple_of(r + OFF, 8), rows)
        left_ref[target, :] = left
        right_ref[target, :] = right
        return 0

    lax.fori_loop(0, ROWS // rows, strip, 0)
    for to_top, lo, hi, r in ((True, top_lo, top_hi, 0), (False, bot_lo, bot_hi, ROWS + OFF)):
        left, right = packed(
            lambda index: (rim_rows(lo, index, to_top), rim_rows(hi, index, to_top)), (8, 128)
        )
        left_ref[r : r + 8, :] = left
        right_ref[r : r + 8, :] = right


def pack_cols(e, h, scale, from_top, from_bottom):
    end = COLS // 128 - 1
    lo4 = pl.BlockSpec((3, LZ, ROWS, 128), lambda r: (0, 0, 0, 0))
    hi4 = pl.BlockSpec((3, LZ, ROWS, 128), lambda r: (0, 0, 0, end))
    lo3 = pl.BlockSpec((LZ, ROWS, 128), lambda r: (0, 0, 0))
    hi3 = pl.BlockSpec((LZ, ROWS, 128), lambda r: (0, 0, end))
    lo2 = pl.BlockSpec((48, 128), lambda r: (0, 0))
    hi2 = pl.BlockSpec((48, 128), lambda r: (0, end))
    out = pl.BlockSpec((USED_R, 128), lambda r: (0, 0))
    return pl.pallas_call(
        pack_cols_kernel,
        grid=(1,),
        in_specs=[lo4, hi4, lo4, hi4, lo3, hi3, lo2, hi2, lo2, hi2],
        out_specs=[out, out],
        out_shape=[jax.ShapeDtypeStruct((USED_R, 128), F32)] * 2,
        compiler_params=params(16),
        name="pack_cols",
    )(e, e, h, h, scale, scale, from_top, from_top, from_bottom, from_bottom)


def rim_tile(from_left, from_right, index):
    lane = lax.broadcasted_iota(jnp.int32, from_left.shape, 1)
    q = 2 * index
    right = pltpu.roll(from_right, 128 - q, 1) if q else from_right
    left = pltpu.roll(from_left, 126 - q, 1)
    return jnp.where(lane < 2, right, jnp.where(lane >= 126, left, 0.0))


def sources_kernel(pos_ref, amp_ref, place_ref, grid_ref):
    groups = NSRC // 128
    row = pos_ref[1] - place_ref[0] * ROWS + OFF
    col = pos_ref[2] - place_ref[1] * COLS
    inside = (row >= OFF - 1) & (row <= ROWS + OFF) & (col >= -1) & (col <= COLS)
    col = jnp.where(col < 0, EXT_C - 1, col)
    taken = jnp.where(inside, 1.0, 0.0)
    lane_a = lax.broadcasted_iota(jnp.int32, (128, 128), 0)
    lane_b = lax.broadcasted_iota(jnp.int32, (128, 128), 1)
    before = jnp.where(lane_a < lane_b, 1.0, 0.0).astype(BF16)
    group_a = lax.broadcasted_iota(jnp.int32, (groups, groups), 0)
    group_b = lax.broadcasted_iota(jnp.int32, (groups, groups), 1)
    earlier = jnp.where(group_b < group_a, 1.0, 0.0).astype(BF16)
    in_group = jnp.dot(taken.astype(BF16), before, preferred_element_type=F32)
    ahead = jnp.dot(earlier, taken.astype(BF16), preferred_element_type=F32)
    rank = in_group + jnp.sum(ahead, axis=1, keepdims=True)
    rank = jnp.where(inside, rank, -1.0)
    features = (
        row.astype(F32),
        col.astype(F32),
        pos_ref[0].astype(F32),
        amp_ref[...],
    )
    count = jnp.sum(taken).astype(jnp.int32)
    slot = lax.broadcasted_iota(jnp.int32, (128, 128), 0).astype(F32)
    feature_lane = lax.broadcasted_iota(jnp.int32, (128, 128), 1)
    row_of = lax.broadcasted_iota(jnp.int32, (USED_R, 128), 0).astype(F32)
    col_of = lax.broadcasted_iota(jnp.int32, (EXT_C, 128), 0).astype(F32)
    grid_ref[...] = jnp.zeros(grid_ref.shape, F32)

    def one_pass(p, _):
        base = (p * 128).astype(F32)
        sums = [jnp.zeros((128, 128), F32) for _ in features]
        found = jnp.zeros((128, 128), F32)
        for g in range(groups):
            chosen = slot == rank[g : g + 1, :] - base
            found = jnp.where(chosen, 1.0, found)
            for f, feature in enumerate(features):
                sums[f] = jnp.where(chosen, feature[g : g + 1, :], sums[f])
        packed = jnp.zeros((128, 128), F32)
        for f, total in enumerate(sums + [found]):
            packed = jnp.where(feature_lane == f, jnp.sum(total, axis=1, keepdims=True), packed)
        packed = packed.T
        src_row, src_col, src_layer = packed[0:1], packed[1:2], packed[2:3]
        amp, valid = packed[3:4], packed[4:5]
        amp_1 = amp.astype(BF16).astype(F32)
        amp_2 = (amp - amp_1).astype(BF16).astype(F32)
        amp_3 = amp - amp_1 - amp_2
        at_col = jnp.where(col_of == src_col, 1.0, 0.0).astype(BF16)
        at_col = jnp.concatenate([at_col] * 3, 1)
        for layer in range(LZ):
            at_row = (row_of == src_row) & (src_layer == layer) & (valid > 0.0)
            weights = jnp.concatenate(
                [jnp.where(at_row, part, 0.0).astype(BF16) for part in (amp_1, amp_2, amp_3)], 1
            )
            added = lax.dot_general(
                weights, at_col, (((1,), (1,)), ((), ())), preferred_element_type=F32
            )
            for tile in range(TILES):
                grid_ref[layer, tile] += added[:, 128 * tile : 128 * tile + 128]
        return 0

    lax.fori_loop(0, (count + 127) // 128, one_pass, 0)


def sources(pos, amp, place):
    return pl.pallas_call(
        sources_kernel,
        in_specs=[vmem(), vmem(), smem()],
        out_specs=vmem(),
        out_shape=jax.ShapeDtypeStruct((LZ, TILES, USED_R, 128), F32),
        compiler_params=params(12),
        cost_estimate=pl.CostEstimate(
            flops=3_000_000_000, bytes_accessed=3_000_000, transcendentals=0
        ),
        name="sources",
    )(pos, amp, place)


def yee_kernel(
    with_fields,
    with_face,
    e_in,
    h_in,
    scale_in,
    grid_in,
    from_left,
    from_right,
    from_top,
    from_bottom,
    place_ref,
    *refs,
):
    refs = list(refs)
    e_out, h_out = (refs.pop(0), refs.pop(0)) if with_fields else (None, None)
    face_out = refs.pop(0) if with_face else None
    e, h, scale, grid = refs[:4]
    refs = refs[4:]
    first = refs.pop(0) if with_face else None
    in_sem, grid_sem, out_sem = refs
    span = ROWS // CHUNKS
    own_tiles = COLS // 128

    arrivals = []
    for chunk in range(CHUNKS):
        here = []
        source_rows = pl.ds(chunk * span, span)
        target_rows = pl.ds(OFF + chunk * span, span)
        for tile in range(own_tiles):
            cols = pl.ds(128 * tile, 128)
            pairs = (
                (e_in.at[:, :, source_rows, cols], e.at[:, :, tile, target_rows, :]),
                (h_in.at[:, :, source_rows, cols], h.at[:, :, tile, target_rows, :]),
                (scale_in.at[:, source_rows, cols], scale.at[:, tile, target_rows, :]),
            )
            for source, target in pairs:
                copy = pltpu.make_async_copy(source, target, in_sem.at[chunk, len(here)])
                copy.start()
                here.append(copy)
        arrivals.append(here)
    grid_copy = pltpu.make_async_copy(grid_in, grid, grid_sem)
    grid_copy.start()

    sub = lax.broadcasted_iota(jnp.int32, (8, 128), 0)
    lane = lax.broadcasted_iota(jnp.int32, (8, 128), 1)

    def array_of(a, layer):
        if a < 3:
            return e.at[a, layer]
        if a < 6:
            return h.at[a - 3, layer]
        return scale.at[layer]

    for index in range(7 * LZ):
        target = array_of(index // LZ, index % LZ)
        top = rim_rows(from_top, index, True)
        bottom = rim_rows(from_bottom, index, False)
        for tile in range(own_tiles):
            cols = slice(128 * tile, 128 * tile + 128)
            target[tile, 0:8, :] = top[:, cols]
            target[tile, ROWS + OFF : ROWS + OFF + 8, :] = bottom[:, cols]
        for tile in range(TILES):
            target[tile, USED_R : USED_R + 8, :] = jnp.zeros((8, 128), F32)

    def rim_strip(s, _):
        r = pl.multiple_of(s * 8, 8)
        left = from_left[pl.ds(r, 8), :]
        right = from_right[pl.ds(r, 8), :]
        for index in range(7 * LZ):
            array_of(index // LZ, index % LZ)[own_tiles, pl.ds(r, 8), :] = rim_tile(
                left, right, index
            )
        return 0

    lax.fori_loop(0, USED_R // 8, rim_strip, 0)

    row_place, col_place = place_ref[0], place_ref[1]
    rim_half = jnp.full((8, 128), courant, F32)
    rim_half = jnp.where((lane >= 64) & (col_place == 0), 0.0, rim_half)
    rim_half = jnp.where((lane < 64) & (col_place == 7), 0.0, rim_half)
    inner_half = jnp.full((8, 128), courant, F32)
    half = [inner_half] * own_tiles + [rim_half]
    half_top = [jnp.where(row_place == 0, 0.0, value) for value in half]
    half_bottom = [jnp.where(row_place == 15, 0.0, value) for value in half]

    def load(ref, a, layer, r):
        return [ref[a, layer, tile, pl.ds(r, 8), :] for tile in range(TILES)]

    def y_next(here):
        moved = [pltpu.roll(value, 127, 1) for value in here]
        return [
            jnp.where(lane == 127, moved[(tile + 1) % TILES], moved[tile]) for tile in range(TILES)
        ]

    def y_last(here):
        moved = [pltpu.roll(value, 1, 1) for value in here]
        return [
            jnp.where(lane == 0, moved[(tile - 1) % TILES], moved[tile]) for tile in range(TILES)
        ]

    zero = [jnp.zeros((8, 128), F32)] * TILES

    def update_h(r, coef):
        for layer in range(LZ):
            ex, ey, ez = (load(e, a, layer, r) for a in range(3))
            top = layer + 1 == LZ
            ex_up = zero if top else load(e, 0, layer + 1, r)
            ey_up = zero if top else load(e, 1, layer + 1, r)
            ey_x, ez_x = load(e, 1, layer, r + 1), load(e, 2, layer, r + 1)
            ex_y, ez_y = y_next(ex), y_next(ez)
            for t in range(TILES):
                curls = (
                    ez_y[t] - ez[t] - (ey_up[t] - ey[t]),
                    ex_up[t] - ex[t] - (ez_x[t] - ez[t]),
                    ey_x[t] - ey[t] - (ex_y[t] - ex[t]),
                )
                for a in range(3):
                    h[a, layer, t, pl.ds(r, 8), :] -= coef[t] * curls[a]

    def update_e(r, moment):
        strength = math.sin(source_rate * moment)
        for layer in range(LZ):
            hx, hy, hz = (load(h, a, layer, r) for a in range(3))
            hx_low = load(h, 0, layer - 1, r) if layer else zero
            hy_low = load(h, 1, layer - 1, r) if layer else zero
            if isinstance(r, int) and r == 0:
                hy_x = [pltpu.roll(value, 1, 0) for value in hy]
                hz_x = [pltpu.roll(value, 1, 0) for value in hz]
            else:
                hy_x, hz_x = load(h, 1, layer, r - 1), load(h, 2, layer, r - 1)
            hx_y, hz_y = y_last(hx), y_last(hz)
            for t in range(TILES):
                rows = pl.ds(r, 8)
                rate = scale[layer, t, rows, :]
                e[0, layer, t, rows, :] += rate * (hz[t] - hz_y[t] - (hy[t] - hy_low[t]))
                e[1, layer, t, rows, :] += rate * (hx[t] - hx_low[t] - (hz[t] - hz_x[t]))
                e[2, layer, t, rows, :] = (
                    e[2, layer, t, rows, :]
                    + rate * (hy[t] - hy_x[t] - (hx[t] - hx_y[t]))
                    + strength * grid[layer, t, rows, :]
                )

    face_of = ((h, 1, -1.0), (h, 0, 1.0), (e, 1, 1.0), (e, 0, -1.0))

    def first_step(s, _):
        r = pl.multiple_of(s * 8, 8)
        update_h(r, half)
        update_e(r, 1.0)
        if with_face:
            for k, (ref, a, _sign) in enumerate(face_of):
                for tile in range(own_tiles):
                    first[k, tile, pl.ds(pl.multiple_of(r - OFF, 8), 8), :] = ref[
                        a, 1, tile, pl.ds(r, 8), :
                    ]
        return 0

    def second_step(s, _):
        own = pl.multiple_of(s * 16, 16)
        for part in range(2):
            r = pl.multiple_of(own + OFF + 8 * part, 8)
            update_h(r, half)
            update_e(r, 2.0)
        if with_face:
            now_rows = pl.ds(pl.multiple_of(own + OFF, 8), 16)
            for k, (ref, a, sign) in enumerate(face_of):
                for tile in range(own_tiles):
                    then = first[k, tile, pl.ds(own, 16), :]
                    now = ref[a, 1, tile, now_rows, :]
                    cols = pl.ds(128 * (tile % 2), 128)
                    target = 4 * k + tile // 2
                    face_out[target, pl.ds(own, 16), cols] = (sign * (then + now)).astype(BF16)
                    face_out[target + 2, pl.ds(own, 16), cols] = (sign * (then - now)).astype(BF16)
        return 0

    strips = span // 8
    for copy in arrivals[0]:
        copy.wait()
    grid_copy.wait()
    update_h(0, half_top)
    update_e(0, 1.0)
    for chunk in range(CHUNKS):
        begin = 1 + chunk * strips
        if chunk + 1 < CHUNKS:
            lax.fori_loop(begin, begin + strips - 1, first_step, 0)
            for copy in arrivals[chunk + 1]:
                copy.wait()
            first_step(jnp.int32(begin + strips - 1), 0)
        else:
            lax.fori_loop(begin, begin + strips, first_step, 0)
    update_h(ROWS + OFF, half_bottom)
    update_e(ROWS + OFF, 1.0)

    update_h(0, half_top)
    sent = []
    for chunk in range(CHUNKS):
        lax.fori_loop(chunk * (span // 16), (chunk + 1) * (span // 16), second_step, 0)
        if with_fields:
            source_rows = pl.ds(OFF + chunk * span, span)
            target_rows = pl.ds(chunk * span, span)
            for tile in range(own_tiles):
                cols = pl.ds(128 * tile, 128)
                for source, target in ((e, e_out), (h, h_out)):
                    copy = pltpu.make_async_copy(
                        source.at[:, :, tile, source_rows, :],
                        target.at[:, :, target_rows, cols],
                        out_sem.at[len(sent)],
                    )
                    copy.start()
                    sent.append(copy)
    for copy in sent:
        copy.wait()


def yee(with_fields, with_face, e, h, scale, grid, rims, place):
    field = jax.ShapeDtypeStruct((3, LZ, ROWS, COLS), F32)
    anywhere = pl.BlockSpec(memory_space=pl.ANY)
    out_shape = []
    out_specs = []
    scratch = [
        pltpu.VMEM((3, LZ, TILES, EXT_R, 128), F32),
        pltpu.VMEM((3, LZ, TILES, EXT_R, 128), F32),
        pltpu.VMEM((LZ, TILES, EXT_R, 128), F32),
        pltpu.VMEM((LZ, TILES, USED_R, 128), F32),
    ]
    if with_fields:
        out_shape += [field, field]
        out_specs += [anywhere, anywhere]
    if with_face:
        out_shape.append(jax.ShapeDtypeStruct((16, ROWS, 256), BF16))
        out_specs.append(vmem())
        scratch.append(pltpu.VMEM((4, COLS // 128, ROWS, 128), F32))
    scratch += [
        pltpu.SemaphoreType.DMA((CHUNKS, 3 * COLS // 128)),
        pltpu.SemaphoreType.DMA,
        pltpu.SemaphoreType.DMA((CHUNKS * 2 * COLS // 128,)),
    ]
    return pl.pallas_call(
        functools.partial(yee_kernel, with_fields, with_face),
        in_specs=[anywhere] * 4 + [vmem()] * 4 + [smem()],
        out_specs=out_specs,
        out_shape=out_shape,
        scratch_shapes=scratch,
        compiler_params=params(28),
        cost_estimate=pl.CostEstimate(
            flops=5_000_000_000, bytes_accessed=40_000_000, transcendentals=0
        ),
        name="yee_fields" if with_fields else "yee_face",
    )(e, h, scale, grid, *rims, place)


def rows_kernel(field_ref, table_ref, out_ref):
    total = jnp.dot(table_ref[...], field_ref[...], preferred_element_type=F32)
    out_ref[...] = total.astype(BF16)


def rows_transform(field, table):
    step = 320
    return pl.pallas_call(
        rows_kernel,
        grid=(1280 // step,),
        in_specs=[
            pl.BlockSpec((N, 256), lambda t: (0, 0)),
            pl.BlockSpec((step, N), lambda t: (t, 0)),
        ],
        out_specs=pl.BlockSpec((step, 256), lambda t: (t, 0)),
        out_shape=jax.ShapeDtypeStruct((1280, 256), BF16),
        compiler_params=params(16),
        name="rows_transform",
    )(field, table)


def columns_kernel(rows_ref, table_ref, out_ref, total, spread):
    step = pl.program_id(0)
    part = jnp.dot(rows_ref[0], table_ref[0], preferred_element_type=F32)
    for g in range(1, GROUP):
        part += jnp.dot(rows_ref[g], table_ref[g], preferred_element_type=F32)

    @pl.when(step == 0)
    def _():
        total[...] = part

    @pl.when(step > 0)
    def _():
        total[...] += part

    @pl.when(step == 16 // GROUP - 1)
    def _():
        sub = lax.broadcasted_iota(jnp.int32, (8, NA), 0)

        def flip(value):
            value = pltpu.roll(value, 4, 0)
            value = jnp.where(sub % 4 < 2, pltpu.roll(value, 6, 0), pltpu.roll(value, 2, 0))
            return jnp.where(sub % 2 == 0, pltpu.roll(value, 7, 0), pltpu.roll(value, 1, 0))

        for q in range(4):
            for plus in (True, False):
                base = 16 * (q if plus else 4 - q)
                cos_re, cos_im = total[base : base + 8, 0:NA], total[base : base + 8, NA : 2 * NA]
                sin_re = total[base + 8 : base + 16, 0:NA]
                sin_im = total[base + 8 : base + 16, NA : 2 * NA]
                if plus:
                    parts = (cos_re + sin_im, cos_im - sin_re)
                else:
                    parts = (flip(cos_re - sin_im), flip(cos_im + sin_re))
                for ri, value in enumerate(parts):
                    for j in range(8):
                        start = ((8 if plus else 0) * 8 + j) * 8 + 2 * q + ri
                        spread[pl.ds(start, 8, stride=64), :] = value[:, 128 * j : 128 * j + 128]
        out_ref[...] = spread[...].astype(BF16)


def columns(rows, table):
    return pl.pallas_call(
        columns_kernel,
        grid=(16 // GROUP,),
        in_specs=[
            pl.BlockSpec((GROUP, 80, 256), lambda t: (t, 0, 0)),
            pl.BlockSpec((GROUP, 256, 2 * NA), lambda t: (t, 0, 0)),
        ],
        out_specs=pl.BlockSpec((1024, 128), lambda t: (0, 0)),
        out_shape=jax.ShapeDtypeStruct((1024, 128), BF16),
        scratch_shapes=[pltpu.VMEM((80, 2 * NA), F32), pltpu.VMEM((1024, 128), F32)],
        compiler_params=params(24),
        name="columns",
    )(rows, table)


def combine_kernel(parts_ref, coef_ref, place_ref, out_ref):
    sub = lax.broadcasted_iota(jnp.int32, (8, 128), 0)
    real_row = (sub % 2) == 0
    side = jnp.where(real_row, -1.0, 1.0)

    def swap(value):
        return jnp.where(real_row, pltpu.roll(value, 7, 0), pltpu.roll(value, 1, 0)) * side

    def two_blocks(pair, _):
        for comp in range(4):
            totals = parts_ref[(2 * comp) * 8 + pair].astype(F32)
            changes = parts_ref[(2 * comp + 1) * 8 + pair].astype(F32)
            for odd in range(2):
                t = 2 * pair + odd
                where = jnp.where(place_ref[0] >= 8, t, 15 - t)
                total = totals[8 * odd : 8 * odd + 8]
                change = changes[8 * odd : 8 * odd + 8]
                total_swap, change_swap = swap(total), swap(change)
                for f in range(2):
                    value = (
                        coef_ref[f, 0] * total
                        + coef_ref[f, 1] * total_swap
                        + coef_ref[f, 3] * change
                        - coef_ref[f, 2] * change_swap
                    )
                    item = f * 4 + comp
                    for q in range(4):
                        out_ref[where, 16 * q + 2 * item : 16 * q + 2 * item + 2, :] = value[
                            2 * q : 2 * q + 2, :
                        ]
        return 0

    lax.fori_loop(0, 8, two_blocks, 0)


def combine(parts, coef, place):
    return pl.pallas_call(
        combine_kernel,
        in_specs=[vmem(), smem(), smem()],
        out_specs=vmem(),
        out_shape=jax.ShapeDtypeStruct((16, 64, 128), F32),
        compiler_params=params(8),
        name="combine",
    )(parts, coef, place)


def on_device(x_table, y_table, e, h, material, eps, src_pos, src_amp, freqs):
    row_place = lax.axis_index(GX)
    col_place = lax.axis_index("gy")
    place = jnp.stack([row_place, col_place]).astype(jnp.int32)
    up, down = pack_rows(e, h, material, eps)
    from_top = lax.ppermute(down, GX, [(k, k + 1) for k in range(15)])
    from_bottom = lax.ppermute(up, GX, [(k + 1, k) for k in range(15)])
    scale = scales(material, eps)
    left, right = pack_cols(e, h, scale, from_top, from_bottom)
    from_left = lax.ppermute(right, "gy", [(k, k + 1) for k in range(7)])
    from_right = lax.ppermute(left, "gy", [(k + 1, k) for k in range(7)])
    pos = src_pos.T.reshape(3, NSRC // 128, 128)
    amp = src_amp.reshape(NSRC // 128, 128)
    pos, amp, left = lax.optimization_barrier((pos, amp, left))
    grid = sources(pos, amp, place)
    rims = (from_left, from_right, from_top, from_bottom)
    (face,) = yee(False, True, e, h, scale, grid, rims, place)
    e_out, h_out = yee(True, False, e, h, scale, grid, rims, place)

    half = jnp.cos(freqs * 0.5), jnp.sin(freqs * 0.5)
    turn = jnp.cos(freqs * 1.5), jnp.sin(freqs * 1.5)
    coef = jnp.stack(
        [turn[0] * half[0], turn[1] * half[0], turn[0] * half[1], turn[1] * half[1]], 1
    ) * (1.0 / N)

    face = lax.all_to_all(face, GX, 0, 0, tiled=True)
    face, e_out, h_out = lax.optimization_barrier((face, e_out, h_out))
    rows = rows_transform(face.reshape(N, 256), x_table)
    rows = lax.all_to_all(rows.reshape(16, 80, 256), ("gc", "gy"), 0, 0, tiled=True)
    far = columns(rows, y_table)
    far = lax.all_to_all(far.reshape(128, 8, 128), GX + ("gy",), 0, 0, tiled=True)
    far = combine(far.reshape(64, 16, 128), coef, place)
    return e_out, h_out, far.reshape(64, 8, 2, 128)


def solution(mesh):
    fine = Mesh(mesh.devices.reshape(8, 2, 8), ("ga", "gc", "gy"))
    field = P(None, None, GX, "gy")
    placed = (P(), P(), field, field, P(None, GX, "gy"), P(), P(), P(), P())
    mapped = jax.shard_map(
        on_device,
        mesh=fine,
        in_specs=placed,
        out_specs=(field, field, P(GX, None, None, "gy")),
        check_vma=False,
    )
    x_table, y_table = tables()

    def program(e_field, h_field, material, eps_table, src_pos, src_amp, freqs):
        return mapped(
            x_table, y_table, e_field, h_field, material, eps_table, src_pos, src_amp, freqs
        )

    return program
```

```python
import functools
import math

import jax
import jax.numpy as jnp
import ml_dtypes
import numpy as np
from jax import lax
from jax.experimental import pallas as pl
from jax.experimental.pallas import tpu as pltpu
from jax.sharding import Mesh, PartitionSpec as P

LZ = 3
NA = 1024
NMAT = 8
N = 4096
NSRC = 4096
ROWS = 256
COLS = 512
OFF = 8
EXT_R = 280
EXT_C = 640
TILES = 5
GROUP = 4
USED_R = 272
CHUNKS = 2
courant = 0.5
source_rate = 0.7
PERIOD = 4 * N
GX = ("ga", "gc")
MIB = 1 << 20
F32 = jnp.float32
BF16 = jnp.bfloat16


def tables():
    cell = np.arange(N, dtype=np.int64)
    t = np.arange(16)[:, None, None]
    q = np.arange(5)[None, :, None]
    m = np.arange(8)[None, None, :]
    w = (64 * m + 4 * t + q)[..., None]
    phase = np.remainder(w * cell, PERIOD) * (2.0 * math.pi / PERIOD)
    x_table = np.stack([np.cos(phase), np.sin(phase)], 2).reshape(16 * 80, N)
    v = np.arange(NA, dtype=np.int64) + NA // 4
    phase = np.remainder(cell[:, None] * v[None, :], PERIOD) * (2.0 * math.pi / PERIOD)
    y_table = np.concatenate([np.cos(phase), -np.sin(phase)], 1)
    y_table = y_table.reshape(8, 2, 256, 2 * NA).transpose(1, 0, 2, 3).reshape(16, 256, 2 * NA)
    return x_table.astype(ml_dtypes.bfloat16), y_table.astype(ml_dtypes.bfloat16)


def params(mib):
    return pltpu.CompilerParams(vmem_limit_bytes=mib * MIB)


def stay(*arrays):
    return [pltpu.with_memory_space_constraint(array, pltpu.HBM) for array in arrays]


def vmem():
    return pl.BlockSpec(memory_space=pltpu.VMEM)


def smem():
    return pl.BlockSpec(memory_space=pltpu.SMEM)


def scale_of(material, eps_ref):
    shape = (8, material.shape[-1])
    scale = None
    for k in range(NMAT):
        rate = (courant / jnp.full(shape, eps_ref[k], F32))[0:1]
        scale = rate if scale is None else jnp.where(material == k, rate, scale)
    return scale


def scale_kernel(material_ref, eps_ref, scale_ref):
    def strip(s, _):
        r = pl.multiple_of(s * 16, 16)
        for layer in range(LZ):
            scale_ref[layer, pl.ds(r, 16), :] = scale_of(
                material_ref[layer, pl.ds(r, 16), :], eps_ref
            )
        return 0

    lax.fori_loop(0, ROWS // 16, strip, 0)


def scales(material, eps):
    return pl.pallas_call(
        scale_kernel,
        in_specs=[vmem(), smem()],
        out_specs=vmem(),
        out_shape=jax.ShapeDtypeStruct((LZ, ROWS, COLS), F32),
        compiler_params=params(8),
        cost_estimate=pl.CostEstimate(
            flops=1_500_000_000, bytes_accessed=3_000_000, transcendentals=0
        ),
        name="scales",
    )(material, eps)


def pack_rows_kernel(e_lo, e_hi, h_lo, h_hi, m_lo, m_hi, eps_ref, up_ref, down_ref):
    sub = lax.broadcasted_iota(jnp.int32, (8, COLS), 0)
    up = down = None
    for a in range(7):
        for layer in range(LZ):
            index = a * LZ + layer
            if a < 3:
                lo, hi = e_lo[a, layer], e_hi[a, layer]
            elif a < 6:
                lo, hi = h_lo[a - 3, layer], h_hi[a - 3, layer]
            else:
                lo, hi = scale_of(m_lo[layer], eps_ref), scale_of(m_hi[layer], eps_ref)
            p = 2 * (index % 4)
            if p == 0:
                up = jnp.zeros((8, COLS), F32)
                down = jnp.zeros((8, COLS), F32)
            here = (sub == p) | (sub == p + 1)
            up = jnp.where(here, pltpu.roll(lo, p, 0) if p else lo, up)
            down = jnp.where(here, pltpu.roll(hi, (p + 2) % 8, 0) if p != 6 else hi, down)
            tile = index // 4
            up_ref[8 * tile : 8 * tile + 8, :] = up
            down_ref[8 * tile : 8 * tile + 8, :] = down


def pack_rows(e, h, material, eps):
    last = ROWS // 8 - 1
    lo4 = pl.BlockSpec((3, LZ, 8, COLS), lambda r: (0, 0, 0, 0))
    hi4 = pl.BlockSpec((3, LZ, 8, COLS), lambda r: (0, 0, last, 0))
    lo3 = pl.BlockSpec((LZ, 8, COLS), lambda r: (0, 0, 0))
    hi3 = pl.BlockSpec((LZ, 8, COLS), lambda r: (0, last, 0))
    out = pl.BlockSpec((48, COLS), lambda r: (0, 0))
    return pl.pallas_call(
        pack_rows_kernel,
        grid=(1,),
        in_specs=[lo4, hi4, lo4, hi4, lo3, hi3, smem()],
        out_specs=[out, out],
        out_shape=[jax.ShapeDtypeStruct((48, COLS), F32)] * 2,
        compiler_params=params(8),
        name="pack_rows",
    )(*stay(e, e, h, h, material, material), eps)


def rim_rows(packed, index, to_top):
    p, tile = 2 * (index % 4), index // 4
    value = packed[8 * tile : 8 * tile + 8, :]
    sub = lax.broadcasted_iota(jnp.int32, value.shape, 0)
    shift = (6 - p) % 8 if to_top else (8 - p) % 8
    value = pltpu.roll(value, shift, 0) if shift else value
    return jnp.where(sub >= 6 if to_top else sub < 2, value, 0.0)


def pack_cols_kernel(
    e_lo, e_hi, h_lo, h_hi, s_lo, s_hi, top_lo, top_hi, bot_lo, bot_hi, left_ref, right_ref
):
    rows = 32

    def packed(pair_of, shape):
        lane = lax.broadcasted_iota(jnp.int32, shape, 1)
        both = jnp.zeros(shape, F32)
        for index in range(7 * LZ):
            lo, hi = pair_of(index)
            ends = pltpu.roll(jnp.where(lane < 64, lo, hi), 4 * index + 2, 1)
            both = jnp.where(lane // 4 == index, ends, both)
        return jnp.where(lane % 4 >= 2, both, 0.0), jnp.where(lane % 4 < 2, both, 0.0)

    def strip(s, _):
        r = pl.multiple_of(s * rows, rows)
        span = pl.ds(r, rows)

        def pair_of(index):
            a, layer = index // LZ, index % LZ
            if a < 3:
                return e_lo[a, layer, span, :], e_hi[a, layer, span, :]
            if a < 6:
                return h_lo[a - 3, layer, span, :], h_hi[a - 3, layer, span, :]
            return s_lo[layer, span, :], s_hi[layer, span, :]

        left, right = packed(pair_of, (rows, 128))
        target = pl.ds(pl.multiple_of(r + OFF, 8), rows)
        left_ref[target, :] = left
        right_ref[target, :] = right
        return 0

    lax.fori_loop(0, ROWS // rows, strip, 0)
    for to_top, lo, hi, r in ((True, top_lo, top_hi, 0), (False, bot_lo, bot_hi, ROWS + OFF)):
        left, right = packed(
            lambda index: (rim_rows(lo, index, to_top), rim_rows(hi, index, to_top)), (8, 128)
        )
        left_ref[r : r + 8, :] = left
        right_ref[r : r + 8, :] = right


def pack_cols(e, h, scale, from_top, from_bottom):
    end = COLS // 128 - 1
    lo4 = pl.BlockSpec((3, LZ, ROWS, 128), lambda r: (0, 0, 0, 0))
    hi4 = pl.BlockSpec((3, LZ, ROWS, 128), lambda r: (0, 0, 0, end))
    lo3 = pl.BlockSpec((LZ, ROWS, 128), lambda r: (0, 0, 0))
    hi3 = pl.BlockSpec((LZ, ROWS, 128), lambda r: (0, 0, end))
    lo2 = pl.BlockSpec((48, 128), lambda r: (0, 0))
    hi2 = pl.BlockSpec((48, 128), lambda r: (0, end))
    out = pl.BlockSpec((USED_R, 128), lambda r: (0, 0))
    return pl.pallas_call(
        pack_cols_kernel,
        grid=(1,),
        in_specs=[lo4, hi4, lo4, hi4, lo3, hi3, lo2, hi2, lo2, hi2],
        out_specs=[out, out],
        out_shape=[jax.ShapeDtypeStruct((USED_R, 128), F32)] * 2,
        compiler_params=params(16),
        name="pack_cols",
    )(*stay(e, e, h, h), scale, scale, from_top, from_top, from_bottom, from_bottom)


def rim_tile(both, index):
    lane = lax.broadcasted_iota(jnp.int32, both.shape, 1)
    moved = pltpu.roll(both, (126 - 4 * index) % 128, 1)
    return jnp.where((lane < 2) | (lane >= 126), moved, 0.0)


def sources_kernel(pos_ref, amp_ref, place_ref, grid_ref):
    groups = NSRC // 128
    row = pos_ref[1] - place_ref[0] * ROWS + OFF
    col = pos_ref[2] - place_ref[1] * COLS
    inside = (row >= OFF - 1) & (row <= ROWS + OFF) & (col >= -1) & (col <= COLS)
    col = jnp.where(col < 0, EXT_C - 1, col)
    taken = jnp.where(inside, 1.0, 0.0)
    lane_a = lax.broadcasted_iota(jnp.int32, (128, 128), 0)
    lane_b = lax.broadcasted_iota(jnp.int32, (128, 128), 1)
    before = jnp.where(lane_a < lane_b, 1.0, 0.0).astype(BF16)
    group_a = lax.broadcasted_iota(jnp.int32, (groups, groups), 0)
    group_b = lax.broadcasted_iota(jnp.int32, (groups, groups), 1)
    earlier = jnp.where(group_b < group_a, 1.0, 0.0).astype(BF16)
    in_group = jnp.dot(taken.astype(BF16), before, preferred_element_type=F32)
    ahead = jnp.dot(earlier, taken.astype(BF16), preferred_element_type=F32)
    rank = in_group + jnp.sum(ahead, axis=1, keepdims=True)
    rank = jnp.where(inside, rank, -1.0)
    features = (
        row.astype(F32),
        col.astype(F32),
        pos_ref[0].astype(F32),
        amp_ref[...],
    )
    count = jnp.sum(taken).astype(jnp.int32)
    slot = lax.broadcasted_iota(jnp.int32, (128, 128), 0).astype(F32)
    feature_lane = lax.broadcasted_iota(jnp.int32, (128, 128), 1)
    row_of = lax.broadcasted_iota(jnp.int32, (USED_R, 128), 0).astype(F32)
    col_of = lax.broadcasted_iota(jnp.int32, (EXT_C, 128), 0).astype(F32)
    grid_ref[...] = jnp.zeros(grid_ref.shape, F32)

    def one_pass(p, _):
        base = (p * 128).astype(F32)
        sums = [jnp.zeros((128, 128), F32) for _ in features]
        found = jnp.zeros((128, 128), F32)
        for g in range(groups):
            chosen = slot == rank[g : g + 1, :] - base
            found = jnp.where(chosen, 1.0, found)
            for f, feature in enumerate(features):
                sums[f] = jnp.where(chosen, feature[g : g + 1, :], sums[f])
        packed = jnp.zeros((128, 128), F32)
        for f, total in enumerate(sums + [found]):
            packed = jnp.where(feature_lane == f, jnp.sum(total, axis=1, keepdims=True), packed)
        packed = packed.T
        src_row, src_col, src_layer = packed[0:1], packed[1:2], packed[2:3]
        amp, valid = packed[3:4], packed[4:5]
        amp_1 = amp.astype(BF16).astype(F32)
        amp_2 = (amp - amp_1).astype(BF16).astype(F32)
        amp_3 = amp - amp_1 - amp_2
        at_col = jnp.where(col_of == src_col, 1.0, 0.0).astype(BF16)
        at_col = jnp.concatenate([at_col] * 3, 1)
        for layer in range(LZ):
            at_row = (row_of == src_row) & (src_layer == layer) & (valid > 0.0)
            weights = jnp.concatenate(
                [jnp.where(at_row, part, 0.0).astype(BF16) for part in (amp_1, amp_2, amp_3)], 1
            )
            added = lax.dot_general(
                weights, at_col, (((1,), (1,)), ((), ())), preferred_element_type=F32
            )
            for tile in range(TILES):
                grid_ref[layer, tile] += added[:, 128 * tile : 128 * tile + 128]
        return 0

    lax.fori_loop(0, (count + 127) // 128, one_pass, 0)


def sources(pos, amp, place):
    return pl.pallas_call(
        sources_kernel,
        in_specs=[vmem(), vmem(), smem()],
        out_specs=vmem(),
        out_shape=jax.ShapeDtypeStruct((LZ, TILES, USED_R, 128), F32),
        compiler_params=params(12),
        cost_estimate=pl.CostEstimate(
            flops=3_000_000_000, bytes_accessed=3_000_000, transcendentals=0
        ),
        name="sources",
    )(pos, amp, place)


def yee_kernel(
    with_fields,
    with_face,
    e_in,
    h_in,
    scale_in,
    grid_in,
    from_left,
    from_right,
    from_top,
    from_bottom,
    place_ref,
    *refs,
):
    refs = list(refs)
    e_out, h_out = (refs.pop(0), refs.pop(0)) if with_fields else (None, None)
    face_out = refs.pop(0) if with_face else None
    e, h, scale, grid = refs[:4]
    refs = refs[4:]
    first = refs.pop(0) if with_face else None
    in_sem, grid_sem, out_sem = refs
    span = ROWS // CHUNKS
    own_tiles = COLS // 128

    arrivals = []
    for chunk in range(CHUNKS):
        here = []
        source_rows = pl.ds(chunk * span, span)
        target_rows = pl.ds(OFF + chunk * span, span)
        for tile in range(own_tiles):
            cols = pl.ds(128 * tile, 128)
            pairs = (
                (e_in.at[:, :, source_rows, cols], e.at[:, :, tile, target_rows, :]),
                (h_in.at[:, :, source_rows, cols], h.at[:, :, tile, target_rows, :]),
                (scale_in.at[:, source_rows, cols], scale.at[:, tile, target_rows, :]),
            )
            for source, target in pairs:
                copy = pltpu.make_async_copy(source, target, in_sem.at[chunk, len(here)])
                copy.start()
                here.append(copy)
        arrivals.append(here)
    grid_copy = pltpu.make_async_copy(grid_in, grid, grid_sem)
    grid_copy.start()

    sub = lax.broadcasted_iota(jnp.int32, (8, 128), 0)
    lane = lax.broadcasted_iota(jnp.int32, (8, 128), 1)

    def array_of(a, layer):
        if a < 3:
            return e.at[a, layer]
        if a < 6:
            return h.at[a - 3, layer]
        return scale.at[layer]

    for index in range(7 * LZ):
        target = array_of(index // LZ, index % LZ)
        top = rim_rows(from_top, index, True)
        bottom = rim_rows(from_bottom, index, False)
        for tile in range(own_tiles):
            cols = slice(128 * tile, 128 * tile + 128)
            target[tile, 0:8, :] = top[:, cols]
            target[tile, ROWS + OFF : ROWS + OFF + 8, :] = bottom[:, cols]
        for tile in range(TILES):
            target[tile, USED_R : USED_R + 8, :] = jnp.zeros((8, 128), F32)

    def rim_strip(s, _):
        r = pl.multiple_of(s * 16, 16)
        both = from_left[pl.ds(r, 16), :] + from_right[pl.ds(r, 16), :]
        for index in range(7 * LZ):
            array_of(index // LZ, index % LZ)[own_tiles, pl.ds(r, 16), :] = rim_tile(both, index)
        return 0

    lax.fori_loop(0, USED_R // 16, rim_strip, 0, unroll=2)

    row_place, col_place = place_ref[0], place_ref[1]
    rim_half = jnp.full((8, 128), courant, F32)
    rim_half = jnp.where((lane >= 64) & (col_place == 0), 0.0, rim_half)
    rim_half = jnp.where((lane < 64) & (col_place == 7), 0.0, rim_half)
    inner_half = jnp.full((8, 128), courant, F32)
    half = [inner_half] * own_tiles + [rim_half]
    half_top = [jnp.where(row_place == 0, 0.0, value) for value in half]
    half_bottom = [jnp.where(row_place == 15, 0.0, value) for value in half]

    def load(ref, a, layer, r):
        return [ref[a, layer, tile, pl.ds(r, 8), :] for tile in range(TILES)]

    def y_next(here):
        moved = [pltpu.roll(value, 127, 1) for value in here]
        return [
            jnp.where(lane == 127, moved[(tile + 1) % TILES], moved[tile]) for tile in range(TILES)
        ]

    def y_last(here):
        moved = [pltpu.roll(value, 1, 1) for value in here]
        return [
            jnp.where(lane == 0, moved[(tile - 1) % TILES], moved[tile]) for tile in range(TILES)
        ]

    zero = [jnp.zeros((8, 128), F32)] * TILES

    every = frozenset((a, layer) for a in range(3) for layer in range(LZ))
    if with_fields:
        first_e = last_h = last_e = every
    else:
        last_e = frozenset(((0, 1), (1, 1)))
        last_h = frozenset(((0, 0), (1, 0), (0, 1), (1, 1), (2, 1)))
        first_e = every - {(2, 2)}

    def update_h(r, coef, wanted=every):
        for layer in range(LZ):
            if not any((a, layer) in wanted for a in range(3)):
                continue
            ex, ey, ez = (load(e, a, layer, r) for a in range(3))
            top = layer + 1 == LZ
            if (0, layer) in wanted:
                ey_up = zero if top else load(e, 1, layer + 1, r)
                ez_y = y_next(ez)
            if (1, layer) in wanted:
                ex_up = zero if top else load(e, 0, layer + 1, r)
                ez_x = load(e, 2, layer, r + 1)
            if (2, layer) in wanted:
                ey_x, ex_y = load(e, 1, layer, r + 1), y_next(ex)
            for t in range(TILES):
                rows = pl.ds(r, 8)
                if (0, layer) in wanted:
                    h[0, layer, t, rows, :] -= coef[t] * (ez_y[t] - ez[t] - (ey_up[t] - ey[t]))
                if (1, layer) in wanted:
                    h[1, layer, t, rows, :] -= coef[t] * (ex_up[t] - ex[t] - (ez_x[t] - ez[t]))
                if (2, layer) in wanted:
                    h[2, layer, t, rows, :] -= coef[t] * (ey_x[t] - ey[t] - (ex_y[t] - ex[t]))

    def update_e(r, moment, wanted, tiles):
        strength = math.sin(source_rate * moment)
        for layer in range(LZ):
            if not any((a, layer) in wanted for a in range(3)):
                continue
            hx, hy, hz = (load(h, a, layer, r) for a in range(3))
            edge = isinstance(r, int) and r == 0
            if (0, layer) in wanted:
                hy_low = load(h, 1, layer - 1, r) if layer else zero
                hz_y = y_last(hz)
            if (1, layer) in wanted:
                hx_low = load(h, 0, layer - 1, r) if layer else zero
                hz_x = [pltpu.roll(v, 1, 0) for v in hz] if edge else load(h, 2, layer, r - 1)
            if (2, layer) in wanted:
                hy_x = [pltpu.roll(v, 1, 0) for v in hy] if edge else load(h, 1, layer, r - 1)
                hx_y = y_last(hx)
            for t in range(tiles):
                rows = pl.ds(r, 8)
                rate = scale[layer, t, rows, :]
                if (0, layer) in wanted:
                    e[0, layer, t, rows, :] += rate * (hz[t] - hz_y[t] - (hy[t] - hy_low[t]))
                if (1, layer) in wanted:
                    e[1, layer, t, rows, :] += rate * (hx[t] - hx_low[t] - (hz[t] - hz_x[t]))
                if (2, layer) in wanted:
                    e[2, layer, t, rows, :] = (
                        e[2, layer, t, rows, :]
                        + rate * (hy[t] - hy_x[t] - (hx[t] - hx_y[t]))
                        + strength * grid[layer, t, rows, :]
                    )

    face_of = ((h, 1, -1.0), (h, 0, 1.0), (e, 1, 1.0), (e, 0, -1.0))

    def first_step(s, _):
        r = pl.multiple_of(s * 8, 8)
        update_h(r, half)
        update_e(r, 1.0, first_e, TILES)
        if with_face:
            for k, (ref, a, _sign) in enumerate(face_of):
                for tile in range(own_tiles):
                    first[k, tile, pl.ds(pl.multiple_of(r - OFF, 8), 8), :] = ref[
                        a, 1, tile, pl.ds(r, 8), :
                    ]
        return 0

    def second_step(s, _):
        own = pl.multiple_of(s * 16, 16)
        for part in range(2):
            r = pl.multiple_of(own + OFF + 8 * part, 8)
            update_h(r, half, last_h)
            update_e(r, 2.0, last_e, own_tiles)
        if with_face:
            now_rows = pl.ds(pl.multiple_of(own + OFF, 8), 16)
            for k, (ref, a, sign) in enumerate(face_of):
                for tile in range(own_tiles):
                    then = first[k, tile, pl.ds(own, 16), :]
                    now = ref[a, 1, tile, now_rows, :]
                    cols = pl.ds(128 * (tile % 2), 128)
                    target = 4 * k + tile // 2
                    face_out[target, pl.ds(own, 16), cols] = (sign * (then + now)).astype(BF16)
                    face_out[target + 2, pl.ds(own, 16), cols] = (sign * (then - now)).astype(BF16)
        return 0

    strips = span // 8
    for copy in arrivals[0]:
        copy.wait()
    grid_copy.wait()
    update_h(0, half_top)
    update_e(0, 1.0, first_e, TILES)
    for chunk in range(CHUNKS):
        begin = 1 + chunk * strips
        if chunk + 1 < CHUNKS:
            lax.fori_loop(begin, begin + strips - 1, first_step, 0, unroll=2)
            for copy in arrivals[chunk + 1]:
                copy.wait()
            first_step(jnp.int32(begin + strips - 1), 0)
        else:
            lax.fori_loop(begin, begin + strips, first_step, 0, unroll=2)
    update_h(ROWS + OFF, half_bottom)
    update_e(ROWS + OFF, 1.0, first_e, TILES)

    update_h(0, half_top, last_h)
    sent = []
    for chunk in range(CHUNKS):
        lax.fori_loop(chunk * (span // 16), (chunk + 1) * (span // 16), second_step, 0, unroll=2)
        if with_fields:
            source_rows = pl.ds(OFF + chunk * span, span)
            target_rows = pl.ds(chunk * span, span)
            for tile in range(own_tiles):
                cols = pl.ds(128 * tile, 128)
                for source, target in ((e, e_out), (h, h_out)):
                    copy = pltpu.make_async_copy(
                        source.at[:, :, tile, source_rows, :],
                        target.at[:, :, target_rows, cols],
                        out_sem.at[len(sent)],
                    )
                    copy.start()
                    sent.append(copy)
    for copy in sent:
        copy.wait()


def yee(with_fields, with_face, e, h, scale, grid, rims, place):
    field = jax.ShapeDtypeStruct((3, LZ, ROWS, COLS), F32)
    anywhere = pl.BlockSpec(memory_space=pl.ANY)
    out_shape = []
    out_specs = []
    scratch = [
        pltpu.VMEM((3, LZ, TILES, EXT_R, 128), F32),
        pltpu.VMEM((3, LZ, TILES, EXT_R, 128), F32),
        pltpu.VMEM((LZ, TILES, EXT_R, 128), F32),
        pltpu.VMEM((LZ, TILES, USED_R, 128), F32),
    ]
    if with_fields:
        out_shape += [field, field]
        out_specs += [anywhere, anywhere]
    if with_face:
        out_shape.append(jax.ShapeDtypeStruct((16, ROWS, 256), BF16))
        out_specs.append(vmem())
        scratch.append(pltpu.VMEM((4, COLS // 128, ROWS, 128), F32))
    scratch += [
        pltpu.SemaphoreType.DMA((CHUNKS, 3 * COLS // 128)),
        pltpu.SemaphoreType.DMA,
        pltpu.SemaphoreType.DMA((CHUNKS * 2 * COLS // 128,)),
    ]
    return pl.pallas_call(
        functools.partial(yee_kernel, with_fields, with_face),
        in_specs=[anywhere] * 4 + [vmem()] * 4 + [smem()],
        out_specs=out_specs,
        out_shape=out_shape,
        scratch_shapes=scratch,
        compiler_params=params(28),
        cost_estimate=pl.CostEstimate(
            flops=5_000_000_000, bytes_accessed=40_000_000, transcendentals=0
        ),
        name="yee_fields" if with_fields else "yee_face",
    )(*stay(e, h), scale, grid, *rims, place)


def rows_kernel(field_ref, table_ref, out_ref):
    total = jnp.dot(table_ref[...], field_ref[...], preferred_element_type=F32)
    out_ref[...] = total.astype(BF16)


def rows_transform(field, table):
    step = 320
    return pl.pallas_call(
        rows_kernel,
        grid=(1280 // step,),
        in_specs=[
            pl.BlockSpec((N, 256), lambda t: (0, 0)),
            pl.BlockSpec((step, N), lambda t: (t, 0)),
        ],
        out_specs=pl.BlockSpec((step, 256), lambda t: (t, 0)),
        out_shape=jax.ShapeDtypeStruct((1280, 256), BF16),
        compiler_params=params(16),
        name="rows_transform",
    )(field, *stay(table))


def columns_kernel(rows_ref, table_ref, out_ref, total, spread):
    step = pl.program_id(0)
    part = jnp.dot(rows_ref[0], table_ref[0], preferred_element_type=F32)
    for g in range(1, GROUP):
        part += jnp.dot(rows_ref[g], table_ref[g], preferred_element_type=F32)

    @pl.when(step == 0)
    def _():
        total[...] = part

    @pl.when(step > 0)
    def _():
        total[...] += part

    @pl.when(step == 16 // GROUP - 1)
    def _():
        sub = lax.broadcasted_iota(jnp.int32, (8, NA), 0)

        def flip(value):
            value = pltpu.roll(value, 4, 0)
            value = jnp.where(sub % 4 < 2, pltpu.roll(value, 6, 0), pltpu.roll(value, 2, 0))
            return jnp.where(sub % 2 == 0, pltpu.roll(value, 7, 0), pltpu.roll(value, 1, 0))

        for q in range(4):
            for plus in (True, False):
                base = 16 * (q if plus else 4 - q)
                cos_re, cos_im = total[base : base + 8, 0:NA], total[base : base + 8, NA : 2 * NA]
                sin_re = total[base + 8 : base + 16, 0:NA]
                sin_im = total[base + 8 : base + 16, NA : 2 * NA]
                if plus:
                    parts = (cos_re + sin_im, cos_im - sin_re)
                else:
                    parts = (flip(cos_re - sin_im), flip(cos_im + sin_re))
                for ri, value in enumerate(parts):
                    for j in range(8):
                        start = ((8 if plus else 0) * 8 + j) * 8 + 2 * q + ri
                        spread[pl.ds(start, 8, stride=64), :] = value[:, 128 * j : 128 * j + 128]
        out_ref[...] = spread[...].astype(BF16)


def columns(rows, table):
    return pl.pallas_call(
        columns_kernel,
        grid=(16 // GROUP,),
        in_specs=[
            pl.BlockSpec((GROUP, 80, 256), lambda t: (t, 0, 0)),
            pl.BlockSpec((GROUP, 256, 2 * NA), lambda t: (t, 0, 0)),
        ],
        out_specs=pl.BlockSpec((1024, 128), lambda t: (0, 0)),
        out_shape=jax.ShapeDtypeStruct((1024, 128), BF16),
        scratch_shapes=[pltpu.VMEM((80, 2 * NA), F32), pltpu.VMEM((1024, 128), F32)],
        compiler_params=params(24),
        name="columns",
    )(rows, *stay(table))


def combine_kernel(parts_ref, coef_ref, place_ref, out_ref):
    sub = lax.broadcasted_iota(jnp.int32, (8, 128), 0)
    real_row = (sub % 2) == 0
    side = jnp.where(real_row, -1.0, 1.0)

    def swap(value):
        return jnp.where(real_row, pltpu.roll(value, 7, 0), pltpu.roll(value, 1, 0)) * side

    def two_blocks(pair, _):
        for comp in range(4):
            totals = parts_ref[(2 * comp) * 8 + pair].astype(F32)
            changes = parts_ref[(2 * comp + 1) * 8 + pair].astype(F32)
            for odd in range(2):
                t = 2 * pair + odd
                where = jnp.where(place_ref[0] >= 8, t, 15 - t)
                total = totals[8 * odd : 8 * odd + 8]
                change = changes[8 * odd : 8 * odd + 8]
                total_swap, change_swap = swap(total), swap(change)
                for f in range(2):
                    value = (
                        coef_ref[f, 0] * total
                        + coef_ref[f, 1] * total_swap
                        + coef_ref[f, 3] * change
                        - coef_ref[f, 2] * change_swap
                    )
                    item = f * 4 + comp
                    for q in range(4):
                        out_ref[where, 16 * q + 2 * item : 16 * q + 2 * item + 2, :] = value[
                            2 * q : 2 * q + 2, :
                        ]
        return 0

    lax.fori_loop(0, 8, two_blocks, 0)


def combine(parts, coef, place):
    return pl.pallas_call(
        combine_kernel,
        in_specs=[vmem(), smem(), smem()],
        out_specs=vmem(),
        out_shape=jax.ShapeDtypeStruct((16, 64, 128), F32),
        compiler_params=params(8),
        name="combine",
    )(parts, coef, place)


def on_device(x_table, y_table, e, h, material, eps, src_pos, src_amp, freqs):
    row_place = lax.axis_index(GX)
    col_place = lax.axis_index("gy")
    place = jnp.stack([row_place, col_place]).astype(jnp.int32)
    up, down = pack_rows(e, h, material, eps)
    from_top = lax.ppermute(down, GX, [(k, k + 1) for k in range(15)])
    from_bottom = lax.ppermute(up, GX, [(k + 1, k) for k in range(15)])
    scale = scales(material, eps)
    left, right = pack_cols(e, h, scale, from_top, from_bottom)
    from_left = lax.ppermute(right, "gy", [(k, k + 1) for k in range(7)])
    from_right = lax.ppermute(left, "gy", [(k + 1, k) for k in range(7)])
    pos = src_pos.T.reshape(3, NSRC // 128, 128)
    amp = src_amp.reshape(NSRC // 128, 128)
    pos, amp, left = lax.optimization_barrier((pos, amp, left))
    grid = sources(pos, amp, place)
    rims = (from_left, from_right, from_top, from_bottom)
    (face,) = yee(False, True, e, h, scale, grid, rims, place)
    e_out, h_out = yee(True, False, e, h, scale, grid, rims, place)

    half = jnp.cos(freqs * 0.5), jnp.sin(freqs * 0.5)
    turn = jnp.cos(freqs * 1.5), jnp.sin(freqs * 1.5)
    coef = jnp.stack(
        [turn[0] * half[0], turn[1] * half[0], turn[0] * half[1], turn[1] * half[1]], 1
    ) * (1.0 / N)

    face = lax.all_to_all(face, GX, 0, 0, tiled=True)
    face, e_out, h_out = lax.optimization_barrier((face, e_out, h_out))
    rows = rows_transform(face.reshape(N, 256), x_table)
    rows = lax.all_to_all(rows.reshape(16, 80, 256), ("gc", "gy"), 0, 0, tiled=True)
    far = columns(rows, y_table)
    far = lax.all_to_all(far.reshape(128, 8, 128), GX + ("gy",), 0, 0, tiled=True)
    far = combine(far.reshape(64, 16, 128), coef, place)
    return e_out, h_out, far.reshape(64, 8, 2, 128)


def solution(mesh):
    fine = Mesh(mesh.devices.reshape(8, 2, 8), ("ga", "gc", "gy"))
    field = P(None, None, GX, "gy")
    placed = (P(), P(), field, field, P(None, GX, "gy"), P(), P(), P(), P())
    mapped = jax.shard_map(
        on_device,
        mesh=fine,
        in_specs=placed,
        out_specs=(field, field, P(GX, None, None, "gy")),
        check_vma=False,
    )
    x_table, y_table = tables()

    def program(e_field, h_field, material, eps_table, src_pos, src_amp, freqs):
        return mapped(
            x_table, y_table, e_field, h_field, material, eps_table, src_pos, src_amp, freqs
        )

    return program
```

```python
import functools
import math

import jax
import jax.numpy as jnp
import ml_dtypes
import numpy as np
from jax import lax
from jax.experimental import pallas as pl
from jax.experimental.pallas import tpu as pltpu
from jax.sharding import Mesh, PartitionSpec as P

LZ = 3
NA = 1024
NMAT = 8
N = 4096
NSRC = 4096
ROWS = 256
COLS = 512
OFF = 8
EXT_R = 280
EXT_C = 640
TILES = 5
USED_R = 272
CHUNKS = 2
courant = 0.5
source_rate = 0.7
PERIOD = 4 * N
GX = ("ga", "gc")
MIB = 1 << 20
F32 = jnp.float32
BF16 = jnp.bfloat16


def tables():
    cell = np.arange(N, dtype=np.int64)
    t = np.arange(16)[:, None, None]
    q = np.arange(5)[None, :, None]
    m = np.arange(8)[None, None, :]
    w = (64 * m + 4 * t + q)[..., None]
    phase = np.remainder(w * cell, PERIOD) * (2.0 * math.pi / PERIOD)
    x_table = np.stack([np.cos(phase), np.sin(phase)], 2).reshape(16 * 80, N)
    v = np.arange(NA, dtype=np.int64) + NA // 4
    phase = np.remainder(cell[:, None] * v[None, :], PERIOD) * (2.0 * math.pi / PERIOD)
    y_table = np.concatenate([np.cos(phase), -np.sin(phase)], 1)
    y_table = y_table.reshape(8, 2, 256, 2 * NA).transpose(1, 0, 2, 3).reshape(16, 256, 2 * NA)
    return x_table.astype(ml_dtypes.bfloat16), y_table.astype(ml_dtypes.bfloat16)


def params(mib):
    return pltpu.CompilerParams(vmem_limit_bytes=mib * MIB)


def stay(*arrays):
    return [pltpu.with_memory_space_constraint(array, pltpu.HBM) for array in arrays]


def vmem():
    return pl.BlockSpec(memory_space=pltpu.VMEM)


def smem():
    return pl.BlockSpec(memory_space=pltpu.SMEM)


def scale_of(material, eps_ref):
    shape = (8, material.shape[-1])
    scale = None
    for k in range(NMAT):
        rate = (courant / jnp.full(shape, eps_ref[k], F32))[0:1]
        scale = rate if scale is None else jnp.where(material == k, rate, scale)
    return scale


def scale_kernel(material_ref, eps_ref, scale_ref):
    def strip(s, _):
        r = pl.multiple_of(s * 16, 16)
        for layer in range(LZ):
            scale_ref[layer, pl.ds(r, 16), :] = scale_of(
                material_ref[layer, pl.ds(r, 16), :], eps_ref
            )
        return 0

    lax.fori_loop(0, ROWS // 16, strip, 0)


def scales(material, eps):
    return pl.pallas_call(
        scale_kernel,
        in_specs=[vmem(), smem()],
        out_specs=vmem(),
        out_shape=pltpu.HBM((LZ, ROWS, COLS), F32),
        compiler_params=params(8),
        cost_estimate=pl.CostEstimate(
            flops=1_500_000_000, bytes_accessed=3_000_000, transcendentals=0
        ),
        name="scales",
    )(material, eps)


def pack_rows_kernel(e_lo, e_hi, h_lo, h_hi, m_lo, m_hi, eps_ref, up_ref, down_ref):
    sub = lax.broadcasted_iota(jnp.int32, (8, COLS), 0)
    up = down = None
    for a in range(7):
        for layer in range(LZ):
            index = a * LZ + layer
            if a < 3:
                lo, hi = e_lo[a, layer], e_hi[a, layer]
            elif a < 6:
                lo, hi = h_lo[a - 3, layer], h_hi[a - 3, layer]
            else:
                lo, hi = scale_of(m_lo[layer], eps_ref), scale_of(m_hi[layer], eps_ref)
            p = 2 * (index % 4)
            if p == 0:
                up = jnp.zeros((8, COLS), F32)
                down = jnp.zeros((8, COLS), F32)
            here = (sub == p) | (sub == p + 1)
            up = jnp.where(here, pltpu.roll(lo, p, 0) if p else lo, up)
            down = jnp.where(here, pltpu.roll(hi, (p + 2) % 8, 0) if p != 6 else hi, down)
            tile = index // 4
            up_ref[8 * tile : 8 * tile + 8, :] = up
            down_ref[8 * tile : 8 * tile + 8, :] = down


def pack_rows(e, h, material, eps):
    last = ROWS // 8 - 1
    lo4 = pl.BlockSpec((3, LZ, 8, COLS), lambda r: (0, 0, 0, 0))
    hi4 = pl.BlockSpec((3, LZ, 8, COLS), lambda r: (0, 0, last, 0))
    lo3 = pl.BlockSpec((LZ, 8, COLS), lambda r: (0, 0, 0))
    hi3 = pl.BlockSpec((LZ, 8, COLS), lambda r: (0, last, 0))
    out = pl.BlockSpec((48, COLS), lambda r: (0, 0))
    return pl.pallas_call(
        pack_rows_kernel,
        grid=(1,),
        in_specs=[lo4, hi4, lo4, hi4, lo3, hi3, smem()],
        out_specs=[out, out],
        out_shape=[jax.ShapeDtypeStruct((48, COLS), F32)] * 2,
        compiler_params=params(8),
        name="pack_rows",
    )(*stay(e, e, h, h, material, material), eps)


def rim_rows(packed, index, to_top):
    p, tile = 2 * (index % 4), index // 4
    value = packed[8 * tile : 8 * tile + 8, :]
    sub = lax.broadcasted_iota(jnp.int32, value.shape, 0)
    shift = (6 - p) % 8 if to_top else (8 - p) % 8
    value = pltpu.roll(value, shift, 0) if shift else value
    return jnp.where(sub >= 6 if to_top else sub < 2, value, 0.0)


def pack_cols_kernel(
    e_lo, e_hi, h_lo, h_hi, s_lo, s_hi, top_lo, top_hi, bot_lo, bot_hi, left_ref, right_ref
):
    rows = 32

    def packed(pair_of, shape):
        lane = lax.broadcasted_iota(jnp.int32, shape, 1)
        both = jnp.zeros(shape, F32)
        for index in range(7 * LZ):
            lo, hi = pair_of(index)
            ends = pltpu.roll(jnp.where(lane < 64, lo, hi), 4 * index + 2, 1)
            both = jnp.where(lane // 4 == index, ends, both)
        return jnp.where(lane % 4 >= 2, both, 0.0), jnp.where(lane % 4 < 2, both, 0.0)

    def strip(s, _):
        r = pl.multiple_of(s * rows, rows)
        span = pl.ds(r, rows)

        def pair_of(index):
            a, layer = index // LZ, index % LZ
            if a < 3:
                return e_lo[a, layer, span, :], e_hi[a, layer, span, :]
            if a < 6:
                return h_lo[a - 3, layer, span, :], h_hi[a - 3, layer, span, :]
            return s_lo[layer, span, :], s_hi[layer, span, :]

        left, right = packed(pair_of, (rows, 128))
        target = pl.ds(pl.multiple_of(r + OFF, 8), rows)
        left_ref[target, :] = left
        right_ref[target, :] = right
        return 0

    lax.fori_loop(0, ROWS // rows, strip, 0)
    for to_top, lo, hi, r in ((True, top_lo, top_hi, 0), (False, bot_lo, bot_hi, ROWS + OFF)):
        left, right = packed(
            lambda index: (rim_rows(lo, index, to_top), rim_rows(hi, index, to_top)), (8, 128)
        )
        left_ref[r : r + 8, :] = left
        right_ref[r : r + 8, :] = right


def pack_cols(e, h, scale, from_top, from_bottom):
    end = COLS // 128 - 1
    lo4 = pl.BlockSpec((3, LZ, ROWS, 128), lambda r: (0, 0, 0, 0))
    hi4 = pl.BlockSpec((3, LZ, ROWS, 128), lambda r: (0, 0, 0, end))
    lo3 = pl.BlockSpec((LZ, ROWS, 128), lambda r: (0, 0, 0))
    hi3 = pl.BlockSpec((LZ, ROWS, 128), lambda r: (0, 0, end))
    lo2 = pl.BlockSpec((48, 128), lambda r: (0, 0))
    hi2 = pl.BlockSpec((48, 128), lambda r: (0, end))
    out = pl.BlockSpec((USED_R, 128), lambda r: (0, 0))
    return pl.pallas_call(
        pack_cols_kernel,
        grid=(1,),
        in_specs=[lo4, hi4, lo4, hi4, lo3, hi3, lo2, hi2, lo2, hi2],
        out_specs=[out, out],
        out_shape=[jax.ShapeDtypeStruct((USED_R, 128), F32)] * 2,
        compiler_params=params(16),
        name="pack_cols",
    )(*stay(e, e, h, h, scale, scale), from_top, from_top, from_bottom, from_bottom)


def rim_tile(both, index):
    lane = lax.broadcasted_iota(jnp.int32, both.shape, 1)
    moved = pltpu.roll(both, (126 - 4 * index) % 128, 1)
    return jnp.where((lane < 2) | (lane >= 126), moved, 0.0)


def sources_kernel(pos_ref, amp_ref, place_ref, grid_ref):
    groups = NSRC // 128
    row = pos_ref[1] - place_ref[0] * ROWS + OFF
    col = pos_ref[2] - place_ref[1] * COLS
    inside = (row >= OFF - 1) & (row <= ROWS + OFF) & (col >= -1) & (col <= COLS)
    col = jnp.where(col < 0, EXT_C - 1, col)
    taken = jnp.where(inside, 1.0, 0.0)
    lane_a = lax.broadcasted_iota(jnp.int32, (128, 128), 0)
    lane_b = lax.broadcasted_iota(jnp.int32, (128, 128), 1)
    before = jnp.where(lane_a < lane_b, 1.0, 0.0).astype(BF16)
    group_a = lax.broadcasted_iota(jnp.int32, (groups, groups), 0)
    group_b = lax.broadcasted_iota(jnp.int32, (groups, groups), 1)
    earlier = jnp.where(group_b < group_a, 1.0, 0.0).astype(BF16)
    in_group = jnp.dot(taken.astype(BF16), before, preferred_element_type=F32)
    ahead = jnp.dot(earlier, taken.astype(BF16), preferred_element_type=F32)
    rank = in_group + jnp.sum(ahead, axis=1, keepdims=True)
    rank = jnp.where(inside, rank, -1.0)
    features = (
        row.astype(F32),
        col.astype(F32),
        pos_ref[0].astype(F32),
        amp_ref[...],
    )
    count = jnp.sum(taken).astype(jnp.int32)
    slot = lax.broadcasted_iota(jnp.int32, (128, 128), 0).astype(F32)
    feature_lane = lax.broadcasted_iota(jnp.int32, (128, 128), 1)
    row_of = lax.broadcasted_iota(jnp.int32, (USED_R, 128), 0).astype(F32)
    col_of = lax.broadcasted_iota(jnp.int32, (EXT_C, 128), 0).astype(F32)
    grid_ref[...] = jnp.zeros(grid_ref.shape, F32)

    def one_pass(p, _):
        base = (p * 128).astype(F32)
        sums = [jnp.zeros((128, 128), F32) for _ in features]
        found = jnp.zeros((128, 128), F32)
        for g in range(groups):
            chosen = slot == rank[g : g + 1, :] - base
            found = jnp.where(chosen, 1.0, found)
            for f, feature in enumerate(features):
                sums[f] = jnp.where(chosen, feature[g : g + 1, :], sums[f])
        packed = jnp.zeros((128, 128), F32)
        for f, total in enumerate(sums + [found]):
            packed = jnp.where(feature_lane == f, jnp.sum(total, axis=1, keepdims=True), packed)
        packed = packed.T
        src_row, src_col, src_layer = packed[0:1], packed[1:2], packed[2:3]
        amp, valid = packed[3:4], packed[4:5]
        amp_1 = amp.astype(BF16).astype(F32)
        amp_2 = (amp - amp_1).astype(BF16).astype(F32)
        amp_3 = amp - amp_1 - amp_2
        at_col = jnp.where(col_of == src_col, 1.0, 0.0).astype(BF16)
        at_col = jnp.concatenate([at_col] * 3, 1)
        for layer in range(LZ):
            at_row = (row_of == src_row) & (src_layer == layer) & (valid > 0.0)
            weights = jnp.concatenate(
                [jnp.where(at_row, part, 0.0).astype(BF16) for part in (amp_1, amp_2, amp_3)], 1
            )
            added = lax.dot_general(
                weights, at_col, (((1,), (1,)), ((), ())), preferred_element_type=F32
            )
            for tile in range(TILES):
                grid_ref[layer, tile] += added[:, 128 * tile : 128 * tile + 128]
        return 0

    lax.fori_loop(0, (count + 127) // 128, one_pass, 0)


def sources(pos, amp, place):
    return pl.pallas_call(
        sources_kernel,
        in_specs=[vmem(), vmem(), smem()],
        out_specs=vmem(),
        out_shape=pltpu.HBM((LZ, TILES, USED_R, 128), F32),
        compiler_params=params(12),
        cost_estimate=pl.CostEstimate(
            flops=3_000_000_000, bytes_accessed=3_000_000, transcendentals=0
        ),
        name="sources",
    )(pos, amp, place)


def yee_kernel(
    with_fields,
    with_face,
    e_in,
    h_in,
    scale_in,
    grid_in,
    from_left,
    from_right,
    from_top,
    from_bottom,
    place_ref,
    *refs,
):
    refs = list(refs)
    e_out, h_out = (refs.pop(0), refs.pop(0)) if with_fields else (None, None)
    face_target = refs.pop(0) if with_face else None
    e, h, scale, grid = refs[:4]
    refs = refs[4:]
    first, face_out = (refs.pop(0), refs.pop(0)) if with_face else (None, None)
    in_sem, grid_sem, out_sem = refs
    span = ROWS // CHUNKS
    own_tiles = COLS // 128

    arrivals = []
    for chunk in range(CHUNKS):
        here = []
        source_rows = pl.ds(chunk * span, span)
        target_rows = pl.ds(OFF + chunk * span, span)
        for tile in range(own_tiles):
            cols = pl.ds(128 * tile, 128)
            pairs = (
                (e_in.at[:, :, source_rows, cols], e.at[:, :, tile, target_rows, :]),
                (h_in.at[:, :, source_rows, cols], h.at[:, :, tile, target_rows, :]),
                (scale_in.at[:, source_rows, cols], scale.at[:, tile, target_rows, :]),
            )
            for source, target in pairs:
                copy = pltpu.make_async_copy(source, target, in_sem.at[chunk, len(here)])
                copy.start()
                here.append(copy)
        arrivals.append(here)
    grid_copy = pltpu.make_async_copy(grid_in, grid, grid_sem)
    grid_copy.start()

    sub = lax.broadcasted_iota(jnp.int32, (8, 128), 0)
    lane = lax.broadcasted_iota(jnp.int32, (8, 128), 1)

    def array_of(a, layer):
        if a < 3:
            return e.at[a, layer]
        if a < 6:
            return h.at[a - 3, layer]
        return scale.at[layer]

    for index in range(7 * LZ):
        target = array_of(index // LZ, index % LZ)
        top = rim_rows(from_top, index, True)
        bottom = rim_rows(from_bottom, index, False)
        for tile in range(own_tiles):
            cols = slice(128 * tile, 128 * tile + 128)
            target[tile, 0:8, :] = top[:, cols]
            target[tile, ROWS + OFF : ROWS + OFF + 8, :] = bottom[:, cols]
        for tile in range(TILES):
            target[tile, USED_R : USED_R + 8, :] = jnp.zeros((8, 128), F32)

    def rim_strip(s, _):
        r = pl.multiple_of(s * 16, 16)
        both = from_left[pl.ds(r, 16), :] + from_right[pl.ds(r, 16), :]
        for index in range(7 * LZ):
            array_of(index // LZ, index % LZ)[own_tiles, pl.ds(r, 16), :] = rim_tile(both, index)
        return 0

    lax.fori_loop(0, USED_R // 16, rim_strip, 0, unroll=2)

    row_place, col_place = place_ref[0], place_ref[1]
    rim_half = jnp.full((8, 128), courant, F32)
    rim_half = jnp.where((lane >= 64) & (col_place == 0), 0.0, rim_half)
    rim_half = jnp.where((lane < 64) & (col_place == 7), 0.0, rim_half)
    inner_half = jnp.full((8, 128), courant, F32)
    half = [inner_half] * own_tiles + [rim_half]
    half_top = [jnp.where(row_place == 0, 0.0, value) for value in half]
    half_bottom = [jnp.where(row_place == 15, 0.0, value) for value in half]

    def load(ref, a, layer, r):
        return [ref[a, layer, tile, pl.ds(r, 8), :] for tile in range(TILES)]

    def y_next(here):
        moved = [pltpu.roll(value, 127, 1) for value in here]
        return [
            jnp.where(lane == 127, moved[(tile + 1) % TILES], moved[tile]) for tile in range(TILES)
        ]

    def y_last(here):
        moved = [pltpu.roll(value, 1, 1) for value in here]
        return [
            jnp.where(lane == 0, moved[(tile - 1) % TILES], moved[tile]) for tile in range(TILES)
        ]

    zero = [jnp.zeros((8, 128), F32)] * TILES

    every = frozenset((a, layer) for a in range(3) for layer in range(LZ))
    if with_fields:
        first_e = last_h = last_e = every
    else:
        last_e = frozenset(((0, 1), (1, 1)))
        last_h = frozenset(((0, 0), (1, 0), (0, 1), (1, 1), (2, 1)))
        first_e = every - {(2, 2)}

    def update_h(r, coef, wanted=every):
        for layer in range(LZ):
            if not any((a, layer) in wanted for a in range(3)):
                continue
            ex, ey, ez = (load(e, a, layer, r) for a in range(3))
            top = layer + 1 == LZ
            if (0, layer) in wanted:
                ey_up = zero if top else load(e, 1, layer + 1, r)
                ez_y = y_next(ez)
            if (1, layer) in wanted:
                ex_up = zero if top else load(e, 0, layer + 1, r)
                ez_x = load(e, 2, layer, r + 1)
            if (2, layer) in wanted:
                ey_x, ex_y = load(e, 1, layer, r + 1), y_next(ex)
            for t in range(TILES):
                rows = pl.ds(r, 8)
                if (0, layer) in wanted:
                    h[0, layer, t, rows, :] -= coef[t] * (ez_y[t] - ez[t] - (ey_up[t] - ey[t]))
                if (1, layer) in wanted:
                    h[1, layer, t, rows, :] -= coef[t] * (ex_up[t] - ex[t] - (ez_x[t] - ez[t]))
                if (2, layer) in wanted:
                    h[2, layer, t, rows, :] -= coef[t] * (ey_x[t] - ey[t] - (ex_y[t] - ex[t]))

    def update_e(r, moment, wanted, tiles):
        strength = math.sin(source_rate * moment)
        for layer in range(LZ):
            if not any((a, layer) in wanted for a in range(3)):
                continue
            hx, hy, hz = (load(h, a, layer, r) for a in range(3))
            edge = isinstance(r, int) and r == 0
            if (0, layer) in wanted:
                hy_low = load(h, 1, layer - 1, r) if layer else zero
                hz_y = y_last(hz)
            if (1, layer) in wanted:
                hx_low = load(h, 0, layer - 1, r) if layer else zero
                hz_x = [pltpu.roll(v, 1, 0) for v in hz] if edge else load(h, 2, layer, r - 1)
            if (2, layer) in wanted:
                hy_x = [pltpu.roll(v, 1, 0) for v in hy] if edge else load(h, 1, layer, r - 1)
                hx_y = y_last(hx)
            for t in range(tiles):
                rows = pl.ds(r, 8)
                rate = scale[layer, t, rows, :]
                if (0, layer) in wanted:
                    e[0, layer, t, rows, :] += rate * (hz[t] - hz_y[t] - (hy[t] - hy_low[t]))
                if (1, layer) in wanted:
                    e[1, layer, t, rows, :] += rate * (hx[t] - hx_low[t] - (hz[t] - hz_x[t]))
                if (2, layer) in wanted:
                    e[2, layer, t, rows, :] = (
                        e[2, layer, t, rows, :]
                        + rate * (hy[t] - hy_x[t] - (hx[t] - hx_y[t]))
                        + strength * grid[layer, t, rows, :]
                    )

    face_of = ((h, 1, -1.0), (h, 0, 1.0), (e, 1, 1.0), (e, 0, -1.0))

    def first_step(s, _):
        r = pl.multiple_of(s * 8, 8)
        update_h(r, half)
        update_e(r, 1.0, first_e, TILES)
        if with_face:
            for k, (ref, a, _sign) in enumerate(face_of):
                for tile in range(own_tiles):
                    first[k, tile, pl.ds(pl.multiple_of(r - OFF, 8), 8), :] = ref[
                        a, 1, tile, pl.ds(r, 8), :
                    ]
        return 0

    def second_step(s, _):
        own = pl.multiple_of(s * 16, 16)
        for part in range(2):
            r = pl.multiple_of(own + OFF + 8 * part, 8)
            update_h(r, half, last_h)
            update_e(r, 2.0, last_e, own_tiles)
        if with_face:
            now_rows = pl.ds(pl.multiple_of(own + OFF, 8), 16)
            for k, (ref, a, sign) in enumerate(face_of):
                for tile in range(own_tiles):
                    then = first[k, tile, pl.ds(own, 16), :]
                    now = ref[a, 1, tile, now_rows, :]
                    cols = pl.ds(128 * (tile % 2), 128)
                    target = 4 * k + tile // 2
                    face_out[target, pl.ds(own, 16), cols] = (sign * (then + now)).astype(BF16)
                    face_out[target + 2, pl.ds(own, 16), cols] = (sign * (then - now)).astype(BF16)
        return 0

    strips = span // 8
    for copy in arrivals[0]:
        copy.wait()
    grid_copy.wait()
    update_h(0, half_top)
    update_e(0, 1.0, first_e, TILES)
    for chunk in range(CHUNKS):
        begin = 1 + chunk * strips
        if chunk + 1 < CHUNKS:
            lax.fori_loop(begin, begin + strips - 1, first_step, 0, unroll=2)
            for copy in arrivals[chunk + 1]:
                copy.wait()
            first_step(jnp.int32(begin + strips - 1), 0)
        else:
            lax.fori_loop(begin, begin + strips, first_step, 0, unroll=2)
    update_h(ROWS + OFF, half_bottom)
    update_e(ROWS + OFF, 1.0, first_e, TILES)

    update_h(0, half_top, last_h)
    sent = []
    for chunk in range(CHUNKS):
        lax.fori_loop(chunk * (span // 16), (chunk + 1) * (span // 16), second_step, 0, unroll=2)
        if with_face:
            rows = pl.ds(chunk * span, span)
            copy = pltpu.make_async_copy(
                face_out.at[:, rows, :], face_target.at[:, rows, :], out_sem.at[len(sent)]
            )
            copy.start()
            sent.append(copy)
        if with_fields:
            source_rows = pl.ds(OFF + chunk * span, span)
            target_rows = pl.ds(chunk * span, span)
            for tile in range(own_tiles):
                cols = pl.ds(128 * tile, 128)
                for source, target in ((e, e_out), (h, h_out)):
                    copy = pltpu.make_async_copy(
                        source.at[:, :, tile, source_rows, :],
                        target.at[:, :, target_rows, cols],
                        out_sem.at[len(sent)],
                    )
                    copy.start()
                    sent.append(copy)
    for copy in sent:
        copy.wait()


def yee(with_fields, with_face, e, h, scale, grid, rims, place):
    field = jax.ShapeDtypeStruct((3, LZ, ROWS, COLS), F32)
    anywhere = pl.BlockSpec(memory_space=pl.ANY)
    out_shape = []
    out_specs = []
    scratch = [
        pltpu.VMEM((3, LZ, TILES, EXT_R, 128), F32),
        pltpu.VMEM((3, LZ, TILES, EXT_R, 128), F32),
        pltpu.VMEM((LZ, TILES, EXT_R, 128), F32),
        pltpu.VMEM((LZ, TILES, USED_R, 128), F32),
    ]
    if with_fields:
        out_shape += [field, field]
        out_specs += [anywhere, anywhere]
    if with_face:
        out_shape.append(pltpu.HBM((16, ROWS, 256), BF16))
        out_specs.append(anywhere)
        scratch.append(pltpu.VMEM((4, COLS // 128, ROWS, 128), F32))
        scratch.append(pltpu.VMEM((16, ROWS, 256), BF16))
    scratch += [
        pltpu.SemaphoreType.DMA((CHUNKS, 3 * COLS // 128)),
        pltpu.SemaphoreType.DMA,
        pltpu.SemaphoreType.DMA((CHUNKS * (2 * COLS // 128 + 1),)),
    ]
    return pl.pallas_call(
        functools.partial(yee_kernel, with_fields, with_face),
        in_specs=[anywhere] * 4 + [vmem()] * 4 + [smem()],
        out_specs=out_specs,
        out_shape=out_shape,
        scratch_shapes=scratch,
        compiler_params=params(28),
        cost_estimate=pl.CostEstimate(
            flops=5_000_000_000, bytes_accessed=40_000_000, transcendentals=0
        ),
        name="yee_fields" if with_fields else "yee_face",
    )(*stay(e, h, scale, grid), *rims, place)


def fetch_kernel(x_in, y_in, x_out, y_out, sem):
    copies = [
        pltpu.make_async_copy(x_in, x_out, sem.at[0]),
        pltpu.make_async_copy(y_in, y_out, sem.at[1]),
    ]
    for copy in copies:
        copy.start()
    for copy in copies:
        copy.wait()


def fetch(x_table, y_table):
    anywhere = pl.BlockSpec(memory_space=pl.ANY)
    return pl.pallas_call(
        fetch_kernel,
        in_specs=[anywhere, anywhere],
        out_specs=[vmem(), vmem()],
        out_shape=[
            pltpu.VMEM(x_table.shape, x_table.dtype),
            pltpu.VMEM(y_table.shape, y_table.dtype),
        ],
        scratch_shapes=[pltpu.SemaphoreType.DMA((2,))],
        compiler_params=params(4),
        cost_estimate=pl.CostEstimate(
            flops=1_000_000, bytes_accessed=54_000_000, transcendentals=0
        ),
        name="fetch",
    )(*stay(x_table, y_table))


def held(array):
    return pltpu.with_memory_space_constraint(array, pltpu.VMEM)


def rows_kernel(field_ref, table_ref, out_ref):
    def part(s, _):
        span = pl.ds(pl.multiple_of(s * 320, 320), 320)
        total = jnp.dot(table_ref[span, :], field_ref[...], preferred_element_type=F32)
        out_ref[span, :] = total.astype(BF16)
        return 0

    lax.fori_loop(0, 4, part, 0)


def rows_transform(field, table):
    return pl.pallas_call(
        rows_kernel,
        in_specs=[vmem(), vmem()],
        out_specs=vmem(),
        out_shape=jax.ShapeDtypeStruct((1280, 256), BF16),
        compiler_params=params(8),
        name="rows_transform",
    )(field, held(table))


def columns_kernel(rows_ref, table_ref, out_ref, total, spread):
    def width(s, _):
        cols = pl.ds(pl.multiple_of(s * 512, 512), 512)
        part = jnp.dot(rows_ref[0], table_ref[0, :, cols], preferred_element_type=F32)
        for g in range(1, 16):
            part += jnp.dot(rows_ref[g], table_ref[g, :, cols], preferred_element_type=F32)
        total[:, cols] = part
        return 0

    lax.fori_loop(0, 4, width, 0)
    sub = lax.broadcasted_iota(jnp.int32, (8, NA), 0)

    def flip(value):
        value = pltpu.roll(value, 4, 0)
        value = jnp.where(sub % 4 < 2, pltpu.roll(value, 6, 0), pltpu.roll(value, 2, 0))
        return jnp.where(sub % 2 == 0, pltpu.roll(value, 7, 0), pltpu.roll(value, 1, 0))

    for q in range(4):
        for plus in (True, False):
            base = 16 * (q if plus else 4 - q)
            cos_re, cos_im = total[base : base + 8, 0:NA], total[base : base + 8, NA : 2 * NA]
            sin_re = total[base + 8 : base + 16, 0:NA]
            sin_im = total[base + 8 : base + 16, NA : 2 * NA]
            if plus:
                parts = (cos_re + sin_im, cos_im - sin_re)
            else:
                parts = (flip(cos_re - sin_im), flip(cos_im + sin_re))
            for ri, value in enumerate(parts):
                for j in range(8):
                    start = ((8 if plus else 0) * 8 + j) * 8 + 2 * q + ri
                    spread[pl.ds(start, 8, stride=64), :] = value[:, 128 * j : 128 * j + 128]
    out_ref[...] = spread[...].astype(BF16)


def columns(rows, table):
    return pl.pallas_call(
        columns_kernel,
        in_specs=[vmem(), vmem()],
        out_specs=vmem(),
        out_shape=pltpu.HBM((1024, 128), BF16),
        scratch_shapes=[pltpu.VMEM((80, 2 * NA), F32), pltpu.VMEM((1024, 128), F32)],
        compiler_params=params(8),
        name="columns",
    )(rows, held(table))


def combine_kernel(parts_ref, coef_ref, place_ref, out_ref):
    sub = lax.broadcasted_iota(jnp.int32, (8, 128), 0)
    real_row = (sub % 2) == 0
    side = jnp.where(real_row, -1.0, 1.0)

    def swap(value):
        return jnp.where(real_row, pltpu.roll(value, 7, 0), pltpu.roll(value, 1, 0)) * side

    def two_blocks(pair, _):
        for comp in range(4):
            totals = parts_ref[(2 * comp) * 8 + pair].astype(F32)
            changes = parts_ref[(2 * comp + 1) * 8 + pair].astype(F32)
            for odd in range(2):
                t = 2 * pair + odd
                where = jnp.where(place_ref[0] >= 8, t, 15 - t)
                total = totals[8 * odd : 8 * odd + 8]
                change = changes[8 * odd : 8 * odd + 8]
                total_swap, change_swap = swap(total), swap(change)
                for f in range(2):
                    value = (
                        coef_ref[f, 0] * total
                        + coef_ref[f, 1] * total_swap
                        + coef_ref[f, 3] * change
                        - coef_ref[f, 2] * change_swap
                    )
                    item = f * 4 + comp
                    for q in range(4):
                        out_ref[where, 16 * q + 2 * item : 16 * q + 2 * item + 2, :] = value[
                            2 * q : 2 * q + 2, :
                        ]
        return 0

    lax.fori_loop(0, 8, two_blocks, 0)


def combine(parts, coef, place):
    return pl.pallas_call(
        combine_kernel,
        in_specs=[vmem(), smem(), smem()],
        out_specs=vmem(),
        out_shape=jax.ShapeDtypeStruct((16, 64, 128), F32),
        compiler_params=params(8),
        name="combine",
    )(parts, coef, place)


def on_device(x_table, y_table, e, h, material, eps, src_pos, src_amp, freqs):
    row_place = lax.axis_index(GX)
    col_place = lax.axis_index("gy")
    place = jnp.stack([row_place, col_place]).astype(jnp.int32)
    up, down = pack_rows(e, h, material, eps)
    from_top = lax.ppermute(down, GX, [(k, k + 1) for k in range(15)])
    from_bottom = lax.ppermute(up, GX, [(k + 1, k) for k in range(15)])
    scale = scales(material, eps)
    left, right = pack_cols(e, h, scale, from_top, from_bottom)
    from_left = lax.ppermute(right, "gy", [(k, k + 1) for k in range(7)])
    from_right = lax.ppermute(left, "gy", [(k + 1, k) for k in range(7)])
    pos = src_pos.T.reshape(3, NSRC // 128, 128)
    amp = src_amp.reshape(NSRC // 128, 128)
    pos, amp, left = lax.optimization_barrier((pos, amp, left))
    grid = sources(pos, amp, place)
    rims = (from_left, from_right, from_top, from_bottom)
    (face,) = yee(False, True, e, h, scale, grid, rims, place)
    e_out, h_out = yee(True, False, e, h, scale, grid, rims, place)

    half = jnp.cos(freqs * 0.5), jnp.sin(freqs * 0.5)
    turn = jnp.cos(freqs * 1.5), jnp.sin(freqs * 1.5)
    coef = jnp.stack(
        [turn[0] * half[0], turn[1] * half[0], turn[0] * half[1], turn[1] * half[1]], 1
    ) * (1.0 / N)

    face = lax.all_to_all(face, GX, 0, 0, tiled=True)
    x_table, y_table, e_out = lax.optimization_barrier((x_table, y_table, e_out))
    x_table, y_table = fetch(x_table, y_table)
    face, e_out, h_out, x_table, y_table = lax.optimization_barrier(
        (face, e_out, h_out, x_table, y_table)
    )
    rows = rows_transform(face.reshape(N, 256), x_table)
    rows = lax.all_to_all(rows.reshape(16, 80, 256), ("gc", "gy"), 0, 0, tiled=True)
    far = columns(rows, y_table)
    far = lax.all_to_all(far.reshape(128, 8, 128), GX + ("gy",), 0, 0, tiled=True)
    far = combine(far.reshape(64, 16, 128), coef, place)
    return e_out, h_out, far.reshape(64, 8, 2, 128)


def solution(mesh):
    fine = Mesh(mesh.devices.reshape(8, 2, 8), ("ga", "gc", "gy"))
    field = P(None, None, GX, "gy")
    placed = (P(), P(), field, field, P(None, GX, "gy"), P(), P(), P(), P())
    mapped = jax.shard_map(
        on_device,
        mesh=fine,
        in_specs=placed,
        out_specs=(field, field, P(GX, None, None, "gy")),
        check_vma=False,
    )
    x_table, y_table = tables()

    def program(e_field, h_field, material, eps_table, src_pos, src_amp, freqs):
        return mapped(
            x_table, y_table, e_field, h_field, material, eps_table, src_pos, src_amp, freqs
        )

    return program
```

```python
import functools
import math

import jax
import jax.numpy as jnp
import ml_dtypes
import numpy as np
from jax import lax
from jax.experimental import pallas as pl
from jax.experimental.pallas import tpu as pltpu
from jax.sharding import Mesh, PartitionSpec as P

LZ = 3
NA = 1024
NMAT = 8
N = 4096
NSRC = 4096
ROWS = 256
COLS = 512
OFF = 8
EXT_R = 280
EXT_C = 640
TILES = 5
USED_R = 272
FOLD = 136
ROW_STEP = 320
COL_STEP = 256
CHUNKS = 2
courant = 0.5
source_rate = 0.7
PERIOD = 4 * N
GX = ("ga", "gc")
MIB = 1 << 20
F32 = jnp.float32
BF16 = jnp.bfloat16


def tables():
    cell = np.arange(N, dtype=np.int64)
    t = np.arange(16)[:, None, None]
    q = np.arange(5)[None, :, None]
    m = np.arange(8)[None, None, :]
    w = (64 * m + 4 * t + q)[..., None]
    phase = np.remainder(w * cell, PERIOD) * (2.0 * math.pi / PERIOD)
    x_table = np.stack([np.cos(phase), np.sin(phase)], 2).reshape(16 * 80, N)
    v = np.arange(NA, dtype=np.int64) + NA // 4
    phase = np.remainder(cell[:, None] * v[None, :], PERIOD) * (2.0 * math.pi / PERIOD)
    y_table = np.concatenate([np.cos(phase), -np.sin(phase)], 1)
    y_table = y_table.reshape(8, 2, 256, 2 * NA).transpose(1, 0, 2, 3).reshape(16, 256, 2 * NA)
    return x_table.astype(ml_dtypes.bfloat16), y_table.astype(ml_dtypes.bfloat16)


def params(mib):
    return pltpu.CompilerParams(vmem_limit_bytes=mib * MIB)


def stay(*arrays):
    return [pltpu.with_memory_space_constraint(array, pltpu.HBM) for array in arrays]


def vmem():
    return pl.BlockSpec(memory_space=pltpu.VMEM)


def smem():
    return pl.BlockSpec(memory_space=pltpu.SMEM)


def scale_of(material, eps_ref):
    shape = (8, material.shape[-1])
    scale = None
    for k in range(NMAT):
        rate = (courant / jnp.full(shape, eps_ref[k], F32))[0:1]
        scale = rate if scale is None else jnp.where(material == k, rate, scale)
    return scale


def scale_kernel(material_ref, eps_ref, scale_ref):
    def strip(s, _):
        r = pl.multiple_of(s * 16, 16)
        for layer in range(LZ):
            scale_ref[layer, pl.ds(r, 16), :] = scale_of(
                material_ref[layer, pl.ds(r, 16), :], eps_ref
            )
        return 0

    lax.fori_loop(0, ROWS // 16, strip, 0)


def scales(material, eps):
    return pl.pallas_call(
        scale_kernel,
        in_specs=[vmem(), smem()],
        out_specs=vmem(),
        out_shape=jax.ShapeDtypeStruct((LZ, ROWS, COLS), F32),
        compiler_params=params(8),
        cost_estimate=pl.CostEstimate(
            flops=1_500_000_000, bytes_accessed=3_000_000, transcendentals=0
        ),
        name="scales",
    )(material, eps)


def pack_rows_kernel(e_lo, e_hi, h_lo, h_hi, m_lo, m_hi, eps_ref, up_ref, down_ref):
    sub = lax.broadcasted_iota(jnp.int32, (8, COLS), 0)
    up = down = None
    for a in range(7):
        for layer in range(LZ):
            index = a * LZ + layer
            if a < 3:
                lo, hi = e_lo[a, layer], e_hi[a, layer]
            elif a < 6:
                lo, hi = h_lo[a - 3, layer], h_hi[a - 3, layer]
            else:
                lo, hi = scale_of(m_lo[layer], eps_ref), scale_of(m_hi[layer], eps_ref)
            p = 2 * (index % 4)
            if p == 0:
                up = jnp.zeros((8, COLS), F32)
                down = jnp.zeros((8, COLS), F32)
            here = (sub == p) | (sub == p + 1)
            up = jnp.where(here, pltpu.roll(lo, p, 0) if p else lo, up)
            down = jnp.where(here, pltpu.roll(hi, (p + 2) % 8, 0) if p != 6 else hi, down)
            tile = index // 4
            up_ref[8 * tile : 8 * tile + 8, :] = up
            down_ref[8 * tile : 8 * tile + 8, :] = down


def pack_rows(e, h, material, eps):
    last = ROWS // 8 - 1
    lo4 = pl.BlockSpec((3, LZ, 8, COLS), lambda r: (0, 0, 0, 0))
    hi4 = pl.BlockSpec((3, LZ, 8, COLS), lambda r: (0, 0, last, 0))
    lo3 = pl.BlockSpec((LZ, 8, COLS), lambda r: (0, 0, 0))
    hi3 = pl.BlockSpec((LZ, 8, COLS), lambda r: (0, last, 0))
    out = pl.BlockSpec((48, COLS), lambda r: (0, 0))
    return pl.pallas_call(
        pack_rows_kernel,
        grid=(1,),
        in_specs=[lo4, hi4, lo4, hi4, lo3, hi3, smem()],
        out_specs=[out, out],
        out_shape=[jax.ShapeDtypeStruct((48, COLS), F32)] * 2,
        compiler_params=params(8),
        name="pack_rows",
    )(*stay(e, e, h, h, material, material), eps)


def rim_rows(packed, index, to_top):
    p, tile = 2 * (index % 4), index // 4
    value = packed[8 * tile : 8 * tile + 8, :]
    sub = lax.broadcasted_iota(jnp.int32, value.shape, 0)
    shift = (6 - p) % 8 if to_top else (8 - p) % 8
    value = pltpu.roll(value, shift, 0) if shift else value
    return jnp.where(sub >= 6 if to_top else sub < 2, value, 0.0)


def pack_cols_kernel(
    e_lo, e_hi, h_lo, h_hi, s_lo, s_hi, top_lo, top_hi, bot_lo, bot_hi, left_ref, right_ref,
    all_rows,
):
    rows = 32

    def packed(pair_of, shape):
        lane = lax.broadcasted_iota(jnp.int32, shape, 1)
        both = jnp.zeros(shape, F32)
        for index in range(7 * LZ):
            lo, hi = pair_of(index)
            ends = pltpu.roll(jnp.where(lane < 64, lo, hi), 4 * index + 2, 1)
            both = jnp.where(lane // 4 == index, ends, both)
        return both

    def strip(s, _):
        r = pl.multiple_of(s * rows, rows)
        span = pl.ds(r, rows)

        def pair_of(index):
            a, layer = index // LZ, index % LZ
            if a < 3:
                return e_lo[a, layer, span, :], e_hi[a, layer, span, :]
            if a < 6:
                return h_lo[a - 3, layer, span, :], h_hi[a - 3, layer, span, :]
            return s_lo[layer, span, :], s_hi[layer, span, :]

        all_rows[pl.ds(pl.multiple_of(r + OFF, 8), rows), :] = packed(pair_of, (rows, 128))
        return 0

    lax.fori_loop(0, ROWS // rows, strip, 0)
    for to_top, lo, hi, r in ((True, top_lo, top_hi, 0), (False, bot_lo, bot_hi, ROWS + OFF)):
        all_rows[r : r + 8, :] = packed(
            lambda index: (rim_rows(lo, index, to_top), rim_rows(hi, index, to_top)), (8, 128)
        )
    high = lax.broadcasted_iota(jnp.int32, (FOLD, 128), 1) % 4 >= 2
    near, far = all_rows[0:FOLD, :], all_rows[FOLD:USED_R, :]
    left_ref[...] = jnp.where(high, near, pltpu.roll(far, 126, 1))
    right_ref[...] = jnp.where(high, pltpu.roll(far, 2, 1), near)


def pack_cols(e, h, scale, from_top, from_bottom):
    end = COLS // 128 - 1
    lo4 = pl.BlockSpec((3, LZ, ROWS, 128), lambda r: (0, 0, 0, 0))
    hi4 = pl.BlockSpec((3, LZ, ROWS, 128), lambda r: (0, 0, 0, end))
    lo3 = pl.BlockSpec((LZ, ROWS, 128), lambda r: (0, 0, 0))
    hi3 = pl.BlockSpec((LZ, ROWS, 128), lambda r: (0, 0, end))
    lo2 = pl.BlockSpec((48, 128), lambda r: (0, 0))
    hi2 = pl.BlockSpec((48, 128), lambda r: (0, end))
    out = pl.BlockSpec((FOLD, 128), lambda r: (0, 0))
    return pl.pallas_call(
        pack_cols_kernel,
        grid=(1,),
        in_specs=[lo4, hi4, lo4, hi4, lo3, hi3, lo2, hi2, lo2, hi2],
        out_specs=[out, out],
        out_shape=[jax.ShapeDtypeStruct((FOLD, 128), F32)] * 2,
        scratch_shapes=[pltpu.VMEM((USED_R, 128), F32)],
        compiler_params=params(16),
        name="pack_cols",
    )(*stay(e, e, h, h), scale, scale, from_top, from_top, from_bottom, from_bottom)


def rim_tile(both, index):
    lane = lax.broadcasted_iota(jnp.int32, both.shape, 1)
    moved = pltpu.roll(both, (126 - 4 * index) % 128, 1)
    return jnp.where((lane < 2) | (lane >= 126), moved, 0.0)


def sources_kernel(pos_ref, amp_ref, place_ref, grid_ref, kept_ref, sem):
    groups = NSRC // 128
    row = pos_ref[1] - place_ref[0] * ROWS + OFF
    col = pos_ref[2] - place_ref[1] * COLS
    inside = (row >= OFF - 1) & (row <= ROWS + OFF) & (col >= -1) & (col <= COLS)
    col = jnp.where(col < 0, EXT_C - 1, col)
    taken = jnp.where(inside, 1.0, 0.0)
    lane_a = lax.broadcasted_iota(jnp.int32, (128, 128), 0)
    lane_b = lax.broadcasted_iota(jnp.int32, (128, 128), 1)
    before = jnp.where(lane_a < lane_b, 1.0, 0.0).astype(BF16)
    group_a = lax.broadcasted_iota(jnp.int32, (groups, groups), 0)
    group_b = lax.broadcasted_iota(jnp.int32, (groups, groups), 1)
    earlier = jnp.where(group_b < group_a, 1.0, 0.0).astype(BF16)
    in_group = jnp.dot(taken.astype(BF16), before, preferred_element_type=F32)
    ahead = jnp.dot(earlier, taken.astype(BF16), preferred_element_type=F32)
    rank = in_group + jnp.sum(ahead, axis=1, keepdims=True)
    rank = jnp.where(inside, rank, -1.0)
    features = (
        row.astype(F32),
        col.astype(F32),
        pos_ref[0].astype(F32),
        amp_ref[...],
    )
    count = jnp.sum(taken).astype(jnp.int32)
    slot = lax.broadcasted_iota(jnp.int32, (128, 128), 0).astype(F32)
    feature_lane = lax.broadcasted_iota(jnp.int32, (128, 128), 1)
    row_of = lax.broadcasted_iota(jnp.int32, (USED_R, 128), 0).astype(F32)
    col_of = lax.broadcasted_iota(jnp.int32, (EXT_C, 128), 0).astype(F32)
    grid_ref[...] = jnp.zeros(grid_ref.shape, F32)

    def one_pass(p, _):
        base = (p * 128).astype(F32)
        sums = [jnp.zeros((128, 128), F32) for _ in features]
        found = jnp.zeros((128, 128), F32)
        for g in range(groups):
            chosen = slot == rank[g : g + 1, :] - base
            found = jnp.where(chosen, 1.0, found)
            for f, feature in enumerate(features):
                sums[f] = jnp.where(chosen, feature[g : g + 1, :], sums[f])
        packed = jnp.zeros((128, 128), F32)
        for f, total in enumerate(sums + [found]):
            packed = jnp.where(feature_lane == f, jnp.sum(total, axis=1, keepdims=True), packed)
        packed = packed.T
        src_row, src_col, src_layer = packed[0:1], packed[1:2], packed[2:3]
        amp, valid = packed[3:4], packed[4:5]
        amp_1 = amp.astype(BF16).astype(F32)
        amp_2 = (amp - amp_1).astype(BF16).astype(F32)
        amp_3 = amp - amp_1 - amp_2
        at_col = jnp.where(col_of == src_col, 1.0, 0.0).astype(BF16)
        at_col = jnp.concatenate([at_col] * 3, 1)
        for layer in range(LZ):
            at_row = (row_of == src_row) & (src_layer == layer) & (valid > 0.0)
            weights = jnp.concatenate(
                [jnp.where(at_row, part, 0.0).astype(BF16) for part in (amp_1, amp_2, amp_3)], 1
            )
            added = lax.dot_general(
                weights, at_col, (((1,), (1,)), ((), ())), preferred_element_type=F32
            )
            for tile in range(TILES):
                grid_ref[layer, tile] += added[:, 128 * tile : 128 * tile + 128]
        return 0

    lax.fori_loop(0, (count + 127) // 128, one_pass, 0)
    copy = pltpu.make_async_copy(grid_ref, kept_ref, sem)
    copy.start()
    copy.wait()


def sources(pos, amp, place):
    return pl.pallas_call(
        sources_kernel,
        in_specs=[vmem(), vmem(), smem()],
        out_specs=[vmem(), pl.BlockSpec(memory_space=pl.ANY)],
        out_shape=[
            jax.ShapeDtypeStruct((LZ, TILES, USED_R, 128), F32),
            pltpu.HBM((LZ, TILES, USED_R, 128), F32),
        ],
        scratch_shapes=[pltpu.SemaphoreType.DMA],
        compiler_params=params(12),
        cost_estimate=pl.CostEstimate(
            flops=3_000_000_000, bytes_accessed=3_000_000, transcendentals=0
        ),
        name="sources",
    )(pos, amp, place)


def yee_kernel(
    with_fields,
    with_face,
    e_in,
    h_in,
    scale_in,
    grid_in,
    from_left,
    from_right,
    from_top,
    from_bottom,
    place_ref,
    *refs,
):
    refs = list(refs)
    e_out, h_out = (refs.pop(0), refs.pop(0)) if with_fields else (None, None)
    face_target = refs.pop(0) if with_face else None
    e, h, scale, grid = refs[:4]
    refs = refs[4:]
    first, face_out = (refs.pop(0), refs.pop(0)) if with_face else (None, None)
    in_sem, grid_sem, out_sem = refs
    span = ROWS // CHUNKS
    own_tiles = COLS // 128

    grid_copy = pltpu.make_async_copy(grid_in, grid, grid_sem)
    grid_copy.start()
    arrivals = []
    for chunk in range(CHUNKS):
        here = []
        source_rows = pl.ds(chunk * span, span)
        target_rows = pl.ds(OFF + chunk * span, span)
        for tile in range(own_tiles):
            cols = pl.ds(128 * tile, 128)
            pairs = (
                (e_in.at[:, :, source_rows, cols], e.at[:, :, tile, target_rows, :]),
                (h_in.at[:, :, source_rows, cols], h.at[:, :, tile, target_rows, :]),
                (scale_in.at[:, source_rows, cols], scale.at[:, tile, target_rows, :]),
            )
            for source, target in pairs:
                copy = pltpu.make_async_copy(source, target, in_sem.at[chunk, len(here)])
                copy.start()
                here.append(copy)
        arrivals.append(here)
    sub = lax.broadcasted_iota(jnp.int32, (8, 128), 0)
    lane = lax.broadcasted_iota(jnp.int32, (8, 128), 1)

    def array_of(a, layer):
        if a < 3:
            return e.at[a, layer]
        if a < 6:
            return h.at[a - 3, layer]
        return scale.at[layer]

    for index in range(7 * LZ):
        target = array_of(index // LZ, index % LZ)
        top = rim_rows(from_top, index, True)
        bottom = rim_rows(from_bottom, index, False)
        for tile in range(own_tiles):
            cols = slice(128 * tile, 128 * tile + 128)
            target[tile, 0:8, :] = top[:, cols]
            target[tile, ROWS + OFF : ROWS + OFF + 8, :] = bottom[:, cols]
        for tile in range(TILES):
            target[tile, USED_R : USED_R + 8, :] = jnp.zeros((8, 128), F32)

    def rim_strip(s, _):
        r = pl.multiple_of(s * 8, 8)
        left, right = from_left[pl.ds(r, 8), :], from_right[pl.ds(r, 8), :]
        high = lane % 4 >= 2
        near = jnp.where(high, right, left)
        far = jnp.where(high, pltpu.roll(right, 2, 1), pltpu.roll(left, 126, 1))
        for index in range(7 * LZ):
            target = array_of(index // LZ, index % LZ)
            target[own_tiles, pl.ds(r, 8), :] = rim_tile(near, index)
            target[own_tiles, pl.ds(pl.multiple_of(r + FOLD, 8), 8), :] = rim_tile(far, index)
        return 0

    lax.fori_loop(0, FOLD // 8, rim_strip, 0, unroll=2)

    row_place, col_place = place_ref[0], place_ref[1]
    rim_half = jnp.full((8, 128), courant, F32)
    rim_half = jnp.where((lane >= 64) & (col_place == 0), 0.0, rim_half)
    rim_half = jnp.where((lane < 64) & (col_place == 7), 0.0, rim_half)
    inner_half = jnp.full((8, 128), courant, F32)
    half = [inner_half] * own_tiles + [rim_half]
    half_top = [jnp.where(row_place == 0, 0.0, value) for value in half]
    half_bottom = [jnp.where(row_place == 15, 0.0, value) for value in half]

    def load(ref, a, layer, r):
        return [ref[a, layer, tile, pl.ds(r, 8), :] for tile in range(TILES)]

    def y_next(here):
        moved = [pltpu.roll(value, 127, 1) for value in here]
        return [
            jnp.where(lane == 127, moved[(tile + 1) % TILES], moved[tile]) for tile in range(TILES)
        ]

    def y_last(here):
        moved = [pltpu.roll(value, 1, 1) for value in here]
        return [
            jnp.where(lane == 0, moved[(tile - 1) % TILES], moved[tile]) for tile in range(TILES)
        ]

    zero = [jnp.zeros((8, 128), F32)] * TILES

    every = frozenset((a, layer) for a in range(3) for layer in range(LZ))
    if with_fields:
        first_e = last_h = last_e = every
    else:
        last_e = frozenset(((0, 1), (1, 1)))
        last_h = frozenset(((0, 0), (1, 0), (0, 1), (1, 1), (2, 1)))
        first_e = every - {(2, 2)}

    def update_h(r, coef, wanted=every):
        for layer in range(LZ):
            if not any((a, layer) in wanted for a in range(3)):
                continue
            ex, ey, ez = (load(e, a, layer, r) for a in range(3))
            top = layer + 1 == LZ
            if (0, layer) in wanted:
                ey_up = zero if top else load(e, 1, layer + 1, r)
                ez_y = y_next(ez)
            if (1, layer) in wanted:
                ex_up = zero if top else load(e, 0, layer + 1, r)
                ez_x = load(e, 2, layer, r + 1)
            if (2, layer) in wanted:
                ey_x, ex_y = load(e, 1, layer, r + 1), y_next(ex)
            for t in range(TILES):
                rows = pl.ds(r, 8)
                if (0, layer) in wanted:
                    h[0, layer, t, rows, :] -= coef[t] * (ez_y[t] - ez[t] - (ey_up[t] - ey[t]))
                if (1, layer) in wanted:
                    h[1, layer, t, rows, :] -= coef[t] * (ex_up[t] - ex[t] - (ez_x[t] - ez[t]))
                if (2, layer) in wanted:
                    h[2, layer, t, rows, :] -= coef[t] * (ey_x[t] - ey[t] - (ex_y[t] - ex[t]))

    def update_e(r, moment, wanted, tiles):
        strength = math.sin(source_rate * moment)
        for layer in range(LZ):
            if not any((a, layer) in wanted for a in range(3)):
                continue
            hx, hy, hz = (load(h, a, layer, r) for a in range(3))
            edge = isinstance(r, int) and r == 0
            if (0, layer) in wanted:
                hy_low = load(h, 1, layer - 1, r) if layer else zero
                hz_y = y_last(hz)
            if (1, layer) in wanted:
                hx_low = load(h, 0, layer - 1, r) if layer else zero
                hz_x = [pltpu.roll(v, 1, 0) for v in hz] if edge else load(h, 2, layer, r - 1)
            if (2, layer) in wanted:
                hy_x = [pltpu.roll(v, 1, 0) for v in hy] if edge else load(h, 1, layer, r - 1)
                hx_y = y_last(hx)
            for t in range(tiles):
                rows = pl.ds(r, 8)
                rate = scale[layer, t, rows, :]
                if (0, layer) in wanted:
                    e[0, layer, t, rows, :] += rate * (hz[t] - hz_y[t] - (hy[t] - hy_low[t]))
                if (1, layer) in wanted:
                    e[1, layer, t, rows, :] += rate * (hx[t] - hx_low[t] - (hz[t] - hz_x[t]))
                if (2, layer) in wanted:
                    e[2, layer, t, rows, :] = (
                        e[2, layer, t, rows, :]
                        + rate * (hy[t] - hy_x[t] - (hx[t] - hx_y[t]))
                        + strength * grid[layer, t, rows, :]
                    )

    face_of = ((h, 1, -1.0), (h, 0, 1.0), (e, 1, 1.0), (e, 0, -1.0))

    def first_step(s, _):
        r = pl.multiple_of(s * 8, 8)
        update_h(r, half)
        update_e(r, 1.0, first_e, TILES)
        if with_face:
            for k, (ref, a, _sign) in enumerate(face_of):
                for tile in range(own_tiles):
                    first[k, tile, pl.ds(pl.multiple_of(r - OFF, 8), 8), :] = ref[
                        a, 1, tile, pl.ds(r, 8), :
                    ]
        return 0

    def second_step(s, _):
        own = pl.multiple_of(s * 16, 16)
        for part in range(2):
            r = pl.multiple_of(own + OFF + 8 * part, 8)
            update_h(r, half, last_h)
            update_e(r, 2.0, last_e, own_tiles)
        if with_face:
            now_rows = pl.ds(pl.multiple_of(own + OFF, 8), 16)
            for k, (ref, a, sign) in enumerate(face_of):
                for tile in range(own_tiles):
                    then = first[k, tile, pl.ds(own, 16), :]
                    now = ref[a, 1, tile, now_rows, :]
                    cols = pl.ds(128 * (tile % 2), 128)
                    target = 4 * k + tile // 2
                    face_out[target, pl.ds(own, 16), cols] = (sign * (then + now)).astype(BF16)
                    face_out[target + 2, pl.ds(own, 16), cols] = (sign * (then - now)).astype(BF16)
        return 0

    strips = span // 8
    for copy in arrivals[0]:
        copy.wait()
    grid_copy.wait()
    update_h(0, half_top)
    update_e(0, 1.0, first_e, TILES)
    for chunk in range(CHUNKS):
        begin = 1 + chunk * strips
        if chunk + 1 < CHUNKS:
            lax.fori_loop(begin, begin + strips - 1, first_step, 0, unroll=2)
            for copy in arrivals[chunk + 1]:
                copy.wait()
            first_step(jnp.int32(begin + strips - 1), 0)
        else:
            lax.fori_loop(begin, begin + strips, first_step, 0, unroll=2)
    update_h(ROWS + OFF, half_bottom)
    update_e(ROWS + OFF, 1.0, first_e, TILES)

    update_h(0, half_top, last_h)
    sent = []
    for chunk in range(CHUNKS):
        lax.fori_loop(chunk * (span // 16), (chunk + 1) * (span // 16), second_step, 0, unroll=2)
        if with_face:
            rows = pl.ds(chunk * span, span)
            copy = pltpu.make_async_copy(
                face_out.at[:, rows, :], face_target.at[:, rows, :], out_sem.at[len(sent)]
            )
            copy.start()
            sent.append(copy)
        if with_fields:
            source_rows = pl.ds(OFF + chunk * span, span)
            target_rows = pl.ds(chunk * span, span)
            for tile in range(own_tiles):
                cols = pl.ds(128 * tile, 128)
                for source, target in ((e, e_out), (h, h_out)):
                    copy = pltpu.make_async_copy(
                        source.at[:, :, tile, source_rows, :],
                        target.at[:, :, target_rows, cols],
                        out_sem.at[len(sent)],
                    )
                    copy.start()
                    sent.append(copy)
    for copy in sent:
        copy.wait()


def yee(with_fields, with_face, e, h, scale, grid, rims, place):
    field = jax.ShapeDtypeStruct((3, LZ, ROWS, COLS), F32)
    anywhere = pl.BlockSpec(memory_space=pl.ANY)
    out_shape = []
    out_specs = []
    scratch = [
        pltpu.VMEM((3, LZ, TILES, EXT_R, 128), F32),
        pltpu.VMEM((3, LZ, TILES, EXT_R, 128), F32),
        pltpu.VMEM((LZ, TILES, EXT_R, 128), F32),
        pltpu.VMEM((LZ, TILES, USED_R, 128), F32),
    ]
    if with_fields:
        out_shape += [field, field]
        out_specs += [anywhere, anywhere]
    if with_face:
        out_shape.append(pltpu.HBM((16, ROWS, 256), BF16))
        out_specs.append(anywhere)
        scratch.append(pltpu.VMEM((4, COLS // 128, ROWS, 128), F32))
        scratch.append(pltpu.VMEM((16, ROWS, 256), BF16))
    scratch += [
        pltpu.SemaphoreType.DMA((CHUNKS, 3 * COLS // 128)),
        pltpu.SemaphoreType.DMA,
        pltpu.SemaphoreType.DMA((CHUNKS * (2 * COLS // 128 + 1),)),
    ]
    return pl.pallas_call(
        functools.partial(yee_kernel, with_fields, with_face),
        in_specs=[anywhere] * 4 + [vmem()] * 4 + [smem()],
        out_specs=out_specs,
        out_shape=out_shape,
        scratch_shapes=scratch,
        compiler_params=params(28),
        cost_estimate=pl.CostEstimate(
            flops=5_000_000_000, bytes_accessed=40_000_000, transcendentals=0
        ),
        name="yee_fields" if with_fields else "yee_face",
    )(*stay(e, h), scale, grid, *rims, place)


def rows_kernel(field_ref, table_in, out_ref, table, sem):
    def copy_of(s):
        span = pl.ds(pl.multiple_of(s * ROW_STEP, ROW_STEP), ROW_STEP)
        return span, pltpu.make_async_copy(table_in.at[span], table.at[span], sem.at[s])

    for s in range(1280 // ROW_STEP):
        copy_of(s)[1].start()

    def part(s, _):
        span, copy = copy_of(s)
        copy.wait()
        total = jnp.dot(table[span, :], field_ref[...], preferred_element_type=F32)
        out_ref[span, :] = total.astype(BF16)
        return 0

    lax.fori_loop(0, 1280 // ROW_STEP, part, 0)


def rows_transform(field, table):
    return pl.pallas_call(
        rows_kernel,
        in_specs=[vmem(), pl.BlockSpec(memory_space=pl.ANY)],
        out_specs=vmem(),
        out_shape=jax.ShapeDtypeStruct((1280, 256), BF16),
        scratch_shapes=[pltpu.VMEM((1280, N), BF16), pltpu.SemaphoreType.DMA((1280 // ROW_STEP,))],
        compiler_params=params(18),
        name="rows_transform",
    )(field, *stay(table))


def columns_kernel(rows_ref, table_in, out_ref, table, total, spread, sem):
    def copy_of(s):
        cols = pl.ds(pl.multiple_of(s * COL_STEP, COL_STEP), COL_STEP)
        return cols, pltpu.make_async_copy(
            table_in.at[:, :, cols], table.at[:, :, cols], sem.at[s]
        )

    for s in range(2 * NA // COL_STEP):
        copy_of(s)[1].start()

    def width(s, _):
        cols, copy = copy_of(s)
        copy.wait()
        part = jnp.dot(rows_ref[0], table[0, :, cols], preferred_element_type=F32)
        for g in range(1, 16):
            part += jnp.dot(rows_ref[g], table[g, :, cols], preferred_element_type=F32)
        total[:, cols] = part
        return 0

    lax.fori_loop(0, 2 * NA // COL_STEP, width, 0)
    sub = lax.broadcasted_iota(jnp.int32, (8, NA), 0)

    def flip(value):
        value = pltpu.roll(value, 4, 0)
        value = jnp.where(sub % 4 < 2, pltpu.roll(value, 6, 0), pltpu.roll(value, 2, 0))
        return jnp.where(sub % 2 == 0, pltpu.roll(value, 7, 0), pltpu.roll(value, 1, 0))

    for q in range(4):
        for plus in (True, False):
            base = 16 * (q if plus else 4 - q)
            cos_re, cos_im = total[base : base + 8, 0:NA], total[base : base + 8, NA : 2 * NA]
            sin_re = total[base + 8 : base + 16, 0:NA]
            sin_im = total[base + 8 : base + 16, NA : 2 * NA]
            if plus:
                parts = (cos_re + sin_im, cos_im - sin_re)
            else:
                parts = (flip(cos_re - sin_im), flip(cos_im + sin_re))
            for ri, value in enumerate(parts):
                for j in range(8):
                    start = ((8 if plus else 0) * 8 + j) * 8 + 2 * q + ri
                    spread[pl.ds(start, 8, stride=64), :] = value[:, 128 * j : 128 * j + 128]
    out_ref[...] = spread[...].astype(BF16)


def columns(rows, table):
    return pl.pallas_call(
        columns_kernel,
        in_specs=[vmem(), pl.BlockSpec(memory_space=pl.ANY)],
        out_specs=vmem(),
        out_shape=pltpu.HBM((1024, 128), BF16),
        scratch_shapes=[
            pltpu.VMEM((16, 256, 2 * NA), BF16),
            pltpu.VMEM((80, 2 * NA), F32),
            pltpu.VMEM((1024, 128), F32),
            pltpu.SemaphoreType.DMA((2 * NA // COL_STEP,)),
        ],
        compiler_params=params(24),
        name="columns",
    )(rows, *stay(table))


def combine_kernel(parts_ref, coef_ref, place_ref, out_ref):
    sub = lax.broadcasted_iota(jnp.int32, (8, 128), 0)
    real_row = (sub % 2) == 0
    side = jnp.where(real_row, -1.0, 1.0)

    def swap(value):
        return jnp.where(real_row, pltpu.roll(value, 7, 0), pltpu.roll(value, 1, 0)) * side

    def two_blocks(pair, _):
        for comp in range(4):
            totals = parts_ref[(2 * comp) * 8 + pair].astype(F32)
            changes = parts_ref[(2 * comp + 1) * 8 + pair].astype(F32)
            for odd in range(2):
                t = 2 * pair + odd
                where = jnp.where(place_ref[0] >= 8, t, 15 - t)
                total = totals[8 * odd : 8 * odd + 8]
                change = changes[8 * odd : 8 * odd + 8]
                total_swap, change_swap = swap(total), swap(change)
                for f in range(2):
                    value = (
                        coef_ref[f, 0] * total
                        + coef_ref[f, 1] * total_swap
                        + coef_ref[f, 3] * change
                        - coef_ref[f, 2] * change_swap
                    )
                    item = f * 4 + comp
                    for q in range(4):
                        out_ref[where, 16 * q + 2 * item : 16 * q + 2 * item + 2, :] = value[
                            2 * q : 2 * q + 2, :
                        ]
        return 0

    lax.fori_loop(0, 8, two_blocks, 0)


def combine(parts, coef, place):
    return pl.pallas_call(
        combine_kernel,
        in_specs=[vmem(), smem(), smem()],
        out_specs=vmem(),
        out_shape=jax.ShapeDtypeStruct((16, 64, 128), F32),
        compiler_params=params(8),
        name="combine",
    )(parts, coef, place)


def on_device(x_table, y_table, e, h, material, eps, src_pos, src_amp, freqs):
    row_place = lax.axis_index(GX)
    col_place = lax.axis_index("gy")
    place = jnp.stack([row_place, col_place]).astype(jnp.int32)
    up, down = pack_rows(e, h, material, eps)
    from_top = lax.ppermute(down, GX, [(k, k + 1) for k in range(15)])
    from_bottom = lax.ppermute(up, GX, [(k + 1, k) for k in range(15)])
    scale = scales(material, eps)
    left, right = pack_cols(e, h, scale, from_top, from_bottom)
    from_left = lax.ppermute(right, "gy", [(k, k + 1) for k in range(7)])
    from_right = lax.ppermute(left, "gy", [(k + 1, k) for k in range(7)])
    pos = src_pos.T.reshape(3, NSRC // 128, 128)
    amp = src_amp.reshape(NSRC // 128, 128)
    pos, amp, left = lax.optimization_barrier((pos, amp, left))
    grid, kept_grid = sources(pos, amp, place)
    rims = (from_left, from_right, from_top, from_bottom)
    (face,) = yee(False, True, e, h, scale, grid, rims, place)
    e_out, h_out = yee(True, False, e, h, scale, *stay(kept_grid), rims, place)

    half = jnp.cos(freqs * 0.5), jnp.sin(freqs * 0.5)
    turn = jnp.cos(freqs * 1.5), jnp.sin(freqs * 1.5)
    coef = jnp.stack(
        [turn[0] * half[0], turn[1] * half[0], turn[0] * half[1], turn[1] * half[1]], 1
    ) * (1.0 / N)

    face = lax.all_to_all(face, GX, 0, 0, tiled=True)
    face, e_out, h_out = lax.optimization_barrier((face, e_out, h_out))
    rows = rows_transform(face.reshape(N, 256), x_table)
    rows = lax.all_to_all(rows.reshape(16, 80, 256), ("gc", "gy"), 0, 0, tiled=True)
    far = columns(rows, y_table)
    far = lax.all_to_all(far.reshape(128, 8, 128), GX + ("gy",), 0, 0, tiled=True)
    far = combine(far.reshape(64, 16, 128), coef, place)
    return e_out, h_out, far.reshape(64, 8, 2, 128)


def solution(mesh):
    fine = Mesh(mesh.devices.reshape(8, 2, 8), ("ga", "gc", "gy"))
    field = P(None, None, GX, "gy")
    placed = (P(), P(), field, field, P(None, GX, "gy"), P(), P(), P(), P())
    mapped = jax.shard_map(
        on_device,
        mesh=fine,
        in_specs=placed,
        out_specs=(field, field, P(GX, None, None, "gy")),
        check_vma=False,
    )
    x_table, y_table = tables()

    def program(e_field, h_field, material, eps_table, src_pos, src_amp, freqs):
        return mapped(
            x_table, y_table, e_field, h_field, material, eps_table, src_pos, src_amp, freqs
        )

    return program
```

```python
import functools
import math

import jax
import jax.numpy as jnp
import ml_dtypes
import numpy as np
from jax import lax
from jax.experimental import pallas as pl
from jax.experimental.pallas import tpu as pltpu
from jax.sharding import Mesh, PartitionSpec as P

LZ = 3
NA = 1024
NMAT = 8
N = 4096
NSRC = 4096
ROWS = 256
COLS = 512
OFF = 8
EXT_R = 280
EXT_C = 640
TILES = 5
USED_R = 272
FOLD = 136
ROW_STEP = 320
CHUNKS = 2
courant = 0.5
source_rate = 0.7
PERIOD = 4 * N
GX = ("ga", "gc")
MIB = 1 << 20
F32 = jnp.float32
BF16 = jnp.bfloat16


def tables():
    cell = np.arange(N, dtype=np.int64)
    t = np.arange(16)[:, None, None]
    q = np.arange(5)[None, :, None]
    m = np.arange(8)[None, None, :]
    w = (64 * m + 4 * t + q)[..., None]
    phase = np.remainder(w * cell, PERIOD) * (2.0 * math.pi / PERIOD)
    x_table = np.stack([np.cos(phase), np.sin(phase)], 2).reshape(16 * 80, N)
    v = np.arange(NA, dtype=np.int64) + NA // 4
    inner = np.remainder(cell[:256, None] * v[None, :], PERIOD) * (2.0 * math.pi / PERIOD)
    y_table = np.stack([np.cos(inner), -np.sin(inner)], 1)
    y_table = y_table.reshape(256, 2, 8, 128).transpose(2, 0, 1, 3).reshape(8, 256, 256)
    block = (2 * np.arange(8)[None, :] + np.arange(2)[:, None]).reshape(16)
    outer = np.remainder(256 * block[:, None] * v[None, :], PERIOD) * (2.0 * math.pi / PERIOD)
    y_phase = np.stack([np.cos(outer), -np.sin(outer)], 1)
    y_phase = y_phase.reshape(32, 8, 128).transpose(1, 0, 2)
    half_width = ml_dtypes.bfloat16
    return x_table.astype(half_width), y_table.astype(half_width), y_phase.astype(np.float32)


def params(mib):
    return pltpu.CompilerParams(vmem_limit_bytes=mib * MIB)


def stay(*arrays):
    return [pltpu.with_memory_space_constraint(array, pltpu.HBM) for array in arrays]


def vmem():
    return pl.BlockSpec(memory_space=pltpu.VMEM)


def smem():
    return pl.BlockSpec(memory_space=pltpu.SMEM)


def scale_of(material, eps_ref):
    shape = (8, material.shape[-1])
    scale = None
    for k in range(NMAT):
        rate = (courant / jnp.full(shape, eps_ref[k], F32))[0:1]
        scale = rate if scale is None else jnp.where(material == k, rate, scale)
    return scale


def scale_kernel(material_ref, eps_ref, scale_ref):
    def strip(s, _):
        r = pl.multiple_of(s * 16, 16)
        for layer in range(LZ):
            scale_ref[layer, pl.ds(r, 16), :] = scale_of(
                material_ref[layer, pl.ds(r, 16), :], eps_ref
            )
        return 0

    lax.fori_loop(0, ROWS // 16, strip, 0)


def scales(material, eps):
    return pl.pallas_call(
        scale_kernel,
        in_specs=[vmem(), smem()],
        out_specs=vmem(),
        out_shape=jax.ShapeDtypeStruct((LZ, ROWS, COLS), F32),
        compiler_params=params(8),
        cost_estimate=pl.CostEstimate(
            flops=1_500_000_000, bytes_accessed=3_000_000, transcendentals=0
        ),
        name="scales",
    )(material, eps)


def pack_rows_kernel(e_lo, e_hi, h_lo, h_hi, m_lo, m_hi, eps_ref, up_ref, down_ref):
    sub = lax.broadcasted_iota(jnp.int32, (8, COLS), 0)
    up = down = None
    for a in range(7):
        for layer in range(LZ):
            index = a * LZ + layer
            if a < 3:
                lo, hi = e_lo[a, layer], e_hi[a, layer]
            elif a < 6:
                lo, hi = h_lo[a - 3, layer], h_hi[a - 3, layer]
            else:
                lo, hi = scale_of(m_lo[layer], eps_ref), scale_of(m_hi[layer], eps_ref)
            p = 2 * (index % 4)
            if p == 0:
                up = jnp.zeros((8, COLS), F32)
                down = jnp.zeros((8, COLS), F32)
            here = (sub == p) | (sub == p + 1)
            up = jnp.where(here, pltpu.roll(lo, p, 0) if p else lo, up)
            down = jnp.where(here, pltpu.roll(hi, (p + 2) % 8, 0) if p != 6 else hi, down)
            tile = index // 4
            up_ref[8 * tile : 8 * tile + 8, :] = up
            down_ref[8 * tile : 8 * tile + 8, :] = down


def pack_rows(e, h, material, eps):
    last = ROWS // 8 - 1
    lo4 = pl.BlockSpec((3, LZ, 8, COLS), lambda r: (0, 0, 0, 0))
    hi4 = pl.BlockSpec((3, LZ, 8, COLS), lambda r: (0, 0, last, 0))
    lo3 = pl.BlockSpec((LZ, 8, COLS), lambda r: (0, 0, 0))
    hi3 = pl.BlockSpec((LZ, 8, COLS), lambda r: (0, last, 0))
    out = pl.BlockSpec((48, COLS), lambda r: (0, 0))
    return pl.pallas_call(
        pack_rows_kernel,
        grid=(1,),
        in_specs=[lo4, hi4, lo4, hi4, lo3, hi3, smem()],
        out_specs=[out, out],
        out_shape=[jax.ShapeDtypeStruct((48, COLS), F32)] * 2,
        compiler_params=params(8),
        name="pack_rows",
    )(*stay(e, e, h, h, material, material), eps)


def rim_rows(packed, index, to_top):
    p, tile = 2 * (index % 4), index // 4
    value = packed[8 * tile : 8 * tile + 8, :]
    sub = lax.broadcasted_iota(jnp.int32, value.shape, 0)
    shift = (6 - p) % 8 if to_top else (8 - p) % 8
    value = pltpu.roll(value, shift, 0) if shift else value
    return jnp.where(sub >= 6 if to_top else sub < 2, value, 0.0)


def packed_ends(pair_of, shape):
    lane = lax.broadcasted_iota(jnp.int32, shape, 1)
    both = jnp.zeros(shape, F32)
    for index in range(7 * LZ):
        lo, hi = pair_of(index)
        ends = pltpu.roll(jnp.where(lane < 64, lo, hi), 4 * index + 2, 1)
        both = jnp.where(lane // 4 == index, ends, both)
    return both


def pack_cols_kernel(
    e_lo, e_hi, h_lo, h_hi, s_lo, s_hi, own_ref
):
    rows = 32

    def strip(s, _):
        r = pl.multiple_of(s * rows, rows)
        span = pl.ds(r, rows)

        def pair_of(index):
            a, layer = index // LZ, index % LZ
            if a < 3:
                return e_lo[a, layer, span, :], e_hi[a, layer, span, :]
            if a < 6:
                return h_lo[a - 3, layer, span, :], h_hi[a - 3, layer, span, :]
            return s_lo[layer, span, :], s_hi[layer, span, :]

        own_ref[span, :] = packed_ends(pair_of, (rows, 128))
        return 0

    lax.fori_loop(0, ROWS // rows, strip, 0)


def pack_cols(e, h, scale):
    end = COLS // 128 - 1
    lo4 = pl.BlockSpec((3, LZ, ROWS, 128), lambda r: (0, 0, 0, 0))
    hi4 = pl.BlockSpec((3, LZ, ROWS, 128), lambda r: (0, 0, 0, end))
    lo3 = pl.BlockSpec((LZ, ROWS, 128), lambda r: (0, 0, 0))
    hi3 = pl.BlockSpec((LZ, ROWS, 128), lambda r: (0, 0, end))
    return pl.pallas_call(
        pack_cols_kernel,
        grid=(1,),
        in_specs=[lo4, hi4, lo4, hi4, lo3, hi3],
        out_specs=pl.BlockSpec((ROWS, 128), lambda r: (0, 0)),
        out_shape=jax.ShapeDtypeStruct((ROWS, 128), F32),
        compiler_params=params(16),
        cost_estimate=pl.CostEstimate(
            flops=2_000_000_000, bytes_accessed=6_000_000, transcendentals=0
        ),
        name="pack_cols",
    )(*stay(e, e, h, h), scale, scale)


def fold_cols_kernel(own_ref, top_ref, bottom_ref, left_ref, right_ref, all_rows):
    end = COLS - 128
    all_rows[OFF : OFF + ROWS, :] = own_ref[...]
    for to_top, packed, r in ((True, top_ref, 0), (False, bottom_ref, ROWS + OFF)):

        def pair_of(index):
            rows = rim_rows(packed, index, to_top)
            return rows[:, 0:128], rows[:, end:COLS]

        all_rows[r : r + 8, :] = packed_ends(pair_of, (8, 128))
    high = lax.broadcasted_iota(jnp.int32, (FOLD, 128), 1) % 4 >= 2
    near, far = all_rows[0:FOLD, :], all_rows[FOLD:USED_R, :]
    left_ref[...] = jnp.where(high, near, pltpu.roll(far, 126, 1))
    right_ref[...] = jnp.where(high, pltpu.roll(far, 2, 1), near)


def fold_cols(own, from_top, from_bottom):
    return pl.pallas_call(
        fold_cols_kernel,
        in_specs=[vmem()] * 3,
        out_specs=[vmem()] * 2,
        out_shape=[jax.ShapeDtypeStruct((FOLD, 128), F32)] * 2,
        scratch_shapes=[pltpu.VMEM((USED_R, 128), F32)],
        compiler_params=params(4),
        name="fold_cols",
    )(own, from_top, from_bottom)


def rim_tile(both, index):
    lane = lax.broadcasted_iota(jnp.int32, both.shape, 1)
    moved = pltpu.roll(both, (126 - 4 * index) % 128, 1)
    return jnp.where((lane < 2) | (lane >= 126), moved, 0.0)


def sources_kernel(pos_ref, amp_ref, place_ref, grid_ref, kept_ref, sem):
    groups = NSRC // 128
    row = pos_ref[1] - place_ref[0] * ROWS + OFF
    col = pos_ref[2] - place_ref[1] * COLS
    inside = (row >= OFF - 1) & (row <= ROWS + OFF) & (col >= -1) & (col <= COLS)
    col = jnp.where(col < 0, EXT_C - 1, col)
    taken = jnp.where(inside, 1.0, 0.0)
    lane_a = lax.broadcasted_iota(jnp.int32, (128, 128), 0)
    lane_b = lax.broadcasted_iota(jnp.int32, (128, 128), 1)
    before = jnp.where(lane_a < lane_b, 1.0, 0.0).astype(BF16)
    group_a = lax.broadcasted_iota(jnp.int32, (groups, groups), 0)
    group_b = lax.broadcasted_iota(jnp.int32, (groups, groups), 1)
    earlier = jnp.where(group_b < group_a, 1.0, 0.0).astype(BF16)
    in_group = jnp.dot(taken.astype(BF16), before, preferred_element_type=F32)
    ahead = jnp.dot(earlier, taken.astype(BF16), preferred_element_type=F32)
    rank = in_group + jnp.sum(ahead, axis=1, keepdims=True)
    rank = jnp.where(inside, rank, -1.0)
    features = (
        row.astype(F32),
        col.astype(F32),
        pos_ref[0].astype(F32),
        amp_ref[...],
    )
    count = jnp.sum(taken).astype(jnp.int32)
    slot = lax.broadcasted_iota(jnp.int32, (128, 128), 0).astype(F32)
    feature_lane = lax.broadcasted_iota(jnp.int32, (128, 128), 1)
    row_of = lax.broadcasted_iota(jnp.int32, (USED_R, 128), 0).astype(F32)
    col_of = lax.broadcasted_iota(jnp.int32, (EXT_C, 128), 0).astype(F32)
    grid_ref[...] = jnp.zeros(grid_ref.shape, F32)

    def one_pass(p, _):
        base = (p * 128).astype(F32)
        sums = [jnp.zeros((128, 128), F32) for _ in features]
        found = jnp.zeros((128, 128), F32)
        for g in range(groups):
            chosen = slot == rank[g : g + 1, :] - base
            found = jnp.where(chosen, 1.0, found)
            for f, feature in enumerate(features):
                sums[f] = jnp.where(chosen, feature[g : g + 1, :], sums[f])
        packed = jnp.zeros((128, 128), F32)
        for f, total in enumerate(sums + [found]):
            packed = jnp.where(feature_lane == f, jnp.sum(total, axis=1, keepdims=True), packed)
        packed = packed.T
        src_row, src_col, src_layer = packed[0:1], packed[1:2], packed[2:3]
        amp, valid = packed[3:4], packed[4:5]
        amp_1 = amp.astype(BF16).astype(F32)
        amp_2 = (amp - amp_1).astype(BF16).astype(F32)
        amp_3 = amp - amp_1 - amp_2
        at_col = jnp.where(col_of == src_col, 1.0, 0.0).astype(BF16)
        at_col = jnp.concatenate([at_col] * 3, 1)
        for layer in range(LZ):
            at_row = (row_of == src_row) & (src_layer == layer) & (valid > 0.0)
            weights = jnp.concatenate(
                [jnp.where(at_row, part, 0.0).astype(BF16) for part in (amp_1, amp_2, amp_3)], 1
            )
            added = lax.dot_general(
                weights, at_col, (((1,), (1,)), ((), ())), preferred_element_type=F32
            )
            for tile in range(TILES):
                grid_ref[layer, tile] += added[:, 128 * tile : 128 * tile + 128]
        return 0

    lax.fori_loop(0, (count + 127) // 128, one_pass, 0)
    copy = pltpu.make_async_copy(grid_ref, kept_ref, sem)
    copy.start()
    copy.wait()


def sources(pos, amp, place):
    return pl.pallas_call(
        sources_kernel,
        in_specs=[vmem(), vmem(), smem()],
        out_specs=[vmem(), pl.BlockSpec(memory_space=pl.ANY)],
        out_shape=[
            jax.ShapeDtypeStruct((LZ, TILES, USED_R, 128), F32),
            pltpu.HBM((LZ, TILES, USED_R, 128), F32),
        ],
        scratch_shapes=[pltpu.SemaphoreType.DMA],
        compiler_params=params(12),
        cost_estimate=pl.CostEstimate(
            flops=3_000_000_000, bytes_accessed=3_000_000, transcendentals=0
        ),
        name="sources",
    )(pos, amp, place)


def yee_kernel(
    with_fields,
    with_face,
    e_in,
    h_in,
    scale_in,
    grid_in,
    from_left,
    from_right,
    from_top,
    from_bottom,
    place_ref,
    *refs,
):
    refs = list(refs)
    e_out, h_out = (refs.pop(0), refs.pop(0)) if with_fields else (None, None)
    face_target = refs.pop(0) if with_face else None
    e, h, scale, grid = refs[:4]
    refs = refs[4:]
    first, face_out = (refs.pop(0), refs.pop(0)) if with_face else (None, None)
    in_sem, grid_sem, out_sem = refs
    span = ROWS // CHUNKS
    own_tiles = COLS // 128

    grid_copy = pltpu.make_async_copy(grid_in, grid, grid_sem)
    grid_copy.start()
    arrivals = []
    for chunk in range(CHUNKS):
        here = []
        source_rows = pl.ds(chunk * span, span)
        target_rows = pl.ds(OFF + chunk * span, span)
        for tile in range(own_tiles):
            cols = pl.ds(128 * tile, 128)
            pairs = (
                (e_in.at[:, :, source_rows, cols], e.at[:, :, tile, target_rows, :]),
                (h_in.at[:, :, source_rows, cols], h.at[:, :, tile, target_rows, :]),
                (scale_in.at[:, source_rows, cols], scale.at[:, tile, target_rows, :]),
            )
            for source, target in pairs:
                copy = pltpu.make_async_copy(source, target, in_sem.at[chunk, len(here)])
                copy.start()
                here.append(copy)
        arrivals.append(here)
    sub = lax.broadcasted_iota(jnp.int32, (8, 128), 0)
    lane = lax.broadcasted_iota(jnp.int32, (8, 128), 1)

    def array_of(a, layer):
        if a < 3:
            return e.at[a, layer]
        if a < 6:
            return h.at[a - 3, layer]
        return scale.at[layer]

    for index in range(7 * LZ):
        target = array_of(index // LZ, index % LZ)
        top = rim_rows(from_top, index, True)
        bottom = rim_rows(from_bottom, index, False)
        for tile in range(own_tiles):
            cols = slice(128 * tile, 128 * tile + 128)
            target[tile, 0:8, :] = top[:, cols]
            target[tile, ROWS + OFF : ROWS + OFF + 8, :] = bottom[:, cols]
        for tile in range(TILES):
            target[tile, USED_R : USED_R + 8, :] = jnp.zeros((8, 128), F32)

    def rim_strip(s, _):
        r = pl.multiple_of(s * 8, 8)
        left, right = from_left[pl.ds(r, 8), :], from_right[pl.ds(r, 8), :]
        high = lane % 4 >= 2
        near = jnp.where(high, right, left)
        far = jnp.where(high, pltpu.roll(right, 2, 1), pltpu.roll(left, 126, 1))
        for index in range(7 * LZ):
            target = array_of(index // LZ, index % LZ)
            target[own_tiles, pl.ds(r, 8), :] = rim_tile(near, index)
            target[own_tiles, pl.ds(pl.multiple_of(r + FOLD, 8), 8), :] = rim_tile(far, index)
        return 0

    lax.fori_loop(0, FOLD // 8, rim_strip, 0, unroll=2)

    row_place, col_place = place_ref[0], place_ref[1]
    rim_half = jnp.full((8, 128), courant, F32)
    rim_half = jnp.where((lane >= 64) & (col_place == 0), 0.0, rim_half)
    rim_half = jnp.where((lane < 64) & (col_place == 7), 0.0, rim_half)
    inner_half = jnp.full((8, 128), courant, F32)
    half = [inner_half] * own_tiles + [rim_half]
    half_top = [jnp.where(row_place == 0, 0.0, value) for value in half]
    half_bottom = [jnp.where(row_place == 15, 0.0, value) for value in half]

    def load(ref, a, layer, r):
        return [ref[a, layer, tile, pl.ds(r, 8), :] for tile in range(TILES)]

    def y_next(here):
        moved = [pltpu.roll(value, 127, 1) for value in here]
        return [
            jnp.where(lane == 127, moved[(tile + 1) % TILES], moved[tile]) for tile in range(TILES)
        ]

    def y_last(here):
        moved = [pltpu.roll(value, 1, 1) for value in here]
        return [
            jnp.where(lane == 0, moved[(tile - 1) % TILES], moved[tile]) for tile in range(TILES)
        ]

    zero = [jnp.zeros((8, 128), F32)] * TILES

    every = frozenset((a, layer) for a in range(3) for layer in range(LZ))
    if with_fields:
        first_e = last_h = last_e = every
    else:
        last_e = frozenset(((0, 1), (1, 1)))
        last_h = frozenset(((0, 0), (1, 0), (0, 1), (1, 1), (2, 1)))
        first_e = every - {(2, 2)}

    def update_h(r, coef, wanted=every):
        for layer in range(LZ):
            if not any((a, layer) in wanted for a in range(3)):
                continue
            ex, ey, ez = (load(e, a, layer, r) for a in range(3))
            top = layer + 1 == LZ
            if (0, layer) in wanted:
                ey_up = zero if top else load(e, 1, layer + 1, r)
                ez_y = y_next(ez)
            if (1, layer) in wanted:
                ex_up = zero if top else load(e, 0, layer + 1, r)
                ez_x = load(e, 2, layer, r + 1)
            if (2, layer) in wanted:
                ey_x, ex_y = load(e, 1, layer, r + 1), y_next(ex)
            for t in range(TILES):
                rows = pl.ds(r, 8)
                if (0, layer) in wanted:
                    h[0, layer, t, rows, :] -= coef[t] * (ez_y[t] - ez[t] - (ey_up[t] - ey[t]))
                if (1, layer) in wanted:
                    h[1, layer, t, rows, :] -= coef[t] * (ex_up[t] - ex[t] - (ez_x[t] - ez[t]))
                if (2, layer) in wanted:
                    h[2, layer, t, rows, :] -= coef[t] * (ey_x[t] - ey[t] - (ex_y[t] - ex[t]))

    def update_e(r, moment, wanted, tiles):
        strength = math.sin(source_rate * moment)
        for layer in range(LZ):
            if not any((a, layer) in wanted for a in range(3)):
                continue
            hx, hy, hz = (load(h, a, layer, r) for a in range(3))
            edge = isinstance(r, int) and r == 0
            if (0, layer) in wanted:
                hy_low = load(h, 1, layer - 1, r) if layer else zero
                hz_y = y_last(hz)
            if (1, layer) in wanted:
                hx_low = load(h, 0, layer - 1, r) if layer else zero
                hz_x = [pltpu.roll(v, 1, 0) for v in hz] if edge else load(h, 2, layer, r - 1)
            if (2, layer) in wanted:
                hy_x = [pltpu.roll(v, 1, 0) for v in hy] if edge else load(h, 1, layer, r - 1)
                hx_y = y_last(hx)
            for t in range(tiles):
                rows = pl.ds(r, 8)
                rate = scale[layer, t, rows, :]
                if (0, layer) in wanted:
                    e[0, layer, t, rows, :] += rate * (hz[t] - hz_y[t] - (hy[t] - hy_low[t]))
                if (1, layer) in wanted:
                    e[1, layer, t, rows, :] += rate * (hx[t] - hx_low[t] - (hz[t] - hz_x[t]))
                if (2, layer) in wanted:
                    e[2, layer, t, rows, :] = (
                        e[2, layer, t, rows, :]
                        + rate * (hy[t] - hy_x[t] - (hx[t] - hx_y[t]))
                        + strength * grid[layer, t, rows, :]
                    )

    face_of = ((h, 1, -1.0), (h, 0, 1.0), (e, 1, 1.0), (e, 0, -1.0))

    def first_step(s, _):
        r = pl.multiple_of(s * 8, 8)
        update_h(r, half)
        update_e(r, 1.0, first_e, TILES)
        if with_face:
            for k, (ref, a, _sign) in enumerate(face_of):
                for tile in range(own_tiles):
                    first[k, tile, pl.ds(pl.multiple_of(r - OFF, 8), 8), :] = ref[
                        a, 1, tile, pl.ds(r, 8), :
                    ]
        return 0

    def second_step(s, _):
        own = pl.multiple_of(s * 16, 16)
        for part in range(2):
            r = pl.multiple_of(own + OFF + 8 * part, 8)
            update_h(r, half, last_h)
            update_e(r, 2.0, last_e, own_tiles)
        if with_face:
            now_rows = pl.ds(pl.multiple_of(own + OFF, 8), 16)
            for k, (ref, a, sign) in enumerate(face_of):
                for tile in range(own_tiles):
                    then = first[k, tile, pl.ds(own, 16), :]
                    now = ref[a, 1, tile, now_rows, :]
                    cols = pl.ds(128 * (tile % 2), 128)
                    target = 4 * k + tile // 2
                    face_out[target, pl.ds(own, 16), cols] = (sign * (then + now)).astype(BF16)
                    face_out[target + 2, pl.ds(own, 16), cols] = (sign * (then - now)).astype(BF16)
        return 0

    strips = span // 8
    for copy in arrivals[0]:
        copy.wait()
    grid_copy.wait()
    update_h(0, half_top)
    update_e(0, 1.0, first_e, TILES)
    for chunk in range(CHUNKS):
        begin = 1 + chunk * strips
        if chunk + 1 < CHUNKS:
            lax.fori_loop(begin, begin + strips - 1, first_step, 0, unroll=2)
            for copy in arrivals[chunk + 1]:
                copy.wait()
            first_step(jnp.int32(begin + strips - 1), 0)
        else:
            lax.fori_loop(begin, begin + strips, first_step, 0, unroll=2)
    update_h(ROWS + OFF, half_bottom)
    update_e(ROWS + OFF, 1.0, first_e, TILES)

    update_h(0, half_top, last_h)
    sent = []
    for chunk in range(CHUNKS):
        lax.fori_loop(chunk * (span // 16), (chunk + 1) * (span // 16), second_step, 0, unroll=2)
        if with_face:
            rows = pl.ds(chunk * span, span)
            copy = pltpu.make_async_copy(
                face_out.at[:, rows, :], face_target.at[:, rows, :], out_sem.at[len(sent)]
            )
            copy.start()
            sent.append(copy)
        if with_fields:
            source_rows = pl.ds(OFF + chunk * span, span)
            target_rows = pl.ds(chunk * span, span)
            for tile in range(own_tiles):
                cols = pl.ds(128 * tile, 128)
                for source, target in ((e, e_out), (h, h_out)):
                    copy = pltpu.make_async_copy(
                        source.at[:, :, tile, source_rows, :],
                        target.at[:, :, target_rows, cols],
                        out_sem.at[len(sent)],
                    )
                    copy.start()
                    sent.append(copy)
    for copy in sent:
        copy.wait()


def yee(with_fields, with_face, e, h, scale, grid, rims, place):
    field = jax.ShapeDtypeStruct((3, LZ, ROWS, COLS), F32)
    anywhere = pl.BlockSpec(memory_space=pl.ANY)
    out_shape = []
    out_specs = []
    scratch = [
        pltpu.VMEM((3, LZ, TILES, EXT_R, 128), F32),
        pltpu.VMEM((3, LZ, TILES, EXT_R, 128), F32),
        pltpu.VMEM((LZ, TILES, EXT_R, 128), F32),
        pltpu.VMEM((LZ, TILES, USED_R, 128), F32),
    ]
    if with_fields:
        out_shape += [field, field]
        out_specs += [anywhere, anywhere]
    if with_face:
        out_shape.append(pltpu.HBM((16, ROWS, 256), BF16))
        out_specs.append(anywhere)
        scratch.append(pltpu.VMEM((4, COLS // 128, ROWS, 128), F32))
        scratch.append(pltpu.VMEM((16, ROWS, 256), BF16))
    scratch += [
        pltpu.SemaphoreType.DMA((CHUNKS, 3 * COLS // 128)),
        pltpu.SemaphoreType.DMA,
        pltpu.SemaphoreType.DMA((CHUNKS * (2 * COLS // 128 + 1),)),
    ]
    return pl.pallas_call(
        functools.partial(yee_kernel, with_fields, with_face),
        in_specs=[anywhere] * 4 + [vmem()] * 4 + [smem()],
        out_specs=out_specs,
        out_shape=out_shape,
        scratch_shapes=scratch,
        compiler_params=params(28),
        cost_estimate=pl.CostEstimate(
            flops=5_000_000_000, bytes_accessed=40_000_000, transcendentals=0
        ),
        name="yee_fields" if with_fields else "yee_face",
    )(*stay(e, h), scale, grid, *rims, place)


def rows_kernel(field_ref, table_in, out_ref, table, sem):
    def copy_of(s):
        span = pl.ds(pl.multiple_of(s * ROW_STEP, ROW_STEP), ROW_STEP)
        return span, pltpu.make_async_copy(table_in.at[span], table.at[span], sem.at[s])

    for s in range(1280 // ROW_STEP):
        copy_of(s)[1].start()

    def part(s, _):
        span, copy = copy_of(s)
        copy.wait()
        total = jnp.dot(table[span, :], field_ref[...], preferred_element_type=F32)
        out_ref[span, :] = total.astype(BF16)
        return 0

    lax.fori_loop(0, 1280 // ROW_STEP, part, 0)


def rows_transform(field, table):
    return pl.pallas_call(
        rows_kernel,
        in_specs=[vmem(), pl.BlockSpec(memory_space=pl.ANY)],
        out_specs=vmem(),
        out_shape=jax.ShapeDtypeStruct((1280, 256), BF16),
        scratch_shapes=[pltpu.VMEM((1280, N), BF16), pltpu.SemaphoreType.DMA((1280 // ROW_STEP,))],
        compiler_params=params(18),
        name="rows_transform",
    )(field, *stay(table))


def columns_kernel(rows_ref, table_ref, phase_ref, out_ref, product, total, spread):
    def width(c, _):
        product[...] = jnp.dot(rows_ref[...], table_ref[c], preferred_element_type=F32)
        sum_re = jnp.zeros((80, 128), F32)
        sum_im = jnp.zeros((80, 128), F32)
        for b in range(16):
            part_re = product[80 * b : 80 * b + 80, 0:128]
            part_im = product[80 * b : 80 * b + 80, 128:256]
            turn_re = phase_ref[c, 2 * b : 2 * b + 1, :]
            turn_im = phase_ref[c, 2 * b + 1 : 2 * b + 2, :]
            sum_re += turn_re * part_re - turn_im * part_im
            sum_im += turn_re * part_im + turn_im * part_re
        total[:, pl.ds(pl.multiple_of(128 * c, 128), 128)] = sum_re
        total[:, pl.ds(pl.multiple_of(NA + 128 * c, 128), 128)] = sum_im
        return 0

    lax.fori_loop(0, 8, width, 0, unroll=2)
    sub = lax.broadcasted_iota(jnp.int32, (8, NA), 0)

    def flip(value):
        value = pltpu.roll(value, 4, 0)
        value = jnp.where(sub % 4 < 2, pltpu.roll(value, 6, 0), pltpu.roll(value, 2, 0))
        return jnp.where(sub % 2 == 0, pltpu.roll(value, 7, 0), pltpu.roll(value, 1, 0))

    for q in range(4):
        for plus in (True, False):
            base = 16 * (q if plus else 4 - q)
            cos_re, cos_im = total[base : base + 8, 0:NA], total[base : base + 8, NA : 2 * NA]
            sin_re = total[base + 8 : base + 16, 0:NA]
            sin_im = total[base + 8 : base + 16, NA : 2 * NA]
            if plus:
                parts = (cos_re + sin_im, cos_im - sin_re)
            else:
                parts = (flip(cos_re - sin_im), flip(cos_im + sin_re))
            for ri, value in enumerate(parts):
                for j in range(8):
                    start = ((8 if plus else 0) * 8 + j) * 8 + 2 * q + ri
                    spread[pl.ds(start, 8, stride=64), :] = value[:, 128 * j : 128 * j + 128]
    out_ref[...] = spread[...].astype(BF16)


def columns(rows, table, phase):
    return pl.pallas_call(
        columns_kernel,
        in_specs=[vmem(), vmem(), vmem()],
        out_specs=vmem(),
        out_shape=pltpu.HBM((1024, 128), BF16),
        scratch_shapes=[
            pltpu.VMEM((1280, 256), F32),
            pltpu.VMEM((80, 2 * NA), F32),
            pltpu.VMEM((1024, 128), F32),
        ],
        compiler_params=params(12),
        name="columns",
    )(rows, table, phase)


def combine_kernel(parts_ref, coef_ref, place_ref, out_ref):
    sub = lax.broadcasted_iota(jnp.int32, (8, 128), 0)
    real_row = (sub % 2) == 0
    side = jnp.where(real_row, -1.0, 1.0)

    def swap(value):
        return jnp.where(real_row, pltpu.roll(value, 7, 0), pltpu.roll(value, 1, 0)) * side

    def two_blocks(pair, _):
        for comp in range(4):
            totals = parts_ref[(2 * comp) * 8 + pair].astype(F32)
            changes = parts_ref[(2 * comp + 1) * 8 + pair].astype(F32)
            for odd in range(2):
                t = 2 * pair + odd
                where = jnp.where(place_ref[0] >= 8, t, 15 - t)
                total = totals[8 * odd : 8 * odd + 8]
                change = changes[8 * odd : 8 * odd + 8]
                total_swap, change_swap = swap(total), swap(change)
                for f in range(2):
                    value = (
                        coef_ref[f, 0] * total
                        + coef_ref[f, 1] * total_swap
                        + coef_ref[f, 3] * change
                        - coef_ref[f, 2] * change_swap
                    )
                    item = f * 4 + comp
                    for q in range(4):
                        out_ref[where, 16 * q + 2 * item : 16 * q + 2 * item + 2, :] = value[
                            2 * q : 2 * q + 2, :
                        ]
        return 0

    lax.fori_loop(0, 8, two_blocks, 0)


def combine(parts, coef, place):
    return pl.pallas_call(
        combine_kernel,
        in_specs=[vmem(), smem(), smem()],
        out_specs=vmem(),
        out_shape=jax.ShapeDtypeStruct((16, 64, 128), F32),
        compiler_params=params(8),
        name="combine",
    )(parts, coef, place)


def on_device(x_table, y_table, y_phase, e, h, material, eps, src_pos, src_amp, freqs):
    row_place = lax.axis_index(GX)
    col_place = lax.axis_index("gy")
    place = jnp.stack([row_place, col_place]).astype(jnp.int32)
    up, down = pack_rows(e, h, material, eps)
    from_top = lax.ppermute(down, GX, [(k, k + 1) for k in range(15)])
    from_bottom = lax.ppermute(up, GX, [(k + 1, k) for k in range(15)])
    scale = scales(material, eps)
    own = pack_cols(e, h, scale)
    left, right = fold_cols(own, from_top, from_bottom)
    from_left = lax.ppermute(right, "gy", [(k, k + 1) for k in range(7)])
    from_right = lax.ppermute(left, "gy", [(k + 1, k) for k in range(7)])
    pos = src_pos.T.reshape(3, NSRC // 128, 128)
    amp = src_amp.reshape(NSRC // 128, 128)
    pos, amp, left = lax.optimization_barrier((pos, amp, left))
    grid, kept_grid = sources(pos, amp, place)
    rims = (from_left, from_right, from_top, from_bottom)
    (face,) = yee(False, True, e, h, scale, grid, rims, place)
    e_out, h_out = yee(True, False, e, h, scale, *stay(kept_grid), rims, place)

    half = jnp.cos(freqs * 0.5), jnp.sin(freqs * 0.5)
    turn = jnp.cos(freqs * 1.5), jnp.sin(freqs * 1.5)
    coef = jnp.stack(
        [turn[0] * half[0], turn[1] * half[0], turn[0] * half[1], turn[1] * half[1]], 1
    ) * (1.0 / N)

    face = lax.all_to_all(face, GX, 0, 0, tiled=True)
    face, e_out, h_out = lax.optimization_barrier((face, e_out, h_out))
    rows = rows_transform(face.reshape(N, 256), x_table)
    rows = lax.all_to_all(rows.reshape(16, 80, 256), ("gc", "gy"), 0, 0, tiled=True)
    far = columns(rows.reshape(1280, 256), y_table, y_phase)
    far = lax.all_to_all(far.reshape(128, 8, 128), GX + ("gy",), 0, 0, tiled=True)
    far = combine(far.reshape(64, 16, 128), coef, place)
    return e_out, h_out, far.reshape(64, 8, 2, 128)


def solution(mesh):
    fine = Mesh(mesh.devices.reshape(8, 2, 8), ("ga", "gc", "gy"))
    field = P(None, None, GX, "gy")
    placed = (P(), P(), P(), field, field, P(None, GX, "gy"), P(), P(), P(), P())
    mapped = jax.shard_map(
        on_device,
        mesh=fine,
        in_specs=placed,
        out_specs=(field, field, P(GX, None, None, "gy")),
        check_vma=False,
    )
    constants = tables()

    def program(e_field, h_field, material, eps_table, src_pos, src_amp, freqs):
        return mapped(
            *constants, e_field, h_field, material, eps_table, src_pos, src_amp, freqs
        )

    return program
```

```python
import functools
import math

import jax
import jax.numpy as jnp
import ml_dtypes
import numpy as np
from jax import lax
from jax.experimental import pallas as pl
from jax.experimental.pallas import tpu as pltpu
from jax.sharding import Mesh, PartitionSpec as P

LZ = 3
NA = 1024
NMAT = 8
N = 4096
NSRC = 4096
ROWS = 256
COLS = 512
OFF = 8
EXT_R = 280
EXT_C = 640
TILES = 5
USED_R = 272
FOLD = 136
ROW_STEP = 320
CHUNKS = 2
courant = 0.5
source_rate = 0.7
PERIOD = 4 * N
GX = ("ga", "gc")
MIB = 1 << 20
F32 = jnp.float32
BF16 = jnp.bfloat16


def tables():
    cell = np.arange(N, dtype=np.int64)
    t = np.arange(16)[:, None, None]
    q = np.arange(5)[None, :, None]
    m = np.arange(8)[None, None, :]
    w = (64 * m + 4 * t + q)[..., None]
    phase = np.remainder(w * cell, PERIOD) * (2.0 * math.pi / PERIOD)
    x_table = np.stack([np.cos(phase), np.sin(phase)], 2).reshape(16 * 80, N)
    v = np.arange(NA, dtype=np.int64) + NA // 4
    inner = np.remainder(cell[:256, None] * v[None, :], PERIOD) * (2.0 * math.pi / PERIOD)
    y_table = np.stack([np.cos(inner), -np.sin(inner)], 1)
    y_table = y_table.reshape(256, 2, 8, 128).transpose(2, 0, 1, 3).reshape(8, 256, 256)
    block = (2 * np.arange(8)[None, :] + np.arange(2)[:, None]).reshape(16)
    outer = np.remainder(256 * block[:, None] * v[None, :], PERIOD) * (2.0 * math.pi / PERIOD)
    y_phase = np.stack([np.cos(outer), -np.sin(outer)], 1)
    y_phase = y_phase.reshape(32, 8, 128).transpose(1, 0, 2)
    half_width = ml_dtypes.bfloat16
    return x_table.astype(half_width), y_table.astype(half_width), y_phase.astype(np.float32)


def params(mib):
    return pltpu.CompilerParams(vmem_limit_bytes=mib * MIB)


def stay(*arrays):
    return [pltpu.with_memory_space_constraint(array, pltpu.HBM) for array in arrays]


def vmem():
    return pl.BlockSpec(memory_space=pltpu.VMEM)


def smem():
    return pl.BlockSpec(memory_space=pltpu.SMEM)


def scale_of(material, eps_ref):
    shape = (8, material.shape[-1])
    scale = None
    for k in range(NMAT):
        rate = (courant / jnp.full(shape, eps_ref[k], F32))[0:1]
        scale = rate if scale is None else jnp.where(material == k, rate, scale)
    return scale


def scale_kernel(material_ref, eps_ref, scale_ref):
    def strip(s, _):
        r = pl.multiple_of(s * 16, 16)
        for layer in range(LZ):
            scale_ref[layer, pl.ds(r, 16), :] = scale_of(
                material_ref[layer, pl.ds(r, 16), :], eps_ref
            )
        return 0

    lax.fori_loop(0, ROWS // 16, strip, 0)


def scales(material, eps):
    return pl.pallas_call(
        scale_kernel,
        in_specs=[vmem(), smem()],
        out_specs=vmem(),
        out_shape=jax.ShapeDtypeStruct((LZ, ROWS, COLS), F32),
        compiler_params=params(8),
        cost_estimate=pl.CostEstimate(
            flops=1_500_000_000, bytes_accessed=3_000_000, transcendentals=0
        ),
        name="scales",
    )(material, eps)


def pack_rows_kernel(e_lo, e_hi, h_lo, h_hi, m_lo, m_hi, eps_ref, up_ref, down_ref):
    sub = lax.broadcasted_iota(jnp.int32, (8, COLS), 0)
    up = down = None
    for a in range(7):
        for layer in range(LZ):
            index = a * LZ + layer
            if a < 3:
                lo, hi = e_lo[a, layer], e_hi[a, layer]
            elif a < 6:
                lo, hi = h_lo[a - 3, layer], h_hi[a - 3, layer]
            else:
                lo, hi = scale_of(m_lo[layer], eps_ref), scale_of(m_hi[layer], eps_ref)
            p = 2 * (index % 4)
            if p == 0:
                up = jnp.zeros((8, COLS), F32)
                down = jnp.zeros((8, COLS), F32)
            here = (sub == p) | (sub == p + 1)
            up = jnp.where(here, pltpu.roll(lo, p, 0) if p else lo, up)
            down = jnp.where(here, pltpu.roll(hi, (p + 2) % 8, 0) if p != 6 else hi, down)
            tile = index // 4
            up_ref[8 * tile : 8 * tile + 8, :] = up
            down_ref[8 * tile : 8 * tile + 8, :] = down


def pack_rows(e, h, material, eps):
    last = ROWS // 8 - 1
    lo4 = pl.BlockSpec((3, LZ, 8, COLS), lambda r: (0, 0, 0, 0))
    hi4 = pl.BlockSpec((3, LZ, 8, COLS), lambda r: (0, 0, last, 0))
    lo3 = pl.BlockSpec((LZ, 8, COLS), lambda r: (0, 0, 0))
    hi3 = pl.BlockSpec((LZ, 8, COLS), lambda r: (0, last, 0))
    out = pl.BlockSpec((48, COLS), lambda r: (0, 0))
    return pl.pallas_call(
        pack_rows_kernel,
        grid=(1,),
        in_specs=[lo4, hi4, lo4, hi4, lo3, hi3, smem()],
        out_specs=[out, out],
        out_shape=[jax.ShapeDtypeStruct((48, COLS), F32)] * 2,
        compiler_params=params(8),
        name="pack_rows",
    )(*stay(e, e, h, h, material, material, eps))


def rim_rows(packed, index, to_top):
    p, tile = 2 * (index % 4), index // 4
    value = packed[8 * tile : 8 * tile + 8, :]
    sub = lax.broadcasted_iota(jnp.int32, value.shape, 0)
    shift = (6 - p) % 8 if to_top else (8 - p) % 8
    value = pltpu.roll(value, shift, 0) if shift else value
    return jnp.where(sub >= 6 if to_top else sub < 2, value, 0.0)


def packed_ends(pair_of, shape):
    lane = lax.broadcasted_iota(jnp.int32, shape, 1)
    both = jnp.zeros(shape, F32)
    for index in range(7 * LZ):
        lo, hi = pair_of(index)
        ends = pltpu.roll(jnp.where(lane < 64, lo, hi), 4 * index + 2, 1)
        both = jnp.where(lane // 4 == index, ends, both)
    return both


def pack_cols_kernel(
    e_lo, e_hi, h_lo, h_hi, s_lo, s_hi, own_ref
):
    rows = 32

    def strip(s, _):
        r = pl.multiple_of(s * rows, rows)
        span = pl.ds(r, rows)

        def pair_of(index):
            a, layer = index // LZ, index % LZ
            if a < 3:
                return e_lo[a, layer, span, :], e_hi[a, layer, span, :]
            if a < 6:
                return h_lo[a - 3, layer, span, :], h_hi[a - 3, layer, span, :]
            return s_lo[layer, span, :], s_hi[layer, span, :]

        own_ref[span, :] = packed_ends(pair_of, (rows, 128))
        return 0

    lax.fori_loop(0, ROWS // rows, strip, 0)


def pack_cols(e, h, scale):
    end = COLS // 128 - 1
    lo4 = pl.BlockSpec((3, LZ, ROWS, 128), lambda r: (0, 0, 0, 0))
    hi4 = pl.BlockSpec((3, LZ, ROWS, 128), lambda r: (0, 0, 0, end))
    lo3 = pl.BlockSpec((LZ, ROWS, 128), lambda r: (0, 0, 0))
    hi3 = pl.BlockSpec((LZ, ROWS, 128), lambda r: (0, 0, end))
    return pl.pallas_call(
        pack_cols_kernel,
        grid=(1,),
        in_specs=[lo4, hi4, lo4, hi4, lo3, hi3],
        out_specs=pl.BlockSpec((ROWS, 128), lambda r: (0, 0)),
        out_shape=jax.ShapeDtypeStruct((ROWS, 128), F32),
        compiler_params=params(16),
        cost_estimate=pl.CostEstimate(
            flops=2_000_000_000, bytes_accessed=6_000_000, transcendentals=0
        ),
        name="pack_cols",
    )(*stay(e, e, h, h), scale, scale)


def fold_cols_kernel(own_ref, top_ref, bottom_ref, left_ref, right_ref, all_rows):
    end = COLS - 128
    all_rows[OFF : OFF + ROWS, :] = own_ref[...]
    for to_top, packed, r in ((True, top_ref, 0), (False, bottom_ref, ROWS + OFF)):

        def pair_of(index):
            rows = rim_rows(packed, index, to_top)
            return rows[:, 0:128], rows[:, end:COLS]

        all_rows[r : r + 8, :] = packed_ends(pair_of, (8, 128))
    high = lax.broadcasted_iota(jnp.int32, (FOLD, 128), 1) % 4 >= 2
    near, far = all_rows[0:FOLD, :], all_rows[FOLD:USED_R, :]
    left_ref[...] = jnp.where(high, near, pltpu.roll(far, 126, 1))
    right_ref[...] = jnp.where(high, pltpu.roll(far, 2, 1), near)


def fold_cols(own, from_top, from_bottom):
    return pl.pallas_call(
        fold_cols_kernel,
        in_specs=[vmem()] * 3,
        out_specs=[vmem()] * 2,
        out_shape=[jax.ShapeDtypeStruct((FOLD, 128), F32)] * 2,
        scratch_shapes=[pltpu.VMEM((USED_R, 128), F32)],
        compiler_params=params(4),
        name="fold_cols",
    )(own, from_top, from_bottom)


def rim_tile(both, index):
    lane = lax.broadcasted_iota(jnp.int32, both.shape, 1)
    moved = pltpu.roll(both, (126 - 4 * index) % 128, 1)
    return jnp.where((lane < 2) | (lane >= 126), moved, 0.0)


def sources_kernel(pos_ref, amp_ref, place_ref, grid_ref, kept_ref, sem):
    groups = NSRC // 128
    row = pos_ref[1] - place_ref[0] * ROWS + OFF
    col = pos_ref[2] - place_ref[1] * COLS
    inside = (row >= OFF - 1) & (row <= ROWS + OFF) & (col >= -1) & (col <= COLS)
    col = jnp.where(col < 0, EXT_C - 1, col)
    taken = jnp.where(inside, 1.0, 0.0)
    lane_a = lax.broadcasted_iota(jnp.int32, (128, 128), 0)
    lane_b = lax.broadcasted_iota(jnp.int32, (128, 128), 1)
    before = jnp.where(lane_a < lane_b, 1.0, 0.0).astype(BF16)
    group_a = lax.broadcasted_iota(jnp.int32, (groups, groups), 0)
    group_b = lax.broadcasted_iota(jnp.int32, (groups, groups), 1)
    earlier = jnp.where(group_b < group_a, 1.0, 0.0).astype(BF16)
    in_group = jnp.dot(taken.astype(BF16), before, preferred_element_type=F32)
    ahead = jnp.dot(earlier, taken.astype(BF16), preferred_element_type=F32)
    rank = in_group + jnp.sum(ahead, axis=1, keepdims=True)
    rank = jnp.where(inside, rank, -1.0)
    features = (
        row.astype(F32),
        col.astype(F32),
        pos_ref[0].astype(F32),
        amp_ref[...],
    )
    count = jnp.sum(taken).astype(jnp.int32)
    slot = lax.broadcasted_iota(jnp.int32, (128, 128), 0).astype(F32)
    feature_lane = lax.broadcasted_iota(jnp.int32, (128, 128), 1)
    row_of = lax.broadcasted_iota(jnp.int32, (USED_R, 128), 0).astype(F32)
    col_of = lax.broadcasted_iota(jnp.int32, (EXT_C, 128), 0).astype(F32)
    grid_ref[...] = jnp.zeros(grid_ref.shape, F32)

    def one_pass(p, _):
        base = (p * 128).astype(F32)
        sums = [jnp.zeros((128, 128), F32) for _ in features]
        found = jnp.zeros((128, 128), F32)
        for g in range(groups):
            chosen = slot == rank[g : g + 1, :] - base
            found = jnp.where(chosen, 1.0, found)
            for f, feature in enumerate(features):
                sums[f] = jnp.where(chosen, feature[g : g + 1, :], sums[f])
        packed = jnp.zeros((128, 128), F32)
        for f, total in enumerate(sums + [found]):
            packed = jnp.where(feature_lane == f, jnp.sum(total, axis=1, keepdims=True), packed)
        packed = packed.T
        src_row, src_col, src_layer = packed[0:1], packed[1:2], packed[2:3]
        amp, valid = packed[3:4], packed[4:5]
        amp_1 = amp.astype(BF16).astype(F32)
        amp_2 = (amp - amp_1).astype(BF16).astype(F32)
        amp_3 = amp - amp_1 - amp_2
        at_col = jnp.where(col_of == src_col, 1.0, 0.0).astype(BF16)
        at_col = jnp.concatenate([at_col] * 3, 1)
        for layer in range(LZ):
            at_row = (row_of == src_row) & (src_layer == layer) & (valid > 0.0)
            weights = jnp.concatenate(
                [jnp.where(at_row, part, 0.0).astype(BF16) for part in (amp_1, amp_2, amp_3)], 1
            )
            added = lax.dot_general(
                weights, at_col, (((1,), (1,)), ((), ())), preferred_element_type=F32
            )
            for tile in range(TILES):
                grid_ref[layer, tile] += added[:, 128 * tile : 128 * tile + 128]
        return 0

    lax.fori_loop(0, (count + 127) // 128, one_pass, 0)
    copy = pltpu.make_async_copy(grid_ref, kept_ref, sem)
    copy.start()
    copy.wait()


def sources(pos, amp, place):
    return pl.pallas_call(
        sources_kernel,
        in_specs=[vmem(), vmem(), smem()],
        out_specs=[vmem(), pl.BlockSpec(memory_space=pl.ANY)],
        out_shape=[
            jax.ShapeDtypeStruct((LZ, TILES, USED_R, 128), F32),
            pltpu.HBM((LZ, TILES, USED_R, 128), F32),
        ],
        scratch_shapes=[pltpu.SemaphoreType.DMA],
        compiler_params=params(12),
        cost_estimate=pl.CostEstimate(
            flops=3_000_000_000, bytes_accessed=3_000_000, transcendentals=0
        ),
        name="sources",
    )(pos, amp, place)


def yee_kernel(
    with_fields,
    with_face,
    e_in,
    h_in,
    scale_in,
    grid_in,
    from_left,
    from_right,
    from_top,
    from_bottom,
    place_ref,
    *refs,
):
    refs = list(refs)
    e_out, h_out = (refs.pop(0), refs.pop(0)) if with_fields else (None, None)
    face_target = refs.pop(0) if with_face else None
    e, h, scale, grid = refs[:4]
    refs = refs[4:]
    first, face_out = (refs.pop(0), refs.pop(0)) if with_face else (None, None)
    in_sem, grid_sem, out_sem = refs
    span = ROWS // CHUNKS
    own_tiles = COLS // 128

    grid_copy = pltpu.make_async_copy(grid_in, grid, grid_sem)
    grid_copy.start()
    arrivals = []
    for chunk in range(CHUNKS):
        here = []
        source_rows = pl.ds(chunk * span, span)
        target_rows = pl.ds(OFF + chunk * span, span)
        for tile in range(own_tiles):
            cols = pl.ds(128 * tile, 128)
            pairs = (
                (e_in.at[:, :, source_rows, cols], e.at[:, :, tile, target_rows, :]),
                (h_in.at[:, :, source_rows, cols], h.at[:, :, tile, target_rows, :]),
                (scale_in.at[:, source_rows, cols], scale.at[:, tile, target_rows, :]),
            )
            for source, target in pairs:
                copy = pltpu.make_async_copy(source, target, in_sem.at[chunk, len(here)])
                copy.start()
                here.append(copy)
        arrivals.append(here)
    sub = lax.broadcasted_iota(jnp.int32, (8, 128), 0)
    lane = lax.broadcasted_iota(jnp.int32, (8, 128), 1)

    def array_of(a, layer):
        if a < 3:
            return e.at[a, layer]
        if a < 6:
            return h.at[a - 3, layer]
        return scale.at[layer]

    for index in range(7 * LZ):
        target = array_of(index // LZ, index % LZ)
        top = rim_rows(from_top, index, True)
        bottom = rim_rows(from_bottom, index, False)
        for tile in range(own_tiles):
            cols = slice(128 * tile, 128 * tile + 128)
            target[tile, 0:8, :] = top[:, cols]
            target[tile, ROWS + OFF : ROWS + OFF + 8, :] = bottom[:, cols]
        for tile in range(TILES):
            target[tile, USED_R : USED_R + 8, :] = jnp.zeros((8, 128), F32)

    def rim_strip(s, _):
        r = pl.multiple_of(s * 8, 8)
        left, right = from_left[pl.ds(r, 8), :], from_right[pl.ds(r, 8), :]
        high = lane % 4 >= 2
        near = jnp.where(high, right, left)
        far = jnp.where(high, pltpu.roll(right, 2, 1), pltpu.roll(left, 126, 1))
        for index in range(7 * LZ):
            target = array_of(index // LZ, index % LZ)
            target[own_tiles, pl.ds(r, 8), :] = rim_tile(near, index)
            target[own_tiles, pl.ds(pl.multiple_of(r + FOLD, 8), 8), :] = rim_tile(far, index)
        return 0

    lax.fori_loop(0, FOLD // 8, rim_strip, 0, unroll=2)

    row_place, col_place = place_ref[0], place_ref[1]
    rim_half = jnp.full((8, 128), courant, F32)
    rim_half = jnp.where((lane >= 64) & (col_place == 0), 0.0, rim_half)
    rim_half = jnp.where((lane < 64) & (col_place == 7), 0.0, rim_half)
    inner_half = jnp.full((8, 128), courant, F32)
    half = [inner_half] * own_tiles + [rim_half]
    half_top = [jnp.where(row_place == 0, 0.0, value) for value in half]
    half_bottom = [jnp.where(row_place == 15, 0.0, value) for value in half]

    def load(ref, a, layer, r):
        return [ref[a, layer, tile, pl.ds(r, 8), :] for tile in range(TILES)]

    def y_next(here):
        moved = [pltpu.roll(value, 127, 1) for value in here]
        return [
            jnp.where(lane == 127, moved[(tile + 1) % TILES], moved[tile]) for tile in range(TILES)
        ]

    def y_last(here):
        moved = [pltpu.roll(value, 1, 1) for value in here]
        return [
            jnp.where(lane == 0, moved[(tile - 1) % TILES], moved[tile]) for tile in range(TILES)
        ]

    zero = [jnp.zeros((8, 128), F32)] * TILES

    every = frozenset((a, layer) for a in range(3) for layer in range(LZ))
    if with_fields:
        first_e = last_h = last_e = every
    else:
        last_e = frozenset(((0, 1), (1, 1)))
        last_h = frozenset(((0, 0), (1, 0), (0, 1), (1, 1), (2, 1)))
        first_e = every - {(2, 2)}

    def update_h(r, coef, wanted=every):
        for layer in range(LZ):
            if not any((a, layer) in wanted for a in range(3)):
                continue
            ex, ey, ez = (load(e, a, layer, r) for a in range(3))
            top = layer + 1 == LZ
            if (0, layer) in wanted:
                ey_up = zero if top else load(e, 1, layer + 1, r)
                ez_y = y_next(ez)
            if (1, layer) in wanted:
                ex_up = zero if top else load(e, 0, layer + 1, r)
                ez_x = load(e, 2, layer, r + 1)
            if (2, layer) in wanted:
                ey_x, ex_y = load(e, 1, layer, r + 1), y_next(ex)
            for t in range(TILES):
                rows = pl.ds(r, 8)
                if (0, layer) in wanted:
                    h[0, layer, t, rows, :] -= coef[t] * (ez_y[t] - ez[t] - (ey_up[t] - ey[t]))
                if (1, layer) in wanted:
                    h[1, layer, t, rows, :] -= coef[t] * (ex_up[t] - ex[t] - (ez_x[t] - ez[t]))
                if (2, layer) in wanted:
                    h[2, layer, t, rows, :] -= coef[t] * (ey_x[t] - ey[t] - (ex_y[t] - ex[t]))

    def update_e(r, moment, wanted, tiles):
        strength = math.sin(source_rate * moment)
        for layer in range(LZ):
            if not any((a, layer) in wanted for a in range(3)):
                continue
            hx, hy, hz = (load(h, a, layer, r) for a in range(3))
            edge = isinstance(r, int) and r == 0
            if (0, layer) in wanted:
                hy_low = load(h, 1, layer - 1, r) if layer else zero
                hz_y = y_last(hz)
            if (1, layer) in wanted:
                hx_low = load(h, 0, layer - 1, r) if layer else zero
                hz_x = [pltpu.roll(v, 1, 0) for v in hz] if edge else load(h, 2, layer, r - 1)
            if (2, layer) in wanted:
                hy_x = [pltpu.roll(v, 1, 0) for v in hy] if edge else load(h, 1, layer, r - 1)
                hx_y = y_last(hx)
            for t in range(tiles):
                rows = pl.ds(r, 8)
                rate = scale[layer, t, rows, :]
                if (0, layer) in wanted:
                    e[0, layer, t, rows, :] += rate * (hz[t] - hz_y[t] - (hy[t] - hy_low[t]))
                if (1, layer) in wanted:
                    e[1, layer, t, rows, :] += rate * (hx[t] - hx_low[t] - (hz[t] - hz_x[t]))
                if (2, layer) in wanted:
                    e[2, layer, t, rows, :] = (
                        e[2, layer, t, rows, :]
                        + rate * (hy[t] - hy_x[t] - (hx[t] - hx_y[t]))
                        + strength * grid[layer, t, rows, :]
                    )

    face_of = ((h, 1, -1.0), (h, 0, 1.0), (e, 1, 1.0), (e, 0, -1.0))

    def first_step(s, _):
        r = pl.multiple_of(s * 8, 8)
        update_h(r, half)
        update_e(r, 1.0, first_e, TILES)
        if with_face:
            for k, (ref, a, _sign) in enumerate(face_of):
                for tile in range(own_tiles):
                    first[k, tile, pl.ds(pl.multiple_of(r - OFF, 8), 8), :] = ref[
                        a, 1, tile, pl.ds(r, 8), :
                    ]
        return 0

    def second_step(s, _):
        own = pl.multiple_of(s * 16, 16)
        for part in range(2):
            r = pl.multiple_of(own + OFF + 8 * part, 8)
            update_h(r, half, last_h)
            update_e(r, 2.0, last_e, own_tiles)
        if with_face:
            now_rows = pl.ds(pl.multiple_of(own + OFF, 8), 16)
            for k, (ref, a, sign) in enumerate(face_of):
                for tile in range(own_tiles):
                    then = first[k, tile, pl.ds(own, 16), :]
                    now = ref[a, 1, tile, now_rows, :]
                    cols = pl.ds(128 * (tile % 2), 128)
                    target = 4 * k + tile // 2
                    face_out[target, pl.ds(own, 16), cols] = (sign * (then + now)).astype(BF16)
                    face_out[target + 2, pl.ds(own, 16), cols] = (sign * (then - now)).astype(BF16)
        return 0

    strips = span // 8
    for copy in arrivals[0]:
        copy.wait()
    grid_copy.wait()
    update_h(0, half_top)
    update_e(0, 1.0, first_e, TILES)
    for chunk in range(CHUNKS):
        begin = 1 + chunk * strips
        if chunk + 1 < CHUNKS:
            lax.fori_loop(begin, begin + strips - 1, first_step, 0, unroll=2)
            for copy in arrivals[chunk + 1]:
                copy.wait()
            first_step(jnp.int32(begin + strips - 1), 0)
        else:
            lax.fori_loop(begin, begin + strips, first_step, 0, unroll=2)
    update_h(ROWS + OFF, half_bottom)
    update_e(ROWS + OFF, 1.0, first_e, TILES)

    update_h(0, half_top, last_h)
    sent = []
    for chunk in range(CHUNKS):
        lax.fori_loop(chunk * (span // 16), (chunk + 1) * (span // 16), second_step, 0, unroll=2)
        if with_face:
            rows = pl.ds(chunk * span, span)
            copy = pltpu.make_async_copy(
                face_out.at[:, rows, :], face_target.at[:, rows, :], out_sem.at[len(sent)]
            )
            copy.start()
            sent.append(copy)
        if with_fields:
            source_rows = pl.ds(OFF + chunk * span, span)
            target_rows = pl.ds(chunk * span, span)
            for tile in range(own_tiles):
                cols = pl.ds(128 * tile, 128)
                for source, target in ((e, e_out), (h, h_out)):
                    copy = pltpu.make_async_copy(
                        source.at[:, :, tile, source_rows, :],
                        target.at[:, :, target_rows, cols],
                        out_sem.at[len(sent)],
                    )
                    copy.start()
                    sent.append(copy)
    for copy in sent:
        copy.wait()


def yee(with_fields, with_face, e, h, scale, grid, rims, place):
    field = jax.ShapeDtypeStruct((3, LZ, ROWS, COLS), F32)
    anywhere = pl.BlockSpec(memory_space=pl.ANY)
    out_shape = []
    out_specs = []
    scratch = [
        pltpu.VMEM((3, LZ, TILES, EXT_R, 128), F32),
        pltpu.VMEM((3, LZ, TILES, EXT_R, 128), F32),
        pltpu.VMEM((LZ, TILES, EXT_R, 128), F32),
        pltpu.VMEM((LZ, TILES, USED_R, 128), F32),
    ]
    if with_fields:
        out_shape += [field, field]
        out_specs += [anywhere, anywhere]
    if with_face:
        out_shape.append(pltpu.HBM((16, ROWS, 256), BF16))
        out_specs.append(anywhere)
        scratch.append(pltpu.VMEM((4, COLS // 128, ROWS, 128), F32))
        scratch.append(pltpu.VMEM((16, ROWS, 256), BF16))
    scratch += [
        pltpu.SemaphoreType.DMA((CHUNKS, 3 * COLS // 128)),
        pltpu.SemaphoreType.DMA,
        pltpu.SemaphoreType.DMA((CHUNKS * (2 * COLS // 128 + 1),)),
    ]
    return pl.pallas_call(
        functools.partial(yee_kernel, with_fields, with_face),
        in_specs=[anywhere] * 4 + [vmem()] * 4 + [smem()],
        out_specs=out_specs,
        out_shape=out_shape,
        scratch_shapes=scratch,
        compiler_params=params(28),
        cost_estimate=pl.CostEstimate(
            flops=5_000_000_000, bytes_accessed=40_000_000, transcendentals=0
        ),
        name="yee_fields" if with_fields else "yee_face",
    )(*stay(e, h), scale, grid, *rims, place)


def rows_kernel(field_ref, table_in, out_ref, table, sem):
    def copy_of(s):
        span = pl.ds(pl.multiple_of(s * ROW_STEP, ROW_STEP), ROW_STEP)
        return span, pltpu.make_async_copy(table_in.at[span], table.at[span], sem.at[s])

    for s in range(1280 // ROW_STEP):
        copy_of(s)[1].start()

    def part(s, _):
        span, copy = copy_of(s)
        copy.wait()
        total = jnp.dot(table[span, :], field_ref[...], preferred_element_type=F32)
        out_ref[span, :] = total.astype(BF16)
        return 0

    lax.fori_loop(0, 1280 // ROW_STEP, part, 0)


def rows_transform(field, table):
    return pl.pallas_call(
        rows_kernel,
        in_specs=[vmem(), pl.BlockSpec(memory_space=pl.ANY)],
        out_specs=vmem(),
        out_shape=jax.ShapeDtypeStruct((1280, 256), BF16),
        scratch_shapes=[pltpu.VMEM((1280, N), BF16), pltpu.SemaphoreType.DMA((1280 // ROW_STEP,))],
        compiler_params=params(18),
        name="rows_transform",
    )(field, *stay(table))


def columns_kernel(rows_ref, table_ref, phase_ref, out_ref, product, total, spread):
    def width(c, _):
        product[...] = jnp.dot(rows_ref[...], table_ref[c], preferred_element_type=F32)
        sum_re = jnp.zeros((80, 128), F32)
        sum_im = jnp.zeros((80, 128), F32)
        for b in range(16):
            part_re = product[80 * b : 80 * b + 80, 0:128]
            part_im = product[80 * b : 80 * b + 80, 128:256]
            turn_re = phase_ref[c, 2 * b : 2 * b + 1, :]
            turn_im = phase_ref[c, 2 * b + 1 : 2 * b + 2, :]
            sum_re += turn_re * part_re - turn_im * part_im
            sum_im += turn_re * part_im + turn_im * part_re
        total[:, pl.ds(pl.multiple_of(128 * c, 128), 128)] = sum_re
        total[:, pl.ds(pl.multiple_of(NA + 128 * c, 128), 128)] = sum_im
        return 0

    lax.fori_loop(0, 8, width, 0, unroll=2)
    sub = lax.broadcasted_iota(jnp.int32, (8, NA), 0)

    def flip(value):
        value = pltpu.roll(value, 4, 0)
        value = jnp.where(sub % 4 < 2, pltpu.roll(value, 6, 0), pltpu.roll(value, 2, 0))
        return jnp.where(sub % 2 == 0, pltpu.roll(value, 7, 0), pltpu.roll(value, 1, 0))

    for q in range(4):
        for plus in (True, False):
            base = 16 * (q if plus else 4 - q)
            cos_re, cos_im = total[base : base + 8, 0:NA], total[base : base + 8, NA : 2 * NA]
            sin_re = total[base + 8 : base + 16, 0:NA]
            sin_im = total[base + 8 : base + 16, NA : 2 * NA]
            if plus:
                parts = (cos_re + sin_im, cos_im - sin_re)
            else:
                parts = (flip(cos_re - sin_im), flip(cos_im + sin_re))
            for ri, value in enumerate(parts):
                for j in range(8):
                    start = ((8 if plus else 0) * 8 + j) * 8 + 2 * q + ri
                    spread[pl.ds(start, 8, stride=64), :] = value[:, 128 * j : 128 * j + 128]
    out_ref[...] = spread[...].astype(BF16)


def columns(rows, table, phase):
    return pl.pallas_call(
        columns_kernel,
        in_specs=[vmem(), vmem(), vmem()],
        out_specs=vmem(),
        out_shape=pltpu.HBM((1024, 128), BF16),
        scratch_shapes=[
            pltpu.VMEM((1280, 256), F32),
            pltpu.VMEM((80, 2 * NA), F32),
            pltpu.VMEM((1024, 128), F32),
        ],
        compiler_params=params(12),
        name="columns",
    )(rows, table, phase)


def combine_kernel(parts_ref, coef_ref, place_ref, out_ref):
    sub = lax.broadcasted_iota(jnp.int32, (8, 128), 0)
    real_row = (sub % 2) == 0
    side = jnp.where(real_row, -1.0, 1.0)

    def swap(value):
        return jnp.where(real_row, pltpu.roll(value, 7, 0), pltpu.roll(value, 1, 0)) * side

    def two_blocks(pair, _):
        for comp in range(4):
            totals = parts_ref[(2 * comp) * 8 + pair].astype(F32)
            changes = parts_ref[(2 * comp + 1) * 8 + pair].astype(F32)
            for odd in range(2):
                t = 2 * pair + odd
                where = jnp.where(place_ref[0] >= 8, t, 15 - t)
                total = totals[8 * odd : 8 * odd + 8]
                change = changes[8 * odd : 8 * odd + 8]
                total_swap, change_swap = swap(total), swap(change)
                for f in range(2):
                    value = (
                        coef_ref[f, 0] * total
                        + coef_ref[f, 1] * total_swap
                        + coef_ref[f, 3] * change
                        - coef_ref[f, 2] * change_swap
                    )
                    item = f * 4 + comp
                    for q in range(4):
                        out_ref[where, 16 * q + 2 * item : 16 * q + 2 * item + 2, :] = value[
                            2 * q : 2 * q + 2, :
                        ]
        return 0

    lax.fori_loop(0, 8, two_blocks, 0)


def combine(parts, coef, place):
    return pl.pallas_call(
        combine_kernel,
        in_specs=[vmem(), smem(), smem()],
        out_specs=vmem(),
        out_shape=jax.ShapeDtypeStruct((16, 64, 128), F32),
        compiler_params=params(8),
        name="combine",
    )(parts, coef, place)


def on_device(x_table, y_table, y_phase, e, h, material, eps, src_pos, src_amp, freqs):
    row_place = lax.axis_index(GX)
    col_place = lax.axis_index("gy")
    place = jnp.stack([row_place, col_place]).astype(jnp.int32)
    up, down = pack_rows(e, h, material, eps)
    from_top = lax.ppermute(down, GX, [(k, k + 1) for k in range(15)])
    from_bottom = lax.ppermute(up, GX, [(k + 1, k) for k in range(15)])
    scale = scales(material, eps)
    own = pack_cols(e, h, scale)
    left, right = fold_cols(own, from_top, from_bottom)
    from_left = lax.ppermute(right, "gy", [(k, k + 1) for k in range(7)])
    from_right = lax.ppermute(left, "gy", [(k + 1, k) for k in range(7)])
    pos = src_pos.T.reshape(3, NSRC // 128, 128)
    amp = src_amp.reshape(NSRC // 128, 128)
    pos, amp, left = lax.optimization_barrier((pos, amp, left))
    grid, kept_grid = sources(pos, amp, place)
    rims = (from_left, from_right, from_top, from_bottom)
    (face,) = yee(False, True, e, h, scale, grid, rims, place)
    e_out, h_out = yee(True, False, e, h, scale, *stay(kept_grid), rims, place)

    half = jnp.cos(freqs * 0.5), jnp.sin(freqs * 0.5)
    turn = jnp.cos(freqs * 1.5), jnp.sin(freqs * 1.5)
    coef = jnp.stack(
        [turn[0] * half[0], turn[1] * half[0], turn[0] * half[1], turn[1] * half[1]], 1
    ) * (1.0 / N)

    face = lax.all_to_all(face, GX, 0, 0, tiled=True)
    face, e_out, h_out = lax.optimization_barrier((face, e_out, h_out))
    rows = rows_transform(face.reshape(N, 256), x_table)
    rows = lax.all_to_all(rows.reshape(16, 80, 256), ("gc", "gy"), 0, 0, tiled=True)
    far = columns(rows.reshape(1280, 256), y_table, y_phase)
    far = lax.all_to_all(far.reshape(128, 8, 128), GX + ("gy",), 0, 0, tiled=True)
    far = combine(far.reshape(64, 16, 128), coef, place)
    return e_out, h_out, far.reshape(64, 8, 2, 128)


def solution(mesh):
    fine = Mesh(mesh.devices.reshape(8, 2, 8), ("ga", "gc", "gy"))
    field = P(None, None, GX, "gy")
    placed = (P(), P(), P(), field, field, P(None, GX, "gy"), P(), P(), P(), P())
    mapped = jax.shard_map(
        on_device,
        mesh=fine,
        in_specs=placed,
        out_specs=(field, field, P(GX, None, None, "gy")),
        check_vma=False,
    )
    constants = tables()

    def program(e_field, h_field, material, eps_table, src_pos, src_amp, freqs):
        return mapped(
            *constants, e_field, h_field, material, eps_table, src_pos, src_amp, freqs
        )

    return program
```
